128 devices in a mesh: row: 8 (over x, core), col: 16 (over y, z).
Axes of the slice: x: 4, y: 4, z: 4, core: 2. Of those that a mesh axis runs over, the one named last changes fastest.
Arguments:
- slip_rate: float32 [2, 16777216], P(None, ('row', 'col')), may hold values from -6 to 6
- source_cluster: int32 [65536], P(('row', 'col')), may hold values from 0 to 65535, as said below
- near_kernel: float32 [8, 16, 16, 512, 512], P('row', 'col'), may hold values from -0.1875 to 0.1875
- near_pattern: int32 [8, 16, 2, 16], P('row', 'col'), may hold values from 0 to 511, as said below
- far_left: bfloat16 [8, 16, 96, 32, 512], P('row', 'col'), may hold values from -0.3125 to 0.3125
- far_right: bfloat16 [8, 16, 96, 32, 512], P('row', 'col'), may hold values from -0.25 to 0.25
- far_pattern: int32 [8, 16, 2, 96], P('row', 'col'), may hold values from 0 to 511, as said below
- stress: float32 [2, 262144], P(None, ('row', 'col')), may hold values from -1 to 1
- state: float32 [262144], P(('row', 'col')), may hold values from -0.5 to 0.5
- fault_of_row: int32 [262144], P(('row', 'col')), may hold values from 0 to 39
- direct_effect: float32 [40], replicated, may hold values from 0.5 to 1
- evolution_effect: float32 [40], replicated, may hold values from 0.5 to 1.5
- normal_stress: float32 [40], replicated, may hold values from 2 to 4
Outputs:
- new_stress: float32 [2, 262144], P(None, ('row', 'col'))
- new_rate: float32 [262144], P(('row', 'col'))
- new_state: float32 [262144], P(('row', 'col'))
The draws below stay inside these ranges and needn't reach their ends.
Inputs may be any that keep to these rules, and one draw needn't show every extreme that they name: `source_cluster`: A permutation of the 65536 fault clusters. Of the 512 positions held by one device, at most 8 name clusters of one and the same device's block of 512 fault clusters, and some pair reaches 8. `near_pattern`: entries [.., 0, n] are below 128, entries [.., 1, n] below 512. On one device, the dense and far blocks of one piece have distinct row clusters. `far_pattern`: as for near_pattern, jointly with it.
All inputs are finite; a program needn't handle non-finite values.
Results may differ from the reference program's by a relative error of at most 0.0016.
Values sent between devices are 32-bit elements; how exact they have to be, the bound alone decides.
No kernel may reach another device: no remote copies, remote signals or barrier semaphores. Data moves between devices by JAX's collectives and lax.ppermute only.
A program may use at most 128 MiB of HBM per device.

```python
import math
import jax
import jax.numpy as jnp
import numpy as np
from jax import lax

B = 256
R = 32
CLU_DEV = 512
RC_DEV = 128
NP = 2
FP = 12
FAULTS = 40
NCL = 65536
NE = 16777216
NEAR_DEV = 16
FAR_DEV = 96
ROWS = 262144
N_ROW = 8
N_COL = 16


def shuffle_range(key_one, length):
    return jax.random.permutation(key_one, length)


def draw_source_cluster(key, part):
    key = jax.random.fold_in(key, 11)
    senders = N_ROW * N_COL
    base = CLU_DEV // senders
    keys = jax.random.split(key, 5)
    swing = jax.random.randint(keys[0], (senders // 2,), 0, base + 1)
    swing = swing.at[0].set(base)
    quotas = jnp.stack([base + swing, base - swing], axis=1).reshape(senders)
    bounds = jnp.cumsum(quotas)
    position = jnp.arange(CLU_DEV, dtype=jnp.int32)
    segment = jnp.sum((position[:, None] >= bounds[None, :]).astype(jnp.int32), axis=1)
    sender_label = jax.random.permutation(keys[1], senders)
    target_label = jax.random.permutation(keys[2], senders)
    sender_of_label = jnp.argsort(sender_label)
    dest_shuffle = jax.vmap(lambda one: shuffle_range(one, CLU_DEV))(jax.random.split(keys[3], senders))
    send_shuffle = jax.vmap(lambda one: shuffle_range(one, CLU_DEV))(jax.random.split(keys[4], senders))
    labels = (target_label[:, None] - segment[dest_shuffle]) % senders
    sending = sender_of_label[labels]
    values = sending * CLU_DEV + send_shuffle[sending, dest_shuffle]
    return values.reshape(senders * CLU_DEV).astype(jnp.int32)


def block_pattern(key):
    pieces = N_ROW * N_ROW * N_COL
    keys = jax.random.split(jax.random.fold_in(key, 5), 2)
    shuffled = jax.vmap(lambda one: shuffle_range(one, RC_DEV))(jax.random.split(keys[0], pieces))
    chosen = shuffled[:, :NP + FP]
    columns = jax.random.randint(keys[1], (pieces, NP + FP), 0, CLU_DEV)
    return jnp.stack([chosen, columns], axis=1).reshape(N_ROW, N_COL, N_ROW, 2, NP + FP)


def draw_near_pattern(key, part):
    joint = block_pattern(key)
    near_part = joint[:, :, :, :, :NP]
    return jnp.transpose(near_part, (0, 1, 3, 2, 4)).reshape(N_ROW, N_COL, 2, N_ROW * NP).astype(jnp.int32)


def draw_far_pattern(key, part):
    joint = block_pattern(key)
    far_part = joint[:, :, :, :, NP:]
    return jnp.transpose(far_part, (0, 1, 3, 2, 4)).reshape(N_ROW, N_COL, 2, N_ROW * FP).astype(jnp.int32)


def place_ends(values, rng, smallest, high):
    spot = [jax.random.randint(jax.random.fold_in(rng, axis), (), 0, length) for axis, length in enumerate(values.shape)]
    widest = values.shape.index(max(values.shape))
    next_to = spot[:widest] + [(spot[widest] + 1) % values.shape[widest]] + spot[widest + 1:]
    return values.at[tuple(spot)].set(smallest).at[tuple(next_to)].set(high)


def block_scale(own_key, dims, cuts, least, high):
    factor_of = 1.0
    for axis_at, blocks in cuts:
        steps = jax.random.uniform(jax.random.fold_in(jax.random.fold_in(own_key, 6), axis_at), (blocks,), jnp.float32, least / len(cuts), high / len(cuts))
        factor_of = factor_of * jnp.repeat(jnp.exp(steps), dims[axis_at] // blocks).reshape((-1,) + (1,) * (len(dims) - 1 - axis_at))
    return factor_of


def rank_bounds(count, skew):
    weights = [(1 << 20) // math.isqrt(rank ** skew) + 1 for rank in range(1, count + 1)]
    spread = 1 + sum(weights) // (1 << 30)
    return np.cumsum(np.array([max(1, weight // spread) for weight in weights]))


def ranked_ids(own_key, extent, amount, lean):
    listing = rank_bounds(amount, lean)
    ticket = jax.random.randint(jax.random.fold_in(own_key, 1), extent, 0, int(listing[amount - 1]))
    rank = jnp.searchsorted(jnp.asarray(listing, jnp.int32), ticket, side="right")
    return jax.random.permutation(jax.random.fold_in(own_key, 2), amount)[rank].astype(jnp.int32)


def normal_values(rng, shape, width, reach, cuts=(), held_as=jnp.bfloat16):
    result = width * jax.random.normal(rng, shape, jnp.float32)
    if cuts:
        result = result * block_scale(rng, shape, cuts, -0.22, 0.18)
    return jnp.clip(result, -reach, reach).astype(held_as)


def setup_inputs(seed: int = 0) -> dict:
    splits = jax.random.split(jax.random.key(seed), 14)
    return {
        "slip_rate": normal_values(splits[0], (2, NE), 1.0, 6.0, ((1, 128),), jnp.float32),
        "source_cluster": draw_source_cluster(jax.random.fold_in(splits[13], 71), 0),
        "near_kernel": normal_values(splits[2], (N_ROW, N_COL, NEAR_DEV, 2 * B, 2 * B), (2 * B * NEAR_DEV * N_COL // RC_DEV) ** -0.5, 0.1875, ((0, 8), (1, 16)), jnp.float32),
        "near_pattern": draw_near_pattern(jax.random.fold_in(splits[13], 71), 0),
        "far_left": normal_values(splits[4], (N_ROW, N_COL, FAR_DEV, R, 2 * B), (R * FAR_DEV * N_COL // RC_DEV) ** -0.5, 0.3125, ((0, 8), (1, 16))),
        "far_right": normal_values(splits[5], (N_ROW, N_COL, FAR_DEV, R, 2 * B), (2 * B) ** -0.5, 0.25, ((0, 8), (1, 16))),
        "far_pattern": draw_far_pattern(jax.random.fold_in(splits[13], 71), 0),
        "stress": jnp.clip(jax.random.uniform(splits[7], (2, ROWS), jnp.float32, -1.0, 1.0) * block_scale(splits[7], (2, ROWS), ((1, 128),), -0.4, 0.0), -1.0, 1.0),
        "state": jnp.clip(jax.random.uniform(splits[8], (ROWS,), jnp.float32, -0.5, 0.5) * block_scale(splits[8], (ROWS,), ((0, 128),), -0.4, 0.0), -0.5, 0.5),
        "fault_of_row": place_ends(ranked_ids(splits[9], (ROWS,), FAULTS, 2), jax.random.fold_in(splits[9], 3), 0, FAULTS - 1).astype(jnp.int32),
        "direct_effect": jnp.clip(jnp.exp(jax.random.uniform(splits[10], (FAULTS,), jnp.float32, math.log(0.5), math.log(1.0))), 0.5, 1.0),
        "evolution_effect": jnp.clip(jnp.exp(jax.random.uniform(splits[11], (FAULTS,), jnp.float32, math.log(0.5), math.log(1.5))), 0.5, 1.5),
        "normal_stress": jnp.clip(jnp.exp(jax.random.uniform(splits[12], (FAULTS,), jnp.float32, math.log(2.0), math.log(4.0))), 2.0, 4.0),
    }


def reference(slip_rate, source_cluster, near_kernel, near_pattern, far_left, far_right, far_pattern, stress, state, fault_of_row, direct_effect, evolution_effect, normal_stress):
    highest = lax.Precision.HIGHEST
    clusters = slip_rate.reshape(2, NCL, B)
    column = jnp.take(clusters, source_cluster, axis=1).reshape(2, N_ROW, N_COL, CLU_DEV, B)
    near_piece = jnp.arange(NEAR_DEV, dtype=jnp.int32) // NP
    far_piece = jnp.arange(FAR_DEV, dtype=jnp.int32) // FP
    owners = jnp.arange(N_COL, dtype=jnp.int32)

    def one_row(inputs):
        kernel_rows, near_index, left_factor, right_factor, far_index = inputs
        src_near = column[:, near_piece[None, :], owners[:, None], near_index[:, 1, :], :]
        src_near = jnp.transpose(src_near, (1, 2, 0, 3)).reshape(N_COL, NEAR_DEV, 2 * B)
        near_out = jnp.einsum('cnij,cnj->cni', kernel_rows, src_near, precision=highest).reshape(N_COL, NEAR_DEV, 2, B)
        src_far = column[:, far_piece[None, :], owners[:, None], far_index[:, 1, :], :]
        src_far = jnp.transpose(src_far, (1, 2, 0, 3)).reshape(N_COL, FAR_DEV, 2 * B)
        rounded = lax.optimization_barrier(src_far.astype(jnp.bfloat16)).astype(jnp.float32)
        coefficients = jnp.einsum('cnkj,cnj->cnk', right_factor.astype(jnp.float32), rounded, precision=highest)
        coefficients = lax.optimization_barrier(coefficients.astype(jnp.bfloat16)).astype(jnp.float32)
        far_out = jnp.einsum('cnki,cnk->cni', left_factor.astype(jnp.float32), coefficients, precision=highest).reshape(N_COL, FAR_DEV, 2, B)
        summed = jnp.zeros((RC_DEV, 2, B), jnp.float32)
        summed = summed.at[near_index[:, 0, :]].add(near_out)
        summed = summed.at[far_index[:, 0, :]].add(far_out)
        return summed
    rows_all = lax.map(one_row, (near_kernel, near_pattern, far_left, far_right, far_pattern))
    stress_rate = jnp.transpose(rows_all, (2, 0, 1, 3)).reshape(2, ROWS)
    new_stress = stress + 0.25 * stress_rate
    a_row = direct_effect[fault_of_row]
    b_row = evolution_effect[fault_of_row]
    sigma_row = normal_stress[fault_of_row]
    magnitude = jnp.sqrt(new_stress[0] * new_stress[0] + new_stress[1] * new_stress[1] + 1.0)
    new_rate = 2.0 * jnp.exp(-state / a_row) * jnp.sinh(magnitude / (a_row * sigma_row))
    new_state = state + 0.25 * b_row * (jnp.exp(-state / b_row) - new_rate)
    return (new_stress, new_rate, new_state)
```

```python
import functools

import jax
import jax.numpy as jnp
from jax import lax
from jax.experimental import pallas as pl
from jax.experimental.pallas import tpu as pltpu
from jax.sharding import PartitionSpec as P

B = 256
R = 32
CLU_DEV = 512
RC_DEV = 128
NP = 2
FP = 12
N_ROW = 8
N_COL = 16
NEAR = N_ROW * NP
FAR = N_ROW * FP
BLOCKS = NEAR + FAR
LANES = 128
CAP = 8
ROUNDS = 16
FAULTS = 40
STEP_SIZE = 0.25

VMEM = pl.BlockSpec(memory_space=pltpu.VMEM)
SMEM = pl.BlockSpec(memory_space=pltpu.SMEM)
f32 = jnp.float32
bf16 = jnp.bfloat16
i32 = jnp.int32


def iota(shape, dim):
    return lax.broadcasted_iota(i32, shape, dim)


def piece_of(n):
    return jnp.where(n < NEAR, n >> 1, ((n - NEAR) * 43) >> 9)


def active_in(n, rnd):
    piece = piece_of(n)
    within = jnp.where(n < NEAR, n & 1, 2 + (n - NEAR) - FP * piece)
    half = (within >= 7).astype(i32)
    return (n < BLOCKS) & ((rnd < 0) | ((piece == (rnd >> 1)) & (half == (rnd & 1))))


def index_kernel(info_ref, g_ref, req_ref, pos_ref):
    rho = info_ref[0]
    rnd = info_ref[1]
    tables = g_ref[:, 0:CLU_DEV]
    m = g_ref[:, CLU_DEV : CLU_DEV + LANES]
    n = iota((N_ROW, LANES), 1)
    active = active_in(n, rnd)
    tab = jnp.concatenate([tables >> 8, tables & 255], axis=0).astype(f32).astype(bf16)
    piece_mask = (iota((N_ROW, LANES), 0) == piece_of(n)).astype(f32)
    place = iota((CLU_DEV, LANES), 0)
    rows = []
    for r in range(N_ROW):
        onehot = (place == m[r : r + 1, :]).astype(f32).astype(bf16)
        found = jnp.dot(tab, onehot, preferred_element_type=f32)
        value = found[0:N_ROW] * 256.0 + found[N_ROW : 2 * N_ROW]
        rows.append(jnp.sum(value * piece_mask, axis=0, keepdims=True))
    gid = jnp.concatenate(rows, axis=0).astype(i32)
    owner = jnp.where(active, gid >> 9, -1)
    local = gid & (CLU_DEV - 1)
    eye = (iota((LANES, LANES), 0) == iota((LANES, LANES), 1)).astype(f32).astype(bf16)
    owner_t = lax.dot_general(
        eye, owner.astype(f32).astype(bf16), (((1,), (1,)), ((), ())), preferred_element_type=f32
    ).astype(i32)
    before = iota((LANES, LANES), 0) < iota((LANES, LANES), 1)
    slots = []
    for r in range(N_ROW):
        same = (owner_t[:, r : r + 1] == owner[r : r + 1, :]) & before
        slots.append(jnp.sum(same.astype(f32), axis=0, keepdims=True))
    slot = jnp.concatenate(slots, axis=0).astype(i32)
    over = jnp.max(jnp.where(active & (slot >= CAP), 1.0, 0.0))
    pos_ref[...] = jnp.clip(owner * CAP + slot, 0, N_ROW * N_COL * CAP - 1)
    mine = (owner >> 4) == rho
    col_label = iota((N_COL, LANES), 0)
    target = iota((LANES, LANES), 0)
    total = jnp.zeros((2 * N_COL, LANES), f32)
    for r in range(N_ROW):
        sel = (col_label == (owner[r : r + 1, :] & (N_COL - 1))) & mine[r : r + 1, :]
        part = jnp.concatenate(
            [
                jnp.where(sel, local[r : r + 1, :] >> 8, 0),
                jnp.where(sel, local[r : r + 1, :] & 255, 0),
            ],
            axis=0,
        )
        want = jnp.where(slot[r : r + 1, :] < CAP, r * CAP + slot[r : r + 1, :], -1)
        put = (target == want).astype(f32).astype(bf16)
        total = total + lax.dot_general(
            part.astype(f32).astype(bf16), put, (((1,), (1,)), ((), ())), preferred_element_type=f32
        )
    req = total[0:N_COL] * 256.0 + total[N_COL : 2 * N_COL]
    req = jnp.where(iota((N_COL, LANES), 1) == N_ROW * CAP, over, req)
    req_ref[...] = req.astype(i32)


def make_index(info, gathered):
    return pl.pallas_call(
        index_kernel,
        out_shape=(
            jax.ShapeDtypeStruct((N_COL, LANES), i32),
            jax.ShapeDtypeStruct((N_ROW, LANES), i32),
        ),
        in_specs=[SMEM, VMEM],
        out_specs=(VMEM, VMEM),
        name="index",
    )(info, gathered)


def gather_kernel(idx_ref, slip_ref, out_ref, over_ref):
    def one_col(c, over):
        for r in range(N_ROW):
            for k in range(CAP):
                j = idx_ref[c, r * CAP + k]
                out_ref[(r * N_COL + c) * CAP + k] = slip_ref[j]
        return jnp.maximum(over, idx_ref[c, N_ROW * CAP])

    over_ref[0] = lax.fori_loop(0, N_COL, one_col, jnp.int32(0))


def gather_rows(idx, slip):
    return pl.pallas_call(
        gather_kernel,
        out_shape=(
            jax.ShapeDtypeStruct((N_ROW * N_COL * CAP, 2, B), f32),
            jax.ShapeDtypeStruct((1,), i32),
        ),
        in_specs=[SMEM, VMEM],
        out_specs=(VMEM, SMEM),
        name="gather",
    )(idx, slip)


def blocks_kernel(
    info_ref, pos_ref, near_row_ref, far_row_ref, x_ref, near_ref, left_ref, right_ref, out_ref, acc_ref
):
    p = pl.program_id(0)
    me = info_ref[0]

    @pl.when(p == 0)
    def _():
        out_ref[...] = jnp.zeros_like(out_ref)
        acc_ref[...] = jnp.zeros_like(acc_ref)

    chunk = 64
    lane = iota((chunk, LANES), 1)
    for t in range(NP):
        n = p * NP + t
        x = x_ref[pos_ref[me, n]]
        x0, x1 = x[0:1, :], x[1:2, :]
        here = lane == near_row_ref[0, n]
        for s in range(0, 2 * B, chunk):
            rows = pl.ds(s, chunk)
            prod = near_ref[t, rows, 0:B] * x0 + near_ref[t, rows, B : 2 * B] * x1
            total = jnp.sum(prod[:, 0:LANES] + prod[:, LANES:B], axis=1, keepdims=True)
            old = acc_ref[rows, :]
            acc_ref[rows, :] = jnp.where(here, old + total, old)
    for t in range(FP):
        n = p * FP + t
        x = x_ref[pos_ref[me, NEAR + n]].astype(bf16).astype(f32)
        right = right_ref[t].astype(f32)
        prod = right[:, 0:B] * x[0:1, :] + right[:, B : 2 * B] * x[1:2, :]
        coef = jnp.sum(prod[:, 0:LANES] + prod[:, LANES:B], axis=1, keepdims=True)
        coef = coef.astype(bf16).astype(f32)
        far = jnp.sum(left_ref[t].astype(f32) * coef, axis=0, keepdims=True)
        row = pl.ds(far_row_ref[0, n], 1)
        out_ref[row, :] = out_ref[row, :] + far

    @pl.when(p == N_ROW - 1)
    def _():
        out_ref[...] = out_ref[...] + acc_ref[...].T


def block_sums(info, pos, near_index, far_index, x, near, left, right):
    return pl.pallas_call(
        blocks_kernel,
        grid=(N_ROW,),
        out_shape=jax.ShapeDtypeStruct((RC_DEV, 2 * B), f32),
        in_specs=[
            SMEM,
            SMEM,
            SMEM,
            SMEM,
            pl.BlockSpec(x.shape, lambda p: (0, 0, 0)),
            pl.BlockSpec((NP, 2 * B, 2 * B), lambda p: (p, 0, 0)),
            pl.BlockSpec((FP, R, 2 * B), lambda p: (p, 0, 0)),
            pl.BlockSpec((FP, R, 2 * B), lambda p: (p, 0, 0)),
        ],
        out_specs=pl.BlockSpec((RC_DEV, 2 * B), lambda p: (0, 0)),
        scratch_shapes=[pltpu.VMEM((2 * B, LANES), f32)],
        compiler_params=pltpu.CompilerParams(vmem_limit_bytes=24 * 1024 * 1024),
        name="blocks",
    )(info, pos, near_index, far_index, x, near, left, right)


def final_kernel(
    a_ref, b_ref, s_ref, parts_ref, stress_ref, state_ref, fault_ref, out_stress, out_rate, out_state
):
    total = parts_ref[0]
    for c in range(1, N_COL):
        total = total + parts_ref[c]
    groups = RC_DEV // N_COL
    for h in range(2):
        every = pl.ds(h, groups, stride=2)
        state = state_ref[every, :]
        fault = fault_ref[every, :]
        a = jnp.zeros_like(state)
        b = jnp.zeros_like(state)
        sigma = jnp.zeros_like(state)
        for f in range(FAULTS):
            here = fault == f
            a = jnp.where(here, a_ref[f], a)
            b = jnp.where(here, b_ref[f], b)
            sigma = jnp.where(here, s_ref[f], sigma)
        square = jnp.ones_like(state)
        for k in range(2):
            old = jnp.concatenate(
                [
                    stress_ref[k : k + 1, g * B + h * LANES : g * B + (h + 1) * LANES]
                    for g in range(groups)
                ],
                axis=0,
            )
            new = old + STEP_SIZE * total[:, k * B + h * LANES : k * B + (h + 1) * LANES]
            for g in range(groups):
                out_stress[k : k + 1, g * B + h * LANES : g * B + (h + 1) * LANES] = new[g : g + 1, :]
            square = square + new * new
        z = jnp.sqrt(square) / (a * sigma)
        u = state / a
        rate = jnp.exp(z - u) - jnp.exp(-z - u)
        out_rate[every, :] = rate
        out_state[every, :] = state + STEP_SIZE * b * (jnp.exp(-state / b) - rate)


def finish(a, b, s, parts, stress, state, fault):
    rows = stress.shape[1] // LANES
    new_stress, new_rate, new_state = pl.pallas_call(
        final_kernel,
        out_shape=(
            jax.ShapeDtypeStruct(stress.shape, f32),
            jax.ShapeDtypeStruct((rows, LANES), f32),
            jax.ShapeDtypeStruct((rows, LANES), f32),
        ),
        in_specs=[SMEM, SMEM, SMEM, VMEM, VMEM, VMEM, VMEM],
        out_specs=(VMEM, VMEM, VMEM),
        name="finish",
    )(
        a,
        b,
        s,
        parts.reshape(N_COL, RC_DEV // N_COL, 2 * B),
        stress,
        state.reshape(rows, LANES),
        fault.reshape(rows, LANES),
    )
    return (new_stress, new_rate.reshape(-1), new_state.reshape(-1))


def body(
    slip_rate,
    source_cluster,
    near_kernel,
    near_pattern,
    far_left,
    far_right,
    far_pattern,
    stress,
    state,
    fault_of_row,
    direct_effect,
    evolution_effect,
    normal_stress,
):
    near, left, right = near_kernel[0, 0], far_left[0, 0], far_right[0, 0]
    near_index, far_index = near_pattern[0, 0], far_pattern[0, 0]
    slip = jnp.transpose(slip_rate.reshape(2, CLU_DEV, B), (1, 0, 2))
    row = lax.axis_index("row")
    payload = jnp.concatenate(
        [source_cluster, near_index[1], far_index[1], jnp.zeros((LANES - BLOCKS,), i32)]
    )
    gathered = lax.all_to_all(
        jnp.broadcast_to(payload[None, :], (N_ROW, CLU_DEV + LANES)), "row", 0, 0, tiled=True
    )

    def fetch(rnd):
        info = jnp.stack([row, rnd]).astype(i32)
        req, pos = make_index(info, gathered)
        asked = lax.all_to_all(req, "col", 0, 0, tiled=True)
        reply, over = gather_rows(asked, slip)
        return lax.all_to_all(reply, ("row", "col"), 0, 0, tiled=True), pos, over, info

    x, pos, over, info = fetch(jnp.int32(-1))
    fast = block_sums(info, pos, near_index, far_index, x, near, left, right)

    def more(carry):
        return carry[0] < jnp.where(over[0] > 0, ROUNDS, 0)

    def one_round(carry):
        rnd, total = carry
        x, pos, _, info = fetch(rnd)
        n = jnp.arange(LANES, dtype=i32)
        own = lax.dynamic_slice_in_dim(pos, row, 1, 0)[0]
        rows = jnp.where(active_in(n, rnd)[:, None, None], x[own], 0.0)
        places = jnp.broadcast_to(n[None, :], (N_ROW, LANES))
        part = block_sums(info, places, near_index, far_index, rows, near, left, right)
        return rnd + 1, jnp.where(rnd == 0, 0.0, total) + part

    _, summed = lax.while_loop(more, one_round, (jnp.int32(0), fast))
    parts = lax.all_to_all(summed, "col", 0, 0, tiled=True)
    return finish(
        direct_effect, evolution_effect, normal_stress, parts, stress, state, fault_of_row
    )


def solution(mesh):
    return jax.shard_map(
        body,
        mesh=mesh,
        in_specs=(
            P(None, ("row", "col")),
            P(("row", "col")),
            P("row", "col", None, None, None),
            P("row", "col", None, None),
            P("row", "col", None, None, None),
            P("row", "col", None, None, None),
            P("row", "col", None, None),
            P(None, ("row", "col")),
            P(("row", "col")),
            P(("row", "col")),
            P(),
            P(),
            P(),
        ),
        out_specs=(P(None, ("row", "col")), P(("row", "col")), P(("row", "col"))),
        check_vma=False,
    )
```

```python
import functools

import functools

import jax
import jax.numpy as jnp
from jax import lax
from jax.experimental import pallas as pl
from jax.experimental.pallas import tpu as pltpu
from jax.sharding import PartitionSpec as P

B = 256
R = 32
CLU_DEV = 512
RC_DEV = 128
NP = 2
FP = 12
N_ROW = 8
N_COL = 16
NEAR = N_ROW * NP
FAR = N_ROW * FP
BLOCKS = NEAR + FAR
LANES = 128
CAP_COL = 24
CAP_ROW = 32
ROUNDS = 56
PIECE_ROWS = 8
FAULTS = 40
STEP_SIZE = 0.25

VMEM = pl.BlockSpec(memory_space=pltpu.VMEM)
SMEM = pl.BlockSpec(memory_space=pltpu.SMEM)
f32 = jnp.float32
bf16 = jnp.bfloat16
i32 = jnp.int32
NT = (((1,), (1,)), ((), ()))
SMALL = pltpu.CompilerParams(vmem_limit_bytes=6 * 1024 * 1024)


def iota(shape, dim):
    return lax.broadcasted_iota(i32, shape, dim)


def exact(x):
    return x.astype(f32).astype(bf16)


def split(x):
    return jnp.concatenate([x >> 8, x & 255], axis=0)


def piece_of(n):
    return jnp.where(n < NEAR, n >> 1, ((n - NEAR) * 43) >> 9)


def active_in(n, rnd):
    if rnd is None:
        return n < BLOCKS
    piece = piece_of(n)
    within = jnp.where(n < NEAR, n & 1, NP + (n - NEAR) - FP * piece)
    of = (rnd * 37) >> 8
    return (n < BLOCKS) & (piece == of) & ((within >> 1) == rnd - 7 * of)


def payload_kernel(table_ref, near_ref, far_ref, out_ref):
    out_ref[...] = jnp.zeros_like(out_ref)
    for r in range(N_ROW):
        out_ref[r, 0:4, :] = table_ref[...]
        out_ref[r, 4:5, 0:NEAR] = near_ref[1:2, :]
        out_ref[r, 5:6, 0:FAR] = far_ref[1:2, :]
        out_ref[r, 6:7, :] = jnp.full((1, LANES), r, i32)


def make_payload(source_cluster, near_index, far_index):
    return pl.pallas_call(
        payload_kernel,
        out_shape=jax.ShapeDtypeStruct((N_ROW, PIECE_ROWS, LANES), i32),
        in_specs=[VMEM, VMEM, VMEM],
        out_specs=VMEM,
        compiler_params=SMALL,
        name="payload",
    )(source_cluster.reshape(4, LANES), near_index, far_index)


def index_kernel(g_ref, *refs):
    req_ref, snd_ref, pos_ref = refs[-3:]
    rnd = refs[0][1] if len(refs) > 3 else None
    rho = g_ref[0, 6:7, :]
    tables = jnp.concatenate([g_ref[:, q, :] for q in range(4)], axis=1)
    n = iota((N_ROW, LANES), 1)
    m = jnp.where(n < NEAR, g_ref[:, 4, :], pltpu.roll(g_ref[:, 5, :], NEAR, 1))
    active = active_in(n, rnd)
    tab = exact(split(tables))
    piece_mask = (iota((N_ROW, LANES), 0) == piece_of(n)).astype(f32)
    place = iota((CLU_DEV, LANES), 0)
    rows = []
    for r in range(N_ROW):
        onehot = exact(place == m[r : r + 1, :])
        found = jnp.dot(tab, onehot, preferred_element_type=f32)
        value = found[0:N_ROW] * 256.0 + found[N_ROW : 2 * N_ROW]
        rows.append(jnp.sum(value * piece_mask, axis=0, keepdims=True))
    gid = jnp.concatenate(rows, axis=0).astype(i32)
    owner = jnp.where(active, gid >> 9, -1)
    owner_row = owner >> 4
    local = gid & (CLU_DEV - 1)
    every = iota((LANES, LANES), 0)
    counts = jnp.zeros((LANES, LANES), f32)
    for r in range(N_ROW):
        counts = counts + (every == owner[r : r + 1, :]).astype(f32)
    most = jnp.max(jnp.sum(counts, axis=1, keepdims=True))
    col_label = iota((N_COL, LANES), 0) + rho * N_COL
    row_label = iota((N_ROW, LANES), 0)
    to_col = jnp.concatenate([(col_label == owner[r : r + 1, :]).astype(f32) for r in range(N_ROW)], axis=0)
    to_row = jnp.concatenate([(row_label == owner_row[r : r + 1, :]).astype(f32) for r in range(N_ROW)], axis=0)
    sub, lane = iota((LANES, LANES), 0), iota((LANES, LANES), 1)
    scan = jnp.concatenate([exact(sub < lane), jnp.ones((LANES, LANES), bf16)], axis=1)
    ahead = jnp.dot(to_col.astype(bf16), scan, preferred_element_type=f32)
    earlier = exact(((sub & (N_COL - 1)) == (lane & (N_COL - 1))) & (sub > lane))
    offset = jnp.dot(earlier, ahead[:, LANES:].astype(bf16), preferred_element_type=f32)
    first = to_col * (ahead[:, :LANES] + offset)
    second = to_row * jnp.dot(to_row.astype(bf16), scan[:, :LANES], preferred_element_type=f32)
    slot1 = jnp.concatenate(
        [jnp.sum(first[r * N_COL : (r + 1) * N_COL], axis=0, keepdims=True) for r in range(N_ROW)], axis=0
    ).astype(i32)
    slot2 = jnp.concatenate(
        [jnp.sum(second[r * N_ROW : (r + 1) * N_ROW], axis=0, keepdims=True) for r in range(N_ROW)], axis=0
    ).astype(i32)
    deepest = jnp.max(jnp.where(active, slot2, 0).astype(f32))
    over = jnp.where((most > CAP_COL) | (deepest >= CAP_ROW), 1, 0)
    pos = jnp.clip(owner_row * CAP_ROW + slot2, 0, N_ROW * CAP_ROW - 1)
    pos_ref[...] = jnp.sum(jnp.where(row_label == rho, pos, 0).astype(f32), axis=0, keepdims=True).astype(i32)
    mine = owner_row == rho
    pos1 = jnp.clip((owner & (N_COL - 1)) * CAP_COL + slot1, 0, N_COL * CAP_COL - 1)
    req = jnp.zeros((2 * N_COL, LANES), f32)
    snd = jnp.zeros((2 * N_ROW, LANES), f32)
    for r in range(N_ROW):
        sel = to_col[r * N_COL : (r + 1) * N_COL] > 0.5
        value = split(jnp.where(sel, local[r : r + 1, :], 0))
        put = exact(sub == jnp.where(slot1[r : r + 1, :] < CAP_COL, slot1[r : r + 1, :], -1))
        req = req + lax.dot_general(exact(value), put, NT, preferred_element_type=f32)
        value = split(jnp.where((row_label == r) & mine[r : r + 1, :], pos1[r : r + 1, :], 0))
        put = exact(sub == jnp.where(slot2[r : r + 1, :] < CAP_ROW, slot2[r : r + 1, :], -1))
        snd = snd + lax.dot_general(exact(value), put, NT, preferred_element_type=f32)
    req = (req[0:N_COL] * 256.0 + req[N_COL : 2 * N_COL]).astype(i32)
    req_ref[...] = jnp.where(iota((N_COL, LANES), 1) == LANES - 1, over, req)
    snd_ref[...] = (snd[0:N_ROW] * 256.0 + snd[N_ROW : 2 * N_ROW]).astype(i32)


def make_index(gathered, ctl):
    return pl.pallas_call(
        index_kernel,
        out_shape=(
            jax.ShapeDtypeStruct((N_COL, LANES), i32),
            jax.ShapeDtypeStruct((N_ROW, LANES), i32),
            jax.ShapeDtypeStruct((1, LANES), i32),
        ),
        in_specs=[VMEM] + [SMEM] * len(ctl),
        out_specs=(VMEM, VMEM, VMEM),
        compiler_params=SMALL,
        name="index",
    )(gathered, *ctl)


def gather_kernel(idx_ref, slip_ref, out_ref, ctl_ref):
    def one_col(c, over):
        for k in range(CAP_COL):
            out_ref[c * CAP_COL + k] = slip_ref[idx_ref[c, k]]
        return jnp.maximum(over, idx_ref[c, LANES - 1])

    ctl_ref[0] = ROUNDS * lax.fori_loop(0, N_COL, one_col, jnp.int32(0))
    ctl_ref[1] = 0


def gather_rows(idx, slip):
    return pl.pallas_call(
        gather_kernel,
        out_shape=(
            jax.ShapeDtypeStruct((N_COL * CAP_COL, 2, B), f32),
            jax.ShapeDtypeStruct((2,), i32),
        ),
        in_specs=[SMEM, VMEM],
        out_specs=(VMEM, SMEM),
        compiler_params=SMALL,
        name="gather",
    )(idx, slip)


def forward_kernel(idx_ref, got_ref, out_ref):
    def one_row(r, _):
        for k in range(CAP_ROW):
            out_ref[r * CAP_ROW + k] = got_ref[idx_ref[r, k]]
        return 0

    lax.fori_loop(0, N_ROW, one_row, 0)


def forward_rows(idx, got):
    return pl.pallas_call(
        forward_kernel,
        out_shape=jax.ShapeDtypeStruct((N_ROW * CAP_ROW, 2, B), f32),
        in_specs=[SMEM, VMEM],
        out_specs=VMEM,
        compiler_params=SMALL,
        name="forward",
    )(idx, got)


def blocks_kernel(
    steps, pos_ref, near_row_ref, far_row_ref, x_ref, near_ref, left_ref, right_ref, out_ref, acc_ref
):
    step = pl.program_id(0) if steps > 1 else 0
    near_here, pieces_here = NEAR // steps, N_ROW // steps

    @pl.when(step == 0)
    def _():
        out_ref[...] = jnp.zeros_like(out_ref)
        acc_ref[...] = jnp.zeros_like(acc_ref)

    chunk = 64
    lane = iota((chunk, LANES), 1)

    def one_near(t, _):
        n = step * near_here + t
        x = x_ref[pos_ref[0, n]]
        x0, x1 = x[0:1, :], x[1:2, :]
        here = lane == near_row_ref[0, n]
        for s in range(0, 2 * B, chunk):
            rows = pl.ds(s, chunk)
            prod = near_ref[t, rows, 0:B] * x0 + near_ref[t, rows, B : 2 * B] * x1
            total = jnp.sum(prod[:, 0:LANES] + prod[:, LANES:B], axis=1, keepdims=True)
            old = acc_ref[rows, :]
            acc_ref[rows, :] = jnp.where(here, old + total, old)
        return 0

    lax.fori_loop(0, near_here, one_near, 0)

    def some_far(p, _):
        for t in range(FP):
            at = p * FP + t
            n = step * pieces_here * FP + at
            x = x_ref[pos_ref[0, NEAR + n]].astype(bf16).astype(f32)
            right = right_ref[at].astype(f32)
            prod = right[:, 0:B] * x[0:1, :] + right[:, B : 2 * B] * x[1:2, :]
            coef = jnp.sum(prod[:, 0:LANES] + prod[:, LANES:B], axis=1, keepdims=True)
            coef = coef.astype(bf16).astype(f32)
            far = jnp.sum(left_ref[at].astype(f32) * coef, axis=0, keepdims=True)
            row = pl.ds(far_row_ref[0, n], 1)
            out_ref[row, :] = out_ref[row, :] + far
        return 0

    lax.fori_loop(0, pieces_here, some_far, 0)

    @pl.when(step == steps - 1)
    def _():
        out_ref[...] = out_ref[...] + acc_ref[...].T


def block_sums(steps, pos, near_index, far_index, x, near, left, right):
    specs = [SMEM, SMEM, SMEM, VMEM, VMEM, VMEM, VMEM]
    out_spec, extra = VMEM, {}
    if steps > 1:
        specs[4:] = [
            pl.BlockSpec((one.shape[0] // steps,) + one.shape[1:], lambda p: (p, 0, 0))
            for one in (near, left, right)
        ]
        specs[3] = pl.BlockSpec(x.shape, lambda p: (0, 0, 0))
        out_spec = pl.BlockSpec((RC_DEV, 2 * B), lambda p: (0, 0))
        extra = {"grid": (steps,)}
    return pl.pallas_call(
        functools.partial(blocks_kernel, steps),
        out_shape=jax.ShapeDtypeStruct((RC_DEV, 2 * B), f32),
        in_specs=specs,
        out_specs=out_spec,
        scratch_shapes=[pltpu.VMEM((2 * B, LANES), f32)],
        compiler_params=pltpu.CompilerParams(vmem_limit_bytes=26 * 1024 * 1024),
        cost_estimate=pl.CostEstimate(
            flops=2 * (near.size + left.size + right.size),
            transcendentals=0,
            bytes_accessed=4 * (near.size + x.size) + 2 * (left.size + right.size),
        ),
        name="blocks" if steps == 1 else "blocks_streamed",
        **extra,
    )(pos, near_index, far_index, x, near, left, right)


def final_kernel(
    a_ref, b_ref, s_ref, parts_ref, stress_ref, state_ref, fault_ref, out_stress, out_rate, out_state
):
    total = parts_ref[0]
    for c in range(1, N_COL):
        total = total + parts_ref[c]
    groups = RC_DEV // N_COL
    for h in range(2):
        every = pl.ds(h, groups, stride=2)
        state = state_ref[every, :]
        fault = fault_ref[every, :]
        a = jnp.zeros_like(state)
        b = jnp.zeros_like(state)
        sigma = jnp.zeros_like(state)
        for f in range(FAULTS):
            here = fault == f
            a = jnp.where(here, a_ref[f], a)
            b = jnp.where(here, b_ref[f], b)
            sigma = jnp.where(here, s_ref[f], sigma)
        square = jnp.ones_like(state)
        for k in range(2):
            old = jnp.concatenate(
                [
                    stress_ref[k : k + 1, g * B + h * LANES : g * B + (h + 1) * LANES]
                    for g in range(groups)
                ],
                axis=0,
            )
            new = old + STEP_SIZE * total[:, k * B + h * LANES : k * B + (h + 1) * LANES]
            for g in range(groups):
                out_stress[k : k + 1, g * B + h * LANES : g * B + (h + 1) * LANES] = new[g : g + 1, :]
            square = square + new * new
        z = jnp.sqrt(square) / (a * sigma)
        u = state / a
        rate = jnp.exp(z - u) - jnp.exp(-z - u)
        out_rate[every, :] = rate
        out_state[every, :] = state + STEP_SIZE * b * (jnp.exp(-state / b) - rate)


def finish(a, b, s, parts, stress, state, fault):
    rows = stress.shape[1] // LANES
    new_stress, new_rate, new_state = pl.pallas_call(
        final_kernel,
        out_shape=(
            jax.ShapeDtypeStruct(stress.shape, f32),
            jax.ShapeDtypeStruct((rows, LANES), f32),
            jax.ShapeDtypeStruct((rows, LANES), f32),
        ),
        in_specs=[SMEM, SMEM, SMEM, VMEM, VMEM, VMEM, VMEM],
        out_specs=(VMEM, VMEM, VMEM),
        compiler_params=SMALL,
        name="finish",
    )(
        a,
        b,
        s,
        parts.reshape(N_COL, RC_DEV // N_COL, 2 * B),
        stress,
        state.reshape(rows, LANES),
        fault.reshape(rows, LANES),
    )
    return (new_stress, new_rate.reshape(-1), new_state.reshape(-1))


def body(
    slip_rate,
    source_cluster,
    near_kernel,
    near_pattern,
    far_left,
    far_right,
    far_pattern,
    stress,
    state,
    fault_of_row,
    direct_effect,
    evolution_effect,
    normal_stress,
):
    near, left, right = near_kernel[0, 0], far_left[0, 0], far_right[0, 0]
    near_index, far_index = near_pattern[0, 0], far_pattern[0, 0]
    slip = jnp.transpose(slip_rate.reshape(2, CLU_DEV, B), (1, 0, 2))
    gathered = lax.all_to_all(
        make_payload(source_cluster, near_index, far_index), "row", 0, 0, tiled=True
    )

    def fetch(*ctl):
        req, snd, pos = make_index(gathered, ctl)
        asked = lax.all_to_all(req, "col", 0, 0, tiled=True)
        reply, now = gather_rows(asked, slip)
        got = lax.all_to_all(reply, "col", 0, 0, tiled=True)
        return lax.all_to_all(forward_rows(snd, got), "row", 0, 0, tiled=True), pos, now

    x, pos, ctl = fetch()
    fast = block_sums(1, pos, near_index, far_index, x, near, left, right)

    def more(carry):
        return carry[0][1] < carry[0][0]

    def one_round(carry):
        ctl, total = carry
        x, pos, _ = fetch(ctl)
        n = jnp.arange(LANES, dtype=i32)
        rows = jnp.where(active_in(n, ctl[1])[:, None, None], x[pos[0]], 0.0)
        rows = jnp.concatenate([rows, jnp.zeros_like(rows)], axis=0)
        part = block_sums(N_ROW, n[None, :], near_index, far_index, rows, near, left, right)
        return ctl + jnp.arange(2, dtype=i32), jnp.where(ctl[1] == 0, 0.0, total) + part

    _, summed = lax.while_loop(more, one_round, (ctl, fast))
    parts = lax.all_to_all(summed, "col", 0, 0, tiled=True)
    return finish(
        direct_effect, evolution_effect, normal_stress, parts, stress, state, fault_of_row
    )


def solution(mesh):
    return jax.shard_map(
        body,
        mesh=mesh,
        in_specs=(
            P(None, ("row", "col")),
            P(("row", "col")),
            P("row", "col", None, None, None),
            P("row", "col", None, None),
            P("row", "col", None, None, None),
            P("row", "col", None, None, None),
            P("row", "col", None, None),
            P(None, ("row", "col")),
            P(("row", "col")),
            P(("row", "col")),
            P(),
            P(),
            P(),
        ),
        out_specs=(P(None, ("row", "col")), P(("row", "col")), P(("row", "col"))),
        check_vma=False,
    )
```

```python
import functools

import functools

import jax
import jax.numpy as jnp
from jax import lax
from jax.experimental import pallas as pl
from jax.experimental.pallas import tpu as pltpu
from jax.sharding import PartitionSpec as P

B = 256
R = 32
CLU_DEV = 512
RC_DEV = 128
NP = 2
FP = 12
N_ROW = 8
N_COL = 16
NEAR = N_ROW * NP
FAR = N_ROW * FP
BLOCKS = NEAR + FAR
LANES = 128
CAP_COL = 24
CAP_ROW = 32
HELD_A = 4
HELD_B = 2
GROUP = 2
ROUNDS = 56
PIECE_ROWS = 8
FAULTS = 40
STEP_SIZE = 0.25

VMEM = pl.BlockSpec(memory_space=pltpu.VMEM)
SMEM = pl.BlockSpec(memory_space=pltpu.SMEM)
HBM = pl.BlockSpec(memory_space=pltpu.HBM)
f32 = jnp.float32
bf16 = jnp.bfloat16
i32 = jnp.int32
NT = (((1,), (1,)), ((), ()))
SMALL = pltpu.CompilerParams(vmem_limit_bytes=6 * 1024 * 1024)


def in_hbm(x):
    return pltpu.with_memory_space_constraint(x, pltpu.HBM)


def call(kernel, ins, specs, outs, out_specs, name, staged=()):
    count, given, made = len(staged), len(ins), len(outs)

    def run(*refs):
        held = refs[given + count + made : given + 2 * count + made]
        copies = [
            pltpu.make_async_copy(one.at[pl.ds(first, size)], to, done)
            for one, to, done, (_, first, size) in zip(
                refs[given : given + count], held, refs[given + 2 * count + made :], staged
            )
        ]
        for copy in copies:
            copy.start()
        kernel(*refs[:given], *refs[given + count : given + count + made])
        for copy in copies:
            copy.wait()

    return pl.pallas_call(
        run,
        out_shape=tuple(outs)
        + tuple(pltpu.VMEM((size,) + one.shape[1:], one.dtype) for one, _, size in staged),
        in_specs=list(specs) + [HBM] * count,
        out_specs=tuple(out_specs) + (VMEM,) * count,
        scratch_shapes=[pltpu.SemaphoreType.DMA] * count,
        compiler_params=SMALL,
        name=name,
    )(*ins, *(in_hbm(one) for one, _, _ in staged))


def iota(shape, dim):
    return lax.broadcasted_iota(i32, shape, dim)


def exact(x):
    return x.astype(f32).astype(bf16)


def split(x):
    return jnp.concatenate([x >> 8, x & 255], axis=0)


def piece_of(n):
    return jnp.where(n < NEAR, n >> 1, ((n - NEAR) * 43) >> 9)


def active_in(n, rnd):
    if rnd is None:
        return n < BLOCKS
    piece = piece_of(n)
    within = jnp.where(n < NEAR, n & 1, NP + (n - NEAR) - FP * piece)
    of = (rnd * 37) >> 8
    return (n < BLOCKS) & (piece == of) & ((within >> 1) == rnd - 7 * of)


def payload_kernel(table_ref, near_ref, far_ref, out_ref):
    out_ref[...] = jnp.zeros_like(out_ref)
    for r in range(N_ROW):
        out_ref[r, 0:4, :] = table_ref[...]
        out_ref[r, 4:5, 0:NEAR] = near_ref[1:2, :]
        out_ref[r, 5:6, 0:FAR] = far_ref[1:2, :]
        out_ref[r, 6:7, :] = jnp.full((1, LANES), r, i32)


def make_payload(source_cluster, near_index, far_index, staged):
    return call(
        payload_kernel,
        (source_cluster.reshape(4, LANES), near_index, far_index),
        [VMEM, VMEM, VMEM],
        (jax.ShapeDtypeStruct((N_ROW, PIECE_ROWS, LANES), i32),),
        (VMEM,),
        "payload",
        staged,
    )


def index_kernel(g_ref, *refs):
    req_ref, snd_ref, pos_ref = refs[-3:]
    rnd = refs[0][0] if len(refs) > 3 else None
    rho = g_ref[0, 6:7, :]
    tables = jnp.concatenate([g_ref[:, q, :] for q in range(4)], axis=1)
    n = iota((N_ROW, LANES), 1)
    m = jnp.where(n < NEAR, g_ref[:, 4, :], pltpu.roll(g_ref[:, 5, :], NEAR, 1))
    active = active_in(n, rnd)
    tab = exact(split(tables))
    piece_mask = (iota((N_ROW, LANES), 0) == piece_of(n)).astype(f32)
    place = iota((CLU_DEV, LANES), 0)
    rows = []
    for r in range(N_ROW):
        onehot = exact(place == m[r : r + 1, :])
        found = jnp.dot(tab, onehot, preferred_element_type=f32)
        value = found[0:N_ROW] * 256.0 + found[N_ROW : 2 * N_ROW]
        rows.append(jnp.sum(value * piece_mask, axis=0, keepdims=True))
    gid = jnp.concatenate(rows, axis=0).astype(i32)
    owner = jnp.where(active, gid >> 9, -1)
    owner_row = owner >> 4
    local = gid & (CLU_DEV - 1)
    every = iota((LANES, LANES), 0)
    counts = jnp.zeros((LANES, LANES), f32)
    for r in range(N_ROW):
        counts = counts + (every == owner[r : r + 1, :]).astype(f32)
    most = jnp.max(jnp.sum(counts, axis=1, keepdims=True))
    col_label = iota((N_COL, LANES), 0) + rho * N_COL
    row_label = iota((N_ROW, LANES), 0)
    to_col = jnp.concatenate([(col_label == owner[r : r + 1, :]).astype(f32) for r in range(N_ROW)], axis=0)
    to_row = jnp.concatenate([(row_label == owner_row[r : r + 1, :]).astype(f32) for r in range(N_ROW)], axis=0)
    sub, lane = iota((LANES, LANES), 0), iota((LANES, LANES), 1)
    scan = jnp.concatenate([exact(sub < lane), jnp.ones((LANES, LANES), bf16)], axis=1)
    ahead = jnp.dot(to_col.astype(bf16), scan, preferred_element_type=f32)
    earlier = exact(((sub & (N_COL - 1)) == (lane & (N_COL - 1))) & (sub > lane))
    offset = jnp.dot(earlier, ahead[:, LANES:].astype(bf16), preferred_element_type=f32)
    first = to_col * (ahead[:, :LANES] + offset)
    second = to_row * jnp.dot(to_row.astype(bf16), scan[:, :LANES], preferred_element_type=f32)
    slot1 = jnp.concatenate(
        [jnp.sum(first[r * N_COL : (r + 1) * N_COL], axis=0, keepdims=True) for r in range(N_ROW)], axis=0
    ).astype(i32)
    slot2 = jnp.concatenate(
        [jnp.sum(second[r * N_ROW : (r + 1) * N_ROW], axis=0, keepdims=True) for r in range(N_ROW)], axis=0
    ).astype(i32)
    deepest = jnp.max(jnp.where(active, slot2, 0).astype(f32))
    over = jnp.where((most > CAP_COL) | (deepest >= CAP_ROW), 1, 0)
    pos = jnp.clip(owner_row * CAP_ROW + slot2, 0, N_ROW * CAP_ROW - 1)
    pos_ref[...] = jnp.sum(jnp.where(row_label == rho, pos, 0).astype(f32), axis=0, keepdims=True).astype(i32)
    mine = owner_row == rho
    pos1 = jnp.clip((owner & (N_COL - 1)) * CAP_COL + slot1, 0, N_COL * CAP_COL - 1)
    req = jnp.zeros((2 * N_COL, LANES), f32)
    snd = jnp.zeros((2 * N_ROW, LANES), f32)
    for r in range(N_ROW):
        sel = to_col[r * N_COL : (r + 1) * N_COL] > 0.5
        value = split(jnp.where(sel, local[r : r + 1, :], 0))
        put = exact(sub == jnp.where(slot1[r : r + 1, :] < CAP_COL, slot1[r : r + 1, :], -1))
        req = req + lax.dot_general(exact(value), put, NT, preferred_element_type=f32)
        value = split(jnp.where((row_label == r) & mine[r : r + 1, :], pos1[r : r + 1, :], 0))
        put = exact(sub == jnp.where(slot2[r : r + 1, :] < CAP_ROW, slot2[r : r + 1, :], -1))
        snd = snd + lax.dot_general(exact(value), put, NT, preferred_element_type=f32)
    req = (req[0:N_COL] * 256.0 + req[N_COL : 2 * N_COL]).astype(i32)
    req_ref[...] = jnp.where(iota((N_COL, LANES), 1) == LANES - 1, over, req)
    snd_ref[...] = (snd[0:N_ROW] * 256.0 + snd[N_ROW : 2 * N_ROW]).astype(i32)


def make_index(gathered, done, staged=()):
    square = jax.ShapeDtypeStruct((N_ROW, LANES), i32)
    return call(
        index_kernel,
        (gathered, *done),
        [VMEM] + [SMEM] * len(done),
        (jax.ShapeDtypeStruct((N_COL, LANES), i32), square, jax.ShapeDtypeStruct((1, LANES), i32)),
        (VMEM, VMEM, VMEM),
        "index",
        staged,
    )


def gather_kernel(idx_ref, slip_ref, out_ref, rounds_ref, done_ref):
    def one_col(c, over):
        for k in range(CAP_COL):
            out_ref[c * CAP_COL + k] = slip_ref[idx_ref[c, k]]
        return jnp.maximum(over, idx_ref[c, LANES - 1])

    rounds_ref[0] = ROUNDS * lax.fori_loop(0, N_COL, one_col, jnp.int32(0))
    done_ref[0] = 0


def gather_rows(idx, slip, staged=()):
    one = jax.ShapeDtypeStruct((1,), i32)
    return call(
        gather_kernel,
        (idx, slip),
        [SMEM, VMEM],
        (jax.ShapeDtypeStruct((N_COL * CAP_COL, 2, B), f32), one, one),
        (VMEM, SMEM, SMEM),
        "gather",
        staged,
    )


def forward_kernel(idx_ref, got_ref, out_ref):
    def one_row(r, _):
        for k in range(CAP_ROW):
            out_ref[r * CAP_ROW + k] = got_ref[idx_ref[r, k]]
        return 0

    lax.fori_loop(0, N_ROW, one_row, 0)


def forward_rows(idx, got, staged=()):
    return call(
        forward_kernel,
        (idx, got),
        [SMEM, VMEM],
        (jax.ShapeDtypeStruct((N_ROW * CAP_ROW, 2, B), f32),),
        (VMEM,),
        "forward",
        staged,
    )


CHUNK = 64


def add_near(acc_ref, near_ref, at, x, row):
    x0, x1 = x[0:1, :], x[1:2, :]
    here = iota((CHUNK, LANES), 1) == row
    for s in range(0, 2 * B, CHUNK):
        rows = pl.ds(s, CHUNK)
        prod = near_ref[at, rows, 0:B] * x0 + near_ref[at, rows, B : 2 * B] * x1
        total = jnp.sum(prod[:, 0:LANES] + prod[:, LANES:B], axis=1, keepdims=True)
        old = acc_ref[rows, :]
        acc_ref[rows, :] = jnp.where(here, old + total, old)


def add_far(out_ref, left_ref, right_ref, at, x, row):
    x = x.astype(bf16).astype(f32)
    right = right_ref[at].astype(f32)
    prod = right[:, 0:B] * x[0:1, :] + right[:, B : 2 * B] * x[1:2, :]
    coef = jnp.sum(prod[:, 0:LANES] + prod[:, LANES:B], axis=1, keepdims=True)
    coef = coef.astype(bf16).astype(f32)
    far = jnp.sum(left_ref[at].astype(f32) * coef, axis=0, keepdims=True)
    rows = pl.ds(row, 1)
    out_ref[rows, :] = out_ref[rows, :] + far


def blocks_kernel(
    pos_ref, near_row_ref, far_row_ref, x_ref, held_a, held_b, left_ref, right_ref, near_ref,
    out_ref, acc_ref, rest_ref, sems,
):
    first = HELD_A + HELD_B
    copies = [
        pltpu.make_async_copy(
            near_ref.at[pl.ds(first + g * GROUP, GROUP)], rest_ref.at[pl.ds(g * GROUP, GROUP)], sems.at[g]
        )
        for g in range((NEAR - first) // GROUP)
    ]
    for copy in copies:
        copy.start()
    out_ref[...] = jnp.zeros_like(out_ref)
    acc_ref[...] = jnp.zeros_like(acc_ref)

    def some_far(p, _):
        for t in range(FP):
            n = p * FP + t
            add_far(out_ref, left_ref, right_ref, n, x_ref[pos_ref[0, NEAR + n]], far_row_ref[0, n])
        return 0

    lax.fori_loop(0, N_ROW, some_far, 0)

    def near_from(ref, base, start, size):
        def pair(q, _):
            for t in range(2):
                at = start + 2 * q + t
                n = base + at
                add_near(acc_ref, ref, at, x_ref[pos_ref[0, n]], near_row_ref[0, n])
            return 0

        lax.fori_loop(0, size // 2, pair, 0)

    near_from(held_a, 0, 0, HELD_A)
    near_from(held_b, HELD_A, 0, HELD_B)
    for g, copy in enumerate(copies):
        copy.wait()
        near_from(rest_ref, first, g * GROUP, GROUP)
    out_ref[...] = out_ref[...] + acc_ref[...].T


def block_sums(pos, near_index, far_index, x, held_a, held_b, left, right, near):
    rest = NEAR - HELD_A - HELD_B
    return pl.pallas_call(
        blocks_kernel,
        out_shape=jax.ShapeDtypeStruct((RC_DEV, 2 * B), f32),
        in_specs=[SMEM, SMEM, SMEM, VMEM, VMEM, VMEM, VMEM, VMEM, HBM],
        out_specs=VMEM,
        scratch_shapes=[
            pltpu.VMEM((2 * B, LANES), f32),
            pltpu.VMEM((rest, 2 * B, 2 * B), f32),
            pltpu.SemaphoreType.DMA((rest // GROUP,)),
        ],
        compiler_params=pltpu.CompilerParams(vmem_limit_bytes=24 * 1024 * 1024),
        name="blocks",
    )(pos, near_index, far_index, x, held_a, held_b, left, right, in_hbm(near))


def round_kernel(
    pos_ref, near_row_ref, far_row_ref, x_ref, near_ref, left_ref, right_ref, out_ref, acc_ref
):
    p = pl.program_id(0)

    @pl.when(p == 0)
    def _():
        out_ref[...] = jnp.zeros_like(out_ref)
        acc_ref[...] = jnp.zeros_like(acc_ref)

    for t in range(NP):
        n = p * NP + t
        add_near(acc_ref, near_ref, t, x_ref[pos_ref[0, n]], near_row_ref[0, n])
    for t in range(FP):
        n = p * FP + t
        add_far(out_ref, left_ref, right_ref, t, x_ref[pos_ref[0, NEAR + n]], far_row_ref[0, n])

    @pl.when(p == N_ROW - 1)
    def _():
        out_ref[...] = out_ref[...] + acc_ref[...].T


def round_sums(pos, near_index, far_index, x, near, left, right):
    return pl.pallas_call(
        round_kernel,
        grid=(N_ROW,),
        out_shape=jax.ShapeDtypeStruct((RC_DEV, 2 * B), f32),
        in_specs=[SMEM, SMEM, SMEM, pl.BlockSpec(x.shape, lambda p: (0, 0, 0))]
        + [
            pl.BlockSpec((one.shape[0] // N_ROW,) + one.shape[1:], lambda p: (p, 0, 0))
            for one in (near, left, right)
        ],
        out_specs=pl.BlockSpec((RC_DEV, 2 * B), lambda p: (0, 0)),
        scratch_shapes=[pltpu.VMEM((2 * B, LANES), f32)],
        compiler_params=pltpu.CompilerParams(vmem_limit_bytes=10 * 1024 * 1024),
        name="round",
    )(pos, near_index, far_index, x, in_hbm(near), in_hbm(left), in_hbm(right))


def final_kernel(
    a_ref, b_ref, s_ref, parts_ref, stress_ref, state_ref, fault_ref, out_stress, out_rate, out_state
):
    total = parts_ref[0]
    for c in range(1, N_COL):
        total = total + parts_ref[c]
    groups = RC_DEV // N_COL
    for h in range(2):
        every = pl.ds(h, groups, stride=2)
        state = state_ref[every, :]
        fault = fault_ref[every, :]
        a = jnp.zeros_like(state)
        b = jnp.zeros_like(state)
        sigma = jnp.zeros_like(state)
        for f in range(FAULTS):
            here = fault == f
            a = jnp.where(here, a_ref[f], a)
            b = jnp.where(here, b_ref[f], b)
            sigma = jnp.where(here, s_ref[f], sigma)
        square = jnp.ones_like(state)
        for k in range(2):
            old = jnp.concatenate(
                [
                    stress_ref[k : k + 1, g * B + h * LANES : g * B + (h + 1) * LANES]
                    for g in range(groups)
                ],
                axis=0,
            )
            new = old + STEP_SIZE * total[:, k * B + h * LANES : k * B + (h + 1) * LANES]
            for g in range(groups):
                out_stress[k : k + 1, g * B + h * LANES : g * B + (h + 1) * LANES] = new[g : g + 1, :]
            square = square + new * new
        z = jnp.sqrt(square) / (a * sigma)
        u = state / a
        rate = jnp.exp(z - u) - jnp.exp(-z - u)
        out_rate[every, :] = rate
        out_state[every, :] = state + STEP_SIZE * b * (jnp.exp(-state / b) - rate)


def finish(a, b, s, parts, stress, state, fault):
    rows = stress.shape[1] // LANES
    new_stress, new_rate, new_state = pl.pallas_call(
        final_kernel,
        out_shape=(
            jax.ShapeDtypeStruct(stress.shape, f32),
            jax.ShapeDtypeStruct((rows, LANES), f32),
            jax.ShapeDtypeStruct((rows, LANES), f32),
        ),
        in_specs=[SMEM, SMEM, SMEM, VMEM, VMEM, VMEM, VMEM],
        out_specs=(VMEM, VMEM, VMEM),
        compiler_params=SMALL,
        name="finish",
    )(
        a,
        b,
        s,
        parts.reshape(N_COL, RC_DEV // N_COL, 2 * B),
        stress,
        state.reshape(rows, LANES),
        fault.reshape(rows, LANES),
    )
    return (new_stress, new_rate.reshape(-1), new_state.reshape(-1))


def body(
    slip_rate,
    source_cluster,
    near_kernel,
    near_pattern,
    far_left,
    far_right,
    far_pattern,
    stress,
    state,
    fault_of_row,
    direct_effect,
    evolution_effect,
    normal_stress,
):
    near, left, right = near_kernel[0, 0], far_left[0, 0], far_right[0, 0]
    near_index, far_index = near_pattern[0, 0], far_pattern[0, 0]
    slip = jnp.transpose(slip_rate.reshape(2, CLU_DEV, B), (1, 0, 2))
    payload, left_held = make_payload(source_cluster, near_index, far_index, ((left, 0, FAR),))
    gathered = lax.all_to_all(payload, "row", 0, 0, tiled=True)

    def exchange(req, snd, source, staged):
        asked = lax.all_to_all(req, "col", 0, 0, tiled=True)
        reply, rounds, done, *held = gather_rows(asked, source, staged[0])
        got = lax.all_to_all(reply, "col", 0, 0, tiled=True)
        ready, *more_held = forward_rows(snd, got, staged[1])
        return lax.all_to_all(ready, "row", 0, 0, tiled=True), rounds, done, *held, *more_held

    req, snd, pos, slip_held, right_held = make_index(
        gathered, (), ((slip, 0, CLU_DEV), (right, 0, FAR))
    )
    x, rounds, done, held_a, held_b = exchange(
        req, snd, slip_held, (((near, 0, HELD_A),), ((near, HELD_A, HELD_B),))
    )
    fast = block_sums(pos, near_index, far_index, x, held_a, held_b, left_held, right_held, near)

    limit = rounds.reshape(())

    def more(carry):
        return carry[0] < limit

    def one_round(carry):
        k, total = carry
        req, snd, pos, slip_now = make_index(gathered, (k.reshape(1),), ((slip, 0, CLU_DEV),))
        x, _, _ = exchange(req, snd, slip_now, ((), ()))
        n = jnp.arange(LANES, dtype=i32)
        rows = jnp.where(active_in(n, k)[:, None, None], x[pos[0]], 0.0)
        part = round_sums(n[None, :], near_index, far_index, rows, near, left, right)
        return k + 1, jnp.where(k == 0, 0.0, total) + part

    _, summed = lax.while_loop(more, one_round, (done.reshape(()), fast))
    parts = lax.all_to_all(summed, "col", 0, 0, tiled=True)
    return finish(
        direct_effect, evolution_effect, normal_stress, parts, stress, state, fault_of_row
    )


def solution(mesh):
    return jax.shard_map(
        body,
        mesh=mesh,
        in_specs=(
            P(None, ("row", "col")),
            P(("row", "col")),
            P("row", "col", None, None, None),
            P("row", "col", None, None),
            P("row", "col", None, None, None),
            P("row", "col", None, None, None),
            P("row", "col", None, None),
            P(None, ("row", "col")),
            P(("row", "col")),
            P(("row", "col")),
            P(),
            P(),
            P(),
        ),
        out_specs=(P(None, ("row", "col")), P(("row", "col")), P(("row", "col"))),
        check_vma=False,
    )
```

```python
import functools

import functools

import jax
import jax.numpy as jnp
from jax import lax
from jax.experimental import pallas as pl
from jax.experimental.pallas import tpu as pltpu
from jax.sharding import PartitionSpec as P

B = 256
R = 32
CLU_DEV = 512
RC_DEV = 128
NP = 2
FP = 12
N_ROW = 8
N_COL = 16
NEAR = N_ROW * NP
FAR = N_ROW * FP
BLOCKS = NEAR + FAR
LANES = 128
CAP_COL = 24
CAP_ROW = 32
GROUP = 2
HALVES = 2
ROUNDS = 56
PIECE_ROWS = 8
FAULTS = 40
STEP_SIZE = 0.25

VMEM = pl.BlockSpec(memory_space=pltpu.VMEM)
SMEM = pl.BlockSpec(memory_space=pltpu.SMEM)
HBM = pl.BlockSpec(memory_space=pltpu.HBM)
f32 = jnp.float32
bf16 = jnp.bfloat16
i32 = jnp.int32
NT = (((1,), (1,)), ((), ()))
SMALL = pltpu.CompilerParams(vmem_limit_bytes=6 * 1024 * 1024)


def in_hbm(x):
    return pltpu.with_memory_space_constraint(x, pltpu.HBM)


def call(kernel, ins, specs, outs, out_specs, name, staged=()):
    count, given, made = len(staged), len(ins), len(outs)

    def run(*refs):
        held = refs[given + count + made : given + 2 * count + made]
        copies = [
            pltpu.make_async_copy(one.at[pl.ds(first, size)], to, done)
            for one, to, done, (_, first, size) in zip(
                refs[given : given + count], held, refs[given + 2 * count + made :], staged
            )
        ]
        for copy in copies:
            copy.start()
        kernel(*refs[:given], *refs[given + count : given + count + made])
        for copy in copies:
            copy.wait()

    return pl.pallas_call(
        run,
        out_shape=tuple(outs)
        + tuple(pltpu.VMEM((size,) + one.shape[1:], one.dtype) for one, _, size in staged),
        in_specs=list(specs) + [HBM] * count,
        out_specs=tuple(out_specs) + (VMEM,) * count,
        scratch_shapes=[pltpu.SemaphoreType.DMA] * count,
        compiler_params=SMALL,
        name=name,
    )(*ins, *(in_hbm(one) for one, _, _ in staged))


def iota(shape, dim):
    return lax.broadcasted_iota(i32, shape, dim)


def exact(x):
    return x.astype(f32).astype(bf16)


def split(x):
    return jnp.concatenate([x >> 8, x & 255], axis=0)


def piece_of(n):
    return jnp.where(n < NEAR, n >> 1, ((n - NEAR) * 43) >> 9)


def active_in(n, ctl=None):
    if ctl is None:
        return n < BLOCKS
    rnd, rounds = ctl
    piece = piece_of(n)
    within = jnp.where(n < NEAR, n & 1, NP + (n - NEAR) - FP * piece)
    of = (rnd * 37) >> 8
    pair = (piece == of) & ((within >> 1) == rnd - 7 * of)
    return (n < BLOCKS) & (((rounds == HALVES) & ((piece >> 2) == rnd)) | ((rounds != HALVES) & pair))


def payload_kernel(table_ref, near_ref, far_ref, out_ref):
    out_ref[...] = jnp.zeros_like(out_ref)
    for r in range(N_ROW):
        out_ref[r, 0:4, :] = table_ref[...]
        out_ref[r, 4:5, 0:NEAR] = near_ref[1:2, :]
        out_ref[r, 5:6, 0:FAR] = far_ref[1:2, :]
        out_ref[r, 6:7, :] = jnp.full((1, LANES), r, i32)


def make_payload(source_cluster, near_index, far_index):
    return call(
        payload_kernel,
        [in_hbm(one) for one in (source_cluster.reshape(4, LANES), near_index, far_index)],
        [VMEM, VMEM, VMEM],
        (jax.ShapeDtypeStruct((N_ROW, PIECE_ROWS, LANES), i32),),
        (VMEM,),
        "payload",
    )[0]


def index_kernel(g_ref, *refs):
    req_ref, snd_ref, pos_ref = refs[-3:]
    ctl = (refs[0][0] - 1, refs[1][0]) if len(refs) > 3 else None
    rho = g_ref[0, 6:7, :]
    tables = jnp.concatenate([g_ref[:, q, :] for q in range(4)], axis=1)
    n = iota((N_ROW, LANES), 1)
    m = jnp.where(n < NEAR, g_ref[:, 4, :], pltpu.roll(g_ref[:, 5, :], NEAR, 1))
    active = active_in(n, ctl)
    tab = exact(split(tables))
    piece_mask = (iota((N_ROW, LANES), 0) == piece_of(n)).astype(f32)
    place = iota((CLU_DEV, LANES), 0)
    rows = []
    for r in range(N_ROW):
        onehot = exact(place == m[r : r + 1, :])
        found = jnp.dot(tab, onehot, preferred_element_type=f32)
        value = found[0:N_ROW] * 256.0 + found[N_ROW : 2 * N_ROW]
        rows.append(jnp.sum(value * piece_mask, axis=0, keepdims=True))
    gid = jnp.concatenate(rows, axis=0).astype(i32)
    owner = jnp.where(active, gid >> 9, -1)
    owner_row = owner >> 4
    local = gid & (CLU_DEV - 1)
    every = iota((LANES, LANES), 0)
    counts = jnp.zeros((LANES, LANES), f32)
    for r in range(N_ROW):
        counts = counts + (every == owner[r : r + 1, :]).astype(f32)
    early = (piece_of(iota((1, LANES), 1)) < N_ROW // 2).astype(f32)
    col_label = iota((N_COL, LANES), 0) + rho * N_COL
    row_label = iota((N_ROW, LANES), 0)
    to_col = jnp.concatenate([(col_label == owner[r : r + 1, :]).astype(f32) for r in range(N_ROW)], axis=0)
    to_row = jnp.concatenate([(row_label == owner_row[r : r + 1, :]).astype(f32) for r in range(N_ROW)], axis=0)
    sub, lane = iota((LANES, LANES), 0), iota((LANES, LANES), 1)
    scan = jnp.concatenate([exact(sub < lane), jnp.ones((LANES, LANES), bf16)], axis=1)
    ahead = jnp.dot(to_col.astype(bf16), scan, preferred_element_type=f32)
    earlier = exact(((sub & (N_COL - 1)) == (lane & (N_COL - 1))) & (sub > lane))
    offset = jnp.dot(earlier, ahead[:, LANES:].astype(bf16), preferred_element_type=f32)
    first = to_col * (ahead[:, :LANES] + offset)
    second = to_row * jnp.dot(to_row.astype(bf16), scan[:, :LANES], preferred_element_type=f32)
    slot1 = jnp.concatenate(
        [jnp.sum(first[r * N_COL : (r + 1) * N_COL], axis=0, keepdims=True) for r in range(N_ROW)], axis=0
    ).astype(i32)
    slot2 = jnp.concatenate(
        [jnp.sum(second[r * N_ROW : (r + 1) * N_ROW], axis=0, keepdims=True) for r in range(N_ROW)], axis=0
    ).astype(i32)
    fits = [
        (jnp.max(jnp.sum(counts * part, axis=1, keepdims=True)) <= CAP_COL)
        & (jnp.max(jnp.sum(to_row * part, axis=1, keepdims=True)) <= CAP_ROW)
        for part in (jnp.ones((1, LANES), f32), early, 1.0 - early)
    ]
    over = jnp.where(fits[0], 0, jnp.where(fits[1] & fits[2], 1, 2))
    pos = jnp.clip(owner_row * CAP_ROW + slot2, 0, N_ROW * CAP_ROW - 1)
    pos_ref[...] = jnp.sum(jnp.where(row_label == rho, pos, 0).astype(f32), axis=0, keepdims=True).astype(i32)
    mine = owner_row == rho
    pos1 = jnp.clip((owner & (N_COL - 1)) * CAP_COL + slot1, 0, N_COL * CAP_COL - 1)
    req = jnp.zeros((2 * N_COL, LANES), f32)
    snd = jnp.zeros((2 * N_ROW, LANES), f32)
    for r in range(N_ROW):
        sel = to_col[r * N_COL : (r + 1) * N_COL] > 0.5
        value = split(jnp.where(sel, local[r : r + 1, :], 0))
        put = exact(sub == jnp.where(slot1[r : r + 1, :] < CAP_COL, slot1[r : r + 1, :], -1))
        req = req + lax.dot_general(exact(value), put, NT, preferred_element_type=f32)
        value = split(jnp.where((row_label == r) & mine[r : r + 1, :], pos1[r : r + 1, :], 0))
        put = exact(sub == jnp.where(slot2[r : r + 1, :] < CAP_ROW, slot2[r : r + 1, :], -1))
        snd = snd + lax.dot_general(exact(value), put, NT, preferred_element_type=f32)
    req = (req[0:N_COL] * 256.0 + req[N_COL : 2 * N_COL]).astype(i32)
    req_ref[...] = jnp.where(iota((N_COL, LANES), 1) == LANES - 1, over, req)
    snd_ref[...] = (snd[0:N_ROW] * 256.0 + snd[N_ROW : 2 * N_ROW]).astype(i32)


def make_index(gathered, slip, ctl=()):
    square = jax.ShapeDtypeStruct((N_ROW, LANES), i32)
    return call(
        index_kernel,
        (gathered, *ctl),
        [VMEM] + [SMEM] * len(ctl),
        (jax.ShapeDtypeStruct((N_COL, LANES), i32), square, jax.ShapeDtypeStruct((1, LANES), i32)),
        (VMEM, VMEM, VMEM),
        "index",
        ((slip, 0, CLU_DEV),),
    )


def gather_kernel(idx_ref, slip_ref, out_ref, rounds_ref, to_do_ref):
    def one_col(c, over):
        for k in range(CAP_COL):
            out_ref[c * CAP_COL + k] = slip_ref[idx_ref[c, k]]
        return jnp.maximum(over, idx_ref[c, LANES - 1])

    over = lax.fori_loop(0, N_COL, one_col, jnp.int32(0))
    rounds = jnp.where(over == 0, 0, jnp.where(over == 1, HALVES, ROUNDS))
    rounds_ref[0] = rounds
    to_do_ref[0] = rounds


def gather_rows(idx, slip):
    one = jax.ShapeDtypeStruct((1,), i32)
    return call(
        gather_kernel,
        (idx, slip),
        [SMEM, VMEM],
        (jax.ShapeDtypeStruct((N_COL * CAP_COL, 2, B), f32), one, one),
        (VMEM, SMEM, SMEM),
        "gather",
    )


def forward_kernel(idx_ref, got_ref, out_ref):
    def one_row(r, _):
        for k in range(CAP_ROW):
            out_ref[r * CAP_ROW + k] = got_ref[idx_ref[r, k]]
        return 0

    lax.fori_loop(0, N_ROW, one_row, 0)


def forward_rows(idx, got):
    return call(
        forward_kernel,
        (idx, got),
        [SMEM, VMEM],
        (jax.ShapeDtypeStruct((N_ROW * CAP_ROW, 2, B), f32),),
        (VMEM,),
        "forward",
    )[0]


CHUNK = 64


def add_near(acc_ref, near_ref, at, x, row):
    x0, x1 = x[0:1, :], x[1:2, :]
    here = iota((CHUNK, LANES), 1) == row
    for s in range(0, 2 * B, CHUNK):
        rows = pl.ds(s, CHUNK)
        prod = near_ref[at, rows, 0:B] * x0 + near_ref[at, rows, B : 2 * B] * x1
        total = jnp.sum(prod[:, 0:LANES] + prod[:, LANES:B], axis=1, keepdims=True)
        old = acc_ref[rows, :]
        acc_ref[rows, :] = jnp.where(here, old + total, old)


def add_far(out_ref, left_ref, right_ref, at, x, row):
    x = x.astype(bf16).astype(f32)
    right = right_ref[at].astype(f32)
    prod = right[:, 0:B] * x[0:1, :] + right[:, B : 2 * B] * x[1:2, :]
    coef = jnp.sum(prod[:, 0:LANES] + prod[:, LANES:B], axis=1, keepdims=True)
    coef = coef.astype(bf16).astype(f32)
    far = jnp.sum(left_ref[at].astype(f32) * coef, axis=0, keepdims=True)
    rows = pl.ds(row, 1)
    out_ref[rows, :] = out_ref[rows, :] + far


def blocks_kernel(
    pos_ref, near_row_ref, far_row_ref, x_ref, left_ref, right_hbm, near_hbm,
    out_ref, acc_ref, right_ref, near_ref, right_sems, near_sems,
):
    half = FAR // 2
    right_copies = [
        pltpu.make_async_copy(
            right_hbm.at[pl.ds(g * half, half)], right_ref.at[pl.ds(g * half, half)], right_sems.at[g]
        )
        for g in range(2)
    ]
    near_copies = [
        pltpu.make_async_copy(
            near_hbm.at[pl.ds(g * GROUP, GROUP)], near_ref.at[pl.ds(g * GROUP, GROUP)], near_sems.at[g]
        )
        for g in range(NEAR // GROUP)
    ]
    for copy in right_copies + near_copies:
        copy.start()
    out_ref[...] = jnp.zeros_like(out_ref)
    acc_ref[...] = jnp.zeros_like(acc_ref)

    def some_far(p, _):
        for t in range(FP):
            n = p * FP + t
            add_far(out_ref, left_ref, right_ref, n, x_ref[pos_ref[0, NEAR + n]], far_row_ref[0, n])
        return 0

    for g, copy in enumerate(right_copies):
        copy.wait()
        lax.fori_loop(g * N_ROW // 2, (g + 1) * N_ROW // 2, some_far, 0)
    for g, copy in enumerate(near_copies):
        copy.wait()
        for n in range(g * GROUP, (g + 1) * GROUP):
            add_near(acc_ref, near_ref, n, x_ref[pos_ref[0, n]], near_row_ref[0, n])
    out_ref[...] = out_ref[...] + acc_ref[...].T


def block_sums(pos, near_index, far_index, x, left, right, near):
    return pl.pallas_call(
        blocks_kernel,
        out_shape=jax.ShapeDtypeStruct((RC_DEV, 2 * B), f32),
        in_specs=[SMEM, SMEM, SMEM, VMEM, VMEM, HBM, HBM],
        out_specs=VMEM,
        scratch_shapes=[
            pltpu.VMEM((2 * B, LANES), f32),
            pltpu.VMEM(right.shape, bf16),
            pltpu.VMEM(near.shape, f32),
            pltpu.SemaphoreType.DMA((2,)),
            pltpu.SemaphoreType.DMA((NEAR // GROUP,)),
        ],
        compiler_params=pltpu.CompilerParams(vmem_limit_bytes=28 * 1024 * 1024),
        name="blocks",
    )(pos, near_index, far_index, x, left, in_hbm(right), in_hbm(near))


def pick_kernel(to_do_ref, rounds_ref, pos_ref, x_ref, out_ref):
    def one(n, _):
        taken = active_in(n, (to_do_ref[0] - 1, rounds_ref[0]))
        x = x_ref[pos_ref[0, n]]
        out_ref[n] = jnp.where(taken, x, jnp.zeros_like(x))
        return 0

    lax.fori_loop(0, LANES, one, 0)


def pick_rows(to_do, rounds, pos, x):
    return call(
        pick_kernel,
        (to_do, rounds, pos, x),
        [SMEM, SMEM, SMEM, VMEM],
        (jax.ShapeDtypeStruct((LANES, 2, B), f32),),
        (VMEM,),
        "pick",
    )[0]


def round_kernel(
    pos_ref, near_row_ref, far_row_ref, x_ref, near_ref, left_ref, right_ref, out_ref, acc_ref
):
    p = pl.program_id(0)

    @pl.when(p == 0)
    def _():
        out_ref[...] = jnp.zeros_like(out_ref)
        acc_ref[...] = jnp.zeros_like(acc_ref)

    for t in range(NP):
        n = p * NP + t
        add_near(acc_ref, near_ref, t, x_ref[pos_ref[0, n]], near_row_ref[0, n])
    for t in range(FP):
        n = p * FP + t
        add_far(out_ref, left_ref, right_ref, t, x_ref[pos_ref[0, NEAR + n]], far_row_ref[0, n])

    @pl.when(p == N_ROW - 1)
    def _():
        out_ref[...] = out_ref[...] + acc_ref[...].T


def round_sums(pos, near_index, far_index, x, near, left, right):
    return pl.pallas_call(
        round_kernel,
        grid=(N_ROW,),
        out_shape=jax.ShapeDtypeStruct((RC_DEV, 2 * B), f32),
        in_specs=[SMEM, SMEM, SMEM, pl.BlockSpec(x.shape, lambda p: (0, 0, 0))]
        + [
            pl.BlockSpec((one.shape[0] // N_ROW,) + one.shape[1:], lambda p: (p, 0, 0))
            for one in (near, left, right)
        ],
        out_specs=pl.BlockSpec((RC_DEV, 2 * B), lambda p: (0, 0)),
        scratch_shapes=[pltpu.VMEM((2 * B, LANES), f32)],
        compiler_params=pltpu.CompilerParams(vmem_limit_bytes=10 * 1024 * 1024),
        name="round",
    )(pos, near_index, far_index, x, in_hbm(near), in_hbm(left), in_hbm(right))


def final_kernel(
    a_ref, b_ref, s_ref, parts_ref, stress_ref, state_ref, fault_ref, out_stress, out_rate, out_state
):
    total = parts_ref[0]
    for c in range(1, N_COL):
        total = total + parts_ref[c]
    groups = RC_DEV // N_COL
    for h in range(2):
        every = pl.ds(h, groups, stride=2)
        state = state_ref[every, :]
        fault = fault_ref[every, :]
        a = jnp.zeros_like(state)
        b = jnp.zeros_like(state)
        sigma = jnp.zeros_like(state)
        for f in range(FAULTS):
            here = fault == f
            a = jnp.where(here, a_ref[f], a)
            b = jnp.where(here, b_ref[f], b)
            sigma = jnp.where(here, s_ref[f], sigma)
        square = jnp.ones_like(state)
        for k in range(2):
            old = jnp.concatenate(
                [
                    stress_ref[k : k + 1, g * B + h * LANES : g * B + (h + 1) * LANES]
                    for g in range(groups)
                ],
                axis=0,
            )
            new = old + STEP_SIZE * total[:, k * B + h * LANES : k * B + (h + 1) * LANES]
            for g in range(groups):
                out_stress[k : k + 1, g * B + h * LANES : g * B + (h + 1) * LANES] = new[g : g + 1, :]
            square = square + new * new
        z = jnp.sqrt(square) / (a * sigma)
        u = state / a
        rate = jnp.exp(z - u) - jnp.exp(-z - u)
        out_rate[every, :] = rate
        out_state[every, :] = state + STEP_SIZE * b * (jnp.exp(-state / b) - rate)


def finish(a, b, s, parts, stress, state, fault):
    rows = stress.shape[1] // LANES
    new_stress, new_rate, new_state = pl.pallas_call(
        final_kernel,
        out_shape=(
            jax.ShapeDtypeStruct(stress.shape, f32),
            jax.ShapeDtypeStruct((rows, LANES), f32),
            jax.ShapeDtypeStruct((rows, LANES), f32),
        ),
        in_specs=[SMEM, SMEM, SMEM, VMEM, VMEM, VMEM, VMEM],
        out_specs=(VMEM, VMEM, VMEM),
        compiler_params=SMALL,
        name="finish",
    )(
        a,
        b,
        s,
        parts.reshape(N_COL, RC_DEV // N_COL, 2 * B),
        stress,
        state.reshape(rows, LANES),
        fault.reshape(rows, LANES),
    )
    return (new_stress, new_rate.reshape(-1), new_state.reshape(-1))


def body(
    slip_rate,
    source_cluster,
    near_kernel,
    near_pattern,
    far_left,
    far_right,
    far_pattern,
    stress,
    state,
    fault_of_row,
    direct_effect,
    evolution_effect,
    normal_stress,
):
    near, left, right = near_kernel[0, 0], far_left[0, 0], far_right[0, 0]
    near_index, far_index = near_pattern[0, 0], far_pattern[0, 0]
    slip = jnp.transpose(slip_rate.reshape(2, CLU_DEV, B), (1, 0, 2))
    gathered = lax.all_to_all(
        make_payload(source_cluster, near_index, far_index), "row", 0, 0, tiled=True
    )

    def fetch(*ctl):
        req, snd, pos, slip_held = make_index(gathered, slip, ctl)
        asked = lax.all_to_all(req, "col", 0, 0, tiled=True)
        reply, rounds, to_do = gather_rows(asked, slip_held)
        got = lax.all_to_all(reply, "col", 0, 0, tiled=True)
        return lax.all_to_all(forward_rows(snd, got), "row", 0, 0, tiled=True), pos, rounds, to_do

    x, pos, rounds, to_do = fetch()
    fast = block_sums(pos, near_index, far_index, x, left, right, near)

    def one_round(carry):
        to_do, total = carry
        now = to_do.reshape(1)
        x, pos, _, _ = fetch(now, rounds)
        rows = pick_rows(now, rounds, pos, x)
        n = jnp.arange(LANES, dtype=i32)[None, :]
        part = round_sums(n, near_index, far_index, rows, near, left, right)
        return to_do - 1, jnp.where(to_do == rounds[0], 0.0, total) + part

    _, summed = lax.while_loop(lambda carry: carry[0] > 0, one_round, (to_do.reshape(()), fast))
    parts = lax.all_to_all(summed, "col", 0, 0, tiled=True)
    return finish(
        direct_effect, evolution_effect, normal_stress, parts, stress, state, fault_of_row
    )


def solution(mesh):
    return jax.shard_map(
        body,
        mesh=mesh,
        in_specs=(
            P(None, ("row", "col")),
            P(("row", "col")),
            P("row", "col", None, None, None),
            P("row", "col", None, None),
            P("row", "col", None, None, None),
            P("row", "col", None, None, None),
            P("row", "col", None, None),
            P(None, ("row", "col")),
            P(("row", "col")),
            P(("row", "col")),
            P(),
            P(),
            P(),
        ),
        out_specs=(P(None, ("row", "col")), P(("row", "col")), P(("row", "col"))),
        check_vma=False,
    )
```

```python
import functools

import functools

import jax
import jax.numpy as jnp
from jax import lax
from jax.experimental import pallas as pl
from jax.experimental.pallas import tpu as pltpu
from jax.sharding import PartitionSpec as P

B = 256
R = 32
CLU_DEV = 512
RC_DEV = 128
NP = 2
FP = 12
N_ROW = 8
N_COL = 16
NEAR = N_ROW * NP
FAR = N_ROW * FP
BLOCKS = NEAR + FAR
LANES = 128
CAP_COL = 24
CAP_ROW = 32
GROUP = 2
RIGHTS = 4
AHEAD = 8
HALVES = 2
ROUNDS = 56
PIECE_ROWS = 8
FAULTS = 40
STEP_SIZE = 0.25

VMEM = pl.BlockSpec(memory_space=pltpu.VMEM)
SMEM = pl.BlockSpec(memory_space=pltpu.SMEM)
HBM = pl.BlockSpec(memory_space=pltpu.HBM)
ANY = pl.BlockSpec(memory_space=pl.ANY)
f32 = jnp.float32
bf16 = jnp.bfloat16
i32 = jnp.int32
NT = (((1,), (1,)), ((), ()))
SMALL = pltpu.CompilerParams(vmem_limit_bytes=6 * 1024 * 1024)


def in_hbm(x):
    return pltpu.with_memory_space_constraint(x, pltpu.HBM)


def call(kernel, ins, specs, outs, out_specs, name, staged=()):
    count, given, made = len(staged), len(ins), len(outs)

    def run(*refs):
        held = refs[given + count + made : given + 2 * count + made]
        copies = [
            pltpu.make_async_copy(one.at[pl.ds(first, size)], to, done)
            for one, to, done, (_, first, size) in zip(
                refs[given : given + count], held, refs[given + 2 * count + made :], staged
            )
        ]
        for copy in copies:
            copy.start()
        kernel(*refs[:given], *refs[given + count : given + count + made])
        for copy in copies:
            copy.wait()

    return pl.pallas_call(
        run,
        out_shape=tuple(outs)
        + tuple(pltpu.VMEM((size,) + one.shape[1:], one.dtype) for one, _, size in staged),
        in_specs=list(specs) + [HBM] * count,
        out_specs=tuple(out_specs) + (VMEM,) * count,
        scratch_shapes=[pltpu.SemaphoreType.DMA] * count,
        compiler_params=SMALL,
        name=name,
    )(*ins, *(in_hbm(one) for one, _, _ in staged))


def iota(shape, dim):
    return lax.broadcasted_iota(i32, shape, dim)


def exact(x):
    return x.astype(f32).astype(bf16)


def split(x):
    return jnp.concatenate([x >> 8, x & 255], axis=0)


def piece_of(n):
    return jnp.where(n < NEAR, n >> 1, ((n - NEAR) * 43) >> 9)


def active_in(n, ctl=None):
    if ctl is None:
        return n < BLOCKS
    rnd, rounds = ctl
    piece = piece_of(n)
    within = jnp.where(n < NEAR, n & 1, NP + (n - NEAR) - FP * piece)
    of = (rnd * 37) >> 8
    pair = (piece == of) & ((within >> 1) == rnd - 7 * of)
    return (n < BLOCKS) & (((rounds == HALVES) & ((piece >> 2) == rnd)) | ((rounds != HALVES) & pair))


def payload_kernel(table_ref, near_ref, far_ref, out_ref):
    out_ref[...] = jnp.zeros_like(out_ref)
    for r in range(N_ROW):
        out_ref[r, 0:4, :] = table_ref[...]
        out_ref[r, 4:5, 0:NEAR] = near_ref[1:2, :]
        out_ref[r, 5:6, 0:FAR] = far_ref[1:2, :]
        out_ref[r, 6:7, :] = jnp.full((1, LANES), r, i32)


def make_payload(source_cluster, near_index, far_index):
    return call(
        payload_kernel,
        [in_hbm(one) for one in (source_cluster.reshape(4, LANES), near_index, far_index)],
        [VMEM, VMEM, VMEM],
        (jax.ShapeDtypeStruct((N_ROW, PIECE_ROWS, LANES), i32),),
        (VMEM,),
        "payload",
    )[0]


def index_kernel(g_ref, *refs):
    req_ref, snd_ref, pos_ref = refs[-3:]
    ctl = (refs[0][0] - 1, refs[1][0]) if len(refs) > 3 else None
    rho = g_ref[0, 6:7, :]
    tables = jnp.concatenate([g_ref[:, q, :] for q in range(4)], axis=1)
    n = iota((N_ROW, LANES), 1)
    m = jnp.where(n < NEAR, g_ref[:, 4, :], pltpu.roll(g_ref[:, 5, :], NEAR, 1))
    active = active_in(n, ctl)
    tab = exact(split(tables))
    piece_mask = (iota((N_ROW, LANES), 0) == piece_of(n)).astype(f32)
    place = iota((CLU_DEV, LANES), 0)
    rows = []
    for r in range(N_ROW):
        onehot = exact(place == m[r : r + 1, :])
        found = jnp.dot(tab, onehot, preferred_element_type=f32)
        value = found[0:N_ROW] * 256.0 + found[N_ROW : 2 * N_ROW]
        rows.append(jnp.sum(value * piece_mask, axis=0, keepdims=True))
    gid = jnp.concatenate(rows, axis=0).astype(i32)
    owner = jnp.where(active, gid >> 9, -1)
    owner_row = owner >> 4
    local = gid & (CLU_DEV - 1)
    every = iota((LANES, LANES), 0)
    counts = jnp.zeros((LANES, LANES), f32)
    for r in range(N_ROW):
        counts = counts + (every == owner[r : r + 1, :]).astype(f32)
    early = (piece_of(iota((1, LANES), 1)) < N_ROW // 2).astype(f32)
    col_label = iota((N_COL, LANES), 0) + rho * N_COL
    row_label = iota((N_ROW, LANES), 0)
    to_col = jnp.concatenate([(col_label == owner[r : r + 1, :]).astype(f32) for r in range(N_ROW)], axis=0)
    to_row = jnp.concatenate([(row_label == owner_row[r : r + 1, :]).astype(f32) for r in range(N_ROW)], axis=0)
    sub, lane = iota((LANES, LANES), 0), iota((LANES, LANES), 1)
    scan = jnp.concatenate([exact(sub < lane), jnp.ones((LANES, LANES), bf16)], axis=1)
    ahead = jnp.dot(to_col.astype(bf16), scan, preferred_element_type=f32)
    earlier = exact(((sub & (N_COL - 1)) == (lane & (N_COL - 1))) & (sub > lane))
    offset = jnp.dot(earlier, ahead[:, LANES:].astype(bf16), preferred_element_type=f32)
    first = to_col * (ahead[:, :LANES] + offset)
    second = to_row * jnp.dot(to_row.astype(bf16), scan[:, :LANES], preferred_element_type=f32)
    slot1 = jnp.concatenate(
        [jnp.sum(first[r * N_COL : (r + 1) * N_COL], axis=0, keepdims=True) for r in range(N_ROW)], axis=0
    ).astype(i32)
    slot2 = jnp.concatenate(
        [jnp.sum(second[r * N_ROW : (r + 1) * N_ROW], axis=0, keepdims=True) for r in range(N_ROW)], axis=0
    ).astype(i32)
    fits = [
        (jnp.max(jnp.sum(counts * part, axis=1, keepdims=True)) <= CAP_COL)
        & (jnp.max(jnp.sum(to_row * part, axis=1, keepdims=True)) <= CAP_ROW)
        for part in (jnp.ones((1, LANES), f32), early, 1.0 - early)
    ]
    over = jnp.where(fits[0], 0, jnp.where(fits[1] & fits[2], 1, 2))
    pos = jnp.clip(owner_row * CAP_ROW + slot2, 0, N_ROW * CAP_ROW - 1)
    pos_ref[...] = jnp.sum(jnp.where(row_label == rho, pos, 0).astype(f32), axis=0, keepdims=True).astype(i32)
    mine = owner_row == rho
    pos1 = jnp.clip((owner & (N_COL - 1)) * CAP_COL + slot1, 0, N_COL * CAP_COL - 1)
    req = jnp.zeros((2 * N_COL, LANES), f32)
    snd = jnp.zeros((2 * N_ROW, LANES), f32)
    for r in range(N_ROW):
        sel = to_col[r * N_COL : (r + 1) * N_COL] > 0.5
        value = split(jnp.where(sel, local[r : r + 1, :], 0))
        put = exact(sub == jnp.where(slot1[r : r + 1, :] < CAP_COL, slot1[r : r + 1, :], -1))
        req = req + lax.dot_general(exact(value), put, NT, preferred_element_type=f32)
        value = split(jnp.where((row_label == r) & mine[r : r + 1, :], pos1[r : r + 1, :], 0))
        put = exact(sub == jnp.where(slot2[r : r + 1, :] < CAP_ROW, slot2[r : r + 1, :], -1))
        snd = snd + lax.dot_general(exact(value), put, NT, preferred_element_type=f32)
    req = (req[0:N_COL] * 256.0 + req[N_COL : 2 * N_COL]).astype(i32)
    req_ref[...] = jnp.where(iota((N_COL, LANES), 1) == LANES - 1, over, req)
    snd_ref[...] = (snd[0:N_ROW] * 256.0 + snd[N_ROW : 2 * N_ROW]).astype(i32)


def make_index(gathered, slip, ctl=()):
    square = jax.ShapeDtypeStruct((N_ROW, LANES), i32)
    return call(
        index_kernel,
        (gathered, *ctl),
        [VMEM] + [SMEM] * len(ctl),
        (jax.ShapeDtypeStruct((N_COL, LANES), i32), square, jax.ShapeDtypeStruct((1, LANES), i32)),
        (VMEM, VMEM, VMEM),
        "index",
        ((slip, 0, CLU_DEV),),
    )


def gather_kernel(idx_ref, slip_ref, out_ref):
    def one_col(c, _):
        for k in range(CAP_COL):
            out_ref[c * CAP_COL + k] = slip_ref[idx_ref[c, k]]
        return 0

    lax.fori_loop(0, N_COL, one_col, 0)


def gather_rows(idx, slip):
    return call(
        gather_kernel,
        (idx, slip),
        [SMEM, VMEM],
        (jax.ShapeDtypeStruct((N_COL * CAP_COL, 2, B), f32),),
        (VMEM,),
        "gather",
    )[0]


def forward_kernel(idx_ref, got_ref, out_ref):
    def one_row(r, _):
        for k in range(CAP_ROW):
            out_ref[r * CAP_ROW + k] = got_ref[idx_ref[r, k]]
        return 0

    lax.fori_loop(0, N_ROW, one_row, 0)


def forward_rows(idx, got):
    return call(
        forward_kernel,
        (idx, got),
        [SMEM, VMEM],
        (jax.ShapeDtypeStruct((N_ROW * CAP_ROW, 2, B), f32),),
        (VMEM,),
        "forward",
    )[0]


CHUNK = 64


def add_near(acc_ref, near_ref, at, x, row):
    x0, x1 = x[0:1, :], x[1:2, :]
    here = iota((CHUNK, LANES), 1) == row
    for s in range(0, 2 * B, CHUNK):
        rows = pl.ds(s, CHUNK)
        prod = near_ref[at, rows, 0:B] * x0 + near_ref[at, rows, B : 2 * B] * x1
        total = jnp.sum(prod[:, 0:LANES] + prod[:, LANES:B], axis=1, keepdims=True)
        old = acc_ref[rows, :]
        acc_ref[rows, :] = jnp.where(here, old + total, old)


def add_far(out_ref, left_ref, right_ref, at, x, row):
    x = x.astype(bf16).astype(f32)
    right = right_ref[at].astype(f32)
    prod = right[:, 0:B] * x[0:1, :] + right[:, B : 2 * B] * x[1:2, :]
    coef = jnp.sum(prod[:, 0:LANES] + prod[:, LANES:B], axis=1, keepdims=True)
    coef = coef.astype(bf16).astype(f32)
    far = jnp.sum(left_ref[at].astype(f32) * coef, axis=0, keepdims=True)
    rows = pl.ds(row, 1)
    out_ref[rows, :] = out_ref[rows, :] + far


def blocks_kernel(
    pos_hbm, asked_hbm, near_row_hbm, far_row_hbm, a_hbm, b_hbm, s_hbm, fault_ref, x_ref, left_ref,
    right_hbm, near_hbm,
    out_ref, param_ref, rounds_out, to_do_out,
    acc_ref, right_ref, near_ref, pos_ref, asked_ref, near_row_ref, far_row_ref, a_ref, b_ref, s_ref,
    rounds_ref, sems, small_sems, out_sems,
):
    copies = [
        pltpu.make_async_copy(from_ref.at[pl.ds(at, size)], to_ref.at[pl.ds(at, size)], sems.at[k])
        for k, (from_ref, to_ref, at, size) in enumerate(
            [(right_hbm, right_ref, at, FAR // RIGHTS) for at in range(0, FAR, FAR // RIGHTS)]
            + [(near_hbm, near_ref, at, GROUP) for at in range(0, NEAR, GROUP)]
        )
    ]
    small = [
        pltpu.make_async_copy(one, to, small_sems.at[k])
        for k, (one, to) in enumerate(
            [
                (pos_hbm, pos_ref),
                (far_row_hbm, far_row_ref),
                (near_row_hbm, near_row_ref),
                (asked_hbm, asked_ref),
                (a_hbm, a_ref),
                (b_hbm, b_ref),
                (s_hbm, s_ref),
            ]
        )
    ]
    for copy in small:
        copy.start()
    for copy in copies[:AHEAD]:
        copy.start()

    def arrive(k):
        copies[k].wait()
        if k + AHEAD < len(copies):
            copies[k + AHEAD].start()

    out_ref[...] = jnp.zeros_like(out_ref)
    acc_ref[...] = jnp.zeros_like(acc_ref)
    for copy in small:
        copy.wait()
    over = asked_ref[0, LANES - 1]
    for c in range(1, N_COL):
        over = jnp.maximum(over, asked_ref[c, LANES - 1])
    rounds_ref[0] = jnp.where(over == 0, 0, jnp.where(over == 1, HALVES, ROUNDS))
    told = [
        pltpu.make_async_copy(rounds_ref, to, out_sems.at[k])
        for k, to in enumerate((rounds_out, to_do_out))
    ]
    for copy in told:
        copy.start()
    fault = fault_ref[...]
    found = [jnp.zeros(fault.shape, f32) for _ in range(3)]
    for f in range(FAULTS):
        here = fault == f
        found = [jnp.where(here, one[f], old) for one, old in zip((a_ref, b_ref, s_ref), found)]
    for k in range(3):
        param_ref[k] = found[k]

    def some_far(p, _):
        for t in range(FP):
            n = p * FP + t
            add_far(out_ref, left_ref, right_ref, n, x_ref[pos_ref[0, NEAR + n]], far_row_ref[0, n])
        return 0

    for g in range(RIGHTS):
        arrive(g)
        lax.fori_loop(g * N_ROW // RIGHTS, (g + 1) * N_ROW // RIGHTS, some_far, 0)
    for g in range(NEAR // GROUP):
        arrive(RIGHTS + g)
        for n in range(g * GROUP, (g + 1) * GROUP):
            add_near(acc_ref, near_ref, n, x_ref[pos_ref[0, n]], near_row_ref[0, n])
    out_ref[...] = out_ref[...] + acc_ref[...].T
    for copy in told:
        copy.wait()


def block_sums(pos, asked, near_index, far_index, params, fault, x, left, right, near):
    one = jax.ShapeDtypeStruct((1,), i32)
    small = (pos, asked, near_index, far_index, *params)
    return pl.pallas_call(
        blocks_kernel,
        out_shape=(
            jax.ShapeDtypeStruct((RC_DEV, 2 * B), f32),
            jax.ShapeDtypeStruct((3,) + fault.shape, f32),
            one,
            one,
        ),
        in_specs=[ANY] * len(small) + [VMEM, VMEM, VMEM, HBM, HBM],
        out_specs=(VMEM, VMEM, ANY, ANY),
        scratch_shapes=[
            pltpu.VMEM((2 * B, LANES), f32),
            pltpu.VMEM(right.shape, bf16),
            pltpu.VMEM(near.shape, f32),
            *(pltpu.SMEM(x.shape, x.dtype) for x in small),
            pltpu.SMEM((1,), i32),
            pltpu.SemaphoreType.DMA((RIGHTS + NEAR // GROUP,)),
            pltpu.SemaphoreType.DMA((len(small),)),
            pltpu.SemaphoreType.DMA((2,)),
        ],
        compiler_params=pltpu.CompilerParams(vmem_limit_bytes=28 * 1024 * 1024),
        name="blocks",
    )(*small, fault, x, left, in_hbm(right), in_hbm(near))


def pick_kernel(to_do_ref, rounds_ref, pos_ref, x_ref, out_ref):
    def one(n, _):
        taken = active_in(n, (to_do_ref[0] - 1, rounds_ref[0]))
        x = x_ref[pos_ref[0, n]]
        out_ref[n] = jnp.where(taken, x, jnp.zeros_like(x))
        return 0

    lax.fori_loop(0, LANES, one, 0)


def pick_rows(to_do, rounds, pos, x):
    return call(
        pick_kernel,
        (to_do, rounds, pos, x),
        [SMEM, SMEM, SMEM, VMEM],
        (jax.ShapeDtypeStruct((LANES, 2, B), f32),),
        (VMEM,),
        "pick",
    )[0]


def round_kernel(
    pos_ref, near_row_ref, far_row_ref, x_ref, near_ref, left_ref, right_ref, out_ref, acc_ref
):
    p = pl.program_id(0)

    @pl.when(p == 0)
    def _():
        out_ref[...] = jnp.zeros_like(out_ref)
        acc_ref[...] = jnp.zeros_like(acc_ref)

    for t in range(NP):
        n = p * NP + t
        add_near(acc_ref, near_ref, t, x_ref[pos_ref[0, n]], near_row_ref[0, n])
    for t in range(FP):
        n = p * FP + t
        add_far(out_ref, left_ref, right_ref, t, x_ref[pos_ref[0, NEAR + n]], far_row_ref[0, n])

    @pl.when(p == N_ROW - 1)
    def _():
        out_ref[...] = out_ref[...] + acc_ref[...].T


def round_sums(pos, near_index, far_index, x, near, left, right):
    return pl.pallas_call(
        round_kernel,
        grid=(N_ROW,),
        out_shape=jax.ShapeDtypeStruct((RC_DEV, 2 * B), f32),
        in_specs=[SMEM, SMEM, SMEM, pl.BlockSpec(x.shape, lambda p: (0, 0, 0))]
        + [
            pl.BlockSpec((one.shape[0] // N_ROW,) + one.shape[1:], lambda p: (p, 0, 0))
            for one in (near, left, right)
        ],
        out_specs=pl.BlockSpec((RC_DEV, 2 * B), lambda p: (0, 0)),
        scratch_shapes=[pltpu.VMEM((2 * B, LANES), f32)],
        compiler_params=pltpu.CompilerParams(vmem_limit_bytes=10 * 1024 * 1024),
        name="round",
    )(pos, near_index, far_index, x, in_hbm(near), in_hbm(left), in_hbm(right))


def final_kernel(param_ref, parts_ref, stress_ref, state_ref, out_stress, out_rate, out_state):
    total = parts_ref[0]
    for c in range(1, N_COL):
        total = total + parts_ref[c]
    groups = RC_DEV // N_COL
    for h in range(2):
        every = pl.ds(h, groups, stride=2)
        state = state_ref[every, :]
        a, b, sigma = (param_ref[k, every, :] for k in range(3))
        square = jnp.ones_like(state)
        for k in range(2):
            old = jnp.concatenate(
                [
                    stress_ref[k : k + 1, g * B + h * LANES : g * B + (h + 1) * LANES]
                    for g in range(groups)
                ],
                axis=0,
            )
            new = old + STEP_SIZE * total[:, k * B + h * LANES : k * B + (h + 1) * LANES]
            for g in range(groups):
                out_stress[k : k + 1, g * B + h * LANES : g * B + (h + 1) * LANES] = new[g : g + 1, :]
            square = square + new * new
        z = jnp.sqrt(square) / (a * sigma)
        u = state / a
        rate = jnp.exp(z - u) - jnp.exp(-z - u)
        out_rate[every, :] = rate
        out_state[every, :] = state + STEP_SIZE * b * (jnp.exp(-state / b) - rate)


def finish(params, parts, stress, state):
    rows = stress.shape[1] // LANES
    new_stress, new_rate, new_state = call(
        final_kernel,
        (params, parts.reshape(N_COL, RC_DEV // N_COL, 2 * B), stress, state.reshape(rows, LANES)),
        [VMEM] * 4,
        (
            jax.ShapeDtypeStruct(stress.shape, f32),
            jax.ShapeDtypeStruct((rows, LANES), f32),
            jax.ShapeDtypeStruct((rows, LANES), f32),
        ),
        (VMEM,) * 3,
        "finish",
    )
    return (new_stress, new_rate.reshape(-1), new_state.reshape(-1))


def body(
    slip_rate,
    source_cluster,
    near_kernel,
    near_pattern,
    far_left,
    far_right,
    far_pattern,
    stress,
    state,
    fault_of_row,
    direct_effect,
    evolution_effect,
    normal_stress,
):
    near, left, right = near_kernel[0, 0], far_left[0, 0], far_right[0, 0]
    near_index, far_index = near_pattern[0, 0], far_pattern[0, 0]
    slip = jnp.transpose(slip_rate.reshape(2, CLU_DEV, B), (1, 0, 2))
    gathered = lax.all_to_all(
        make_payload(source_cluster, near_index, far_index), "row", 0, 0, tiled=True
    )

    def fetch(*ctl):
        req, snd, pos, slip_held = make_index(gathered, slip, ctl)
        asked = lax.all_to_all(req, "col", 0, 0, tiled=True)
        got = lax.all_to_all(gather_rows(asked, slip_held), "col", 0, 0, tiled=True)
        return lax.all_to_all(forward_rows(snd, got), "row", 0, 0, tiled=True), pos, asked

    x, pos, asked = fetch()
    faults = (direct_effect, evolution_effect, normal_stress)
    fault = fault_of_row.reshape(-1, LANES)
    fast, params, rounds, to_do = block_sums(
        pos, asked, near_index, far_index, faults, fault, x, left, right, near
    )

    def one_round(carry):
        to_do, total = carry
        now = to_do.reshape(1)
        x, pos, _ = fetch(now, rounds)
        rows = pick_rows(now, rounds, pos, x)
        n = jnp.arange(LANES, dtype=i32)[None, :]
        part = round_sums(n, near_index, far_index, rows, near, left, right)
        return to_do - 1, jnp.where(to_do == rounds[0], 0.0, total) + part

    _, summed = lax.while_loop(lambda carry: carry[0] > 0, one_round, (to_do.reshape(()), fast))
    parts = lax.all_to_all(summed, "col", 0, 0, tiled=True)
    return finish(params, parts, stress, state)


def solution(mesh):
    return jax.shard_map(
        body,
        mesh=mesh,
        in_specs=(
            P(None, ("row", "col")),
            P(("row", "col")),
            P("row", "col", None, None, None),
            P("row", "col", None, None),
            P("row", "col", None, None, None),
            P("row", "col", None, None, None),
            P("row", "col", None, None),
            P(None, ("row", "col")),
            P(("row", "col")),
            P(("row", "col")),
            P(),
            P(),
            P(),
        ),
        out_specs=(P(None, ("row", "col")), P(("row", "col")), P(("row", "col"))),
        check_vma=False,
    )
```

```python
import functools

import functools

import jax
import jax.numpy as jnp
from jax import lax
from jax.experimental import pallas as pl
from jax.experimental.pallas import tpu as pltpu
from jax.sharding import PartitionSpec as P

B = 256
R = 32
CLU_DEV = 512
RC_DEV = 128
NP = 2
FP = 12
N_ROW = 8
N_COL = 16
NEAR = N_ROW * NP
FAR = N_ROW * FP
BLOCKS = NEAR + FAR
LANES = 128
CAP_COL = 24
CAP_ROW = 32
HALVES = 2
SPAN = 15 * 10**9
ROUNDS = 56
PIECE_ROWS = 8
FAULTS = 40
STEP_SIZE = 0.25

VMEM = pl.BlockSpec(memory_space=pltpu.VMEM)
SMEM = pl.BlockSpec(memory_space=pltpu.SMEM)
HBM = pl.BlockSpec(memory_space=pltpu.HBM)
ANY = pl.BlockSpec(memory_space=pl.ANY)
f32 = jnp.float32
bf16 = jnp.bfloat16
i32 = jnp.int32
NT = (((1,), (1,)), ((), ()))
SMALL = pltpu.CompilerParams(vmem_limit_bytes=6 * 1024 * 1024)


def in_hbm(x):
    return pltpu.with_memory_space_constraint(x, pltpu.HBM)


def call(kernel, ins, specs, outs, out_specs, name, staged=(), span=0):
    count, given, made = len(staged), len(ins), len(outs)

    def run(*refs):
        held = refs[given + count + made : given + 2 * count + made]
        copies = [
            pltpu.make_async_copy(one.at[pl.ds(first, size)], to, done)
            for one, to, done, (_, first, size) in zip(
                refs[given : given + count], held, refs[given + 2 * count + made :], staged
            )
        ]
        for copy in copies:
            copy.start()
        kernel(*refs[:given], *refs[given + count : given + count + made])
        for copy in copies:
            copy.wait()

    return pl.pallas_call(
        run,
        out_shape=tuple(outs)
        + tuple(pltpu.VMEM((size,) + one.shape[1:], one.dtype) for one, _, size in staged),
        in_specs=list(specs) + [HBM] * count,
        out_specs=tuple(out_specs) + (VMEM,) * count,
        scratch_shapes=[pltpu.SemaphoreType.DMA] * count,
        compiler_params=SMALL,
        cost_estimate=pl.CostEstimate(flops=span, transcendentals=0, bytes_accessed=0) if span else None,
        name=name,
    )(*ins, *(in_hbm(one) for one, _, _ in staged))


def iota(shape, dim):
    return lax.broadcasted_iota(i32, shape, dim)


def exact(x):
    return x.astype(f32).astype(bf16)


def split(x):
    return jnp.concatenate([x >> 8, x & 255], axis=0)


def piece_of(n):
    return jnp.where(n < NEAR, n >> 1, ((n - NEAR) * 43) >> 9)


def active_in(n, ctl=None):
    if ctl is None:
        return n < BLOCKS
    rnd, rounds = ctl
    piece = piece_of(n)
    within = jnp.where(n < NEAR, n & 1, NP + (n - NEAR) - FP * piece)
    of = (rnd * 37) >> 8
    pair = (piece == of) & ((within >> 1) == rnd - 7 * of)
    return (n < BLOCKS) & (((rounds == HALVES) & ((piece >> 2) == rnd)) | ((rounds != HALVES) & pair))


def payload_kernel(table_ref, near_ref, far_ref, out_ref):
    out_ref[...] = jnp.zeros_like(out_ref)
    for r in range(N_ROW):
        out_ref[r, 0:4, :] = table_ref[...]
        out_ref[r, 4:5, 0:NEAR] = near_ref[1:2, :]
        out_ref[r, 5:6, 0:FAR] = far_ref[1:2, :]
        out_ref[r, 6:7, :] = jnp.full((1, LANES), r, i32)


def make_payload(source_cluster, near_index, far_index):
    return call(
        payload_kernel,
        [in_hbm(one) for one in (source_cluster.reshape(4, LANES), near_index, far_index)],
        [VMEM, VMEM, VMEM],
        (jax.ShapeDtypeStruct((N_ROW, PIECE_ROWS, LANES), i32),),
        (VMEM,),
        "payload",
    )[0]


def index_kernel(g_ref, *refs):
    req_ref, snd_ref, pos_ref = refs[-3:]
    ctl = (refs[0][0] - 1, refs[1][0]) if len(refs) > 3 else None
    rho = g_ref[0, 6:7, :]
    tables = jnp.concatenate([g_ref[:, q, :] for q in range(4)], axis=1)
    n = iota((N_ROW, LANES), 1)
    m = jnp.where(n < NEAR, g_ref[:, 4, :], pltpu.roll(g_ref[:, 5, :], NEAR, 1))
    active = active_in(n, ctl)
    tab = exact(split(tables))
    piece_mask = (iota((N_ROW, LANES), 0) == piece_of(n)).astype(f32)
    place = iota((CLU_DEV, LANES), 0)
    rows = []
    for r in range(N_ROW):
        onehot = exact(place == m[r : r + 1, :])
        found = jnp.dot(tab, onehot, preferred_element_type=f32)
        value = found[0:N_ROW] * 256.0 + found[N_ROW : 2 * N_ROW]
        rows.append(jnp.sum(value * piece_mask, axis=0, keepdims=True))
    gid = jnp.concatenate(rows, axis=0).astype(i32)
    owner = jnp.where(active, gid >> 9, -1)
    owner_row = owner >> 4
    local = gid & (CLU_DEV - 1)
    every = iota((LANES, LANES), 0)
    counts = jnp.zeros((LANES, LANES), f32)
    for r in range(N_ROW):
        counts = counts + (every == owner[r : r + 1, :]).astype(f32)
    early = (piece_of(iota((1, LANES), 1)) < N_ROW // 2).astype(f32)
    col_label = iota((N_COL, LANES), 0) + rho * N_COL
    row_label = iota((N_ROW, LANES), 0)
    to_col = jnp.concatenate([(col_label == owner[r : r + 1, :]).astype(f32) for r in range(N_ROW)], axis=0)
    to_row = jnp.concatenate([(row_label == owner_row[r : r + 1, :]).astype(f32) for r in range(N_ROW)], axis=0)
    sub, lane = iota((LANES, LANES), 0), iota((LANES, LANES), 1)
    scan = jnp.concatenate([exact(sub < lane), jnp.ones((LANES, LANES), bf16)], axis=1)
    ahead = jnp.dot(to_col.astype(bf16), scan, preferred_element_type=f32)
    earlier = exact(((sub & (N_COL - 1)) == (lane & (N_COL - 1))) & (sub > lane))
    offset = jnp.dot(earlier, ahead[:, LANES:].astype(bf16), preferred_element_type=f32)
    first = to_col * (ahead[:, :LANES] + offset)
    second = to_row * jnp.dot(to_row.astype(bf16), scan[:, :LANES], preferred_element_type=f32)
    slot1 = jnp.concatenate(
        [jnp.sum(first[r * N_COL : (r + 1) * N_COL], axis=0, keepdims=True) for r in range(N_ROW)], axis=0
    ).astype(i32)
    slot2 = jnp.concatenate(
        [jnp.sum(second[r * N_ROW : (r + 1) * N_ROW], axis=0, keepdims=True) for r in range(N_ROW)], axis=0
    ).astype(i32)
    fits = [
        (jnp.max(jnp.sum(counts * part, axis=1, keepdims=True)) <= CAP_COL)
        & (jnp.max(jnp.sum(to_row * part, axis=1, keepdims=True)) <= CAP_ROW)
        for part in (jnp.ones((1, LANES), f32), early, 1.0 - early)
    ]
    over = jnp.where(fits[0], 0, jnp.where(fits[1] & fits[2], 1, 2))
    pos = jnp.clip(owner_row * CAP_ROW + slot2, 0, N_ROW * CAP_ROW - 1)
    pos_ref[...] = jnp.sum(jnp.where(row_label == rho, pos, 0).astype(f32), axis=0, keepdims=True).astype(i32)
    mine = owner_row == rho
    pos1 = jnp.clip((owner & (N_COL - 1)) * CAP_COL + slot1, 0, N_COL * CAP_COL - 1)
    req = jnp.zeros((2 * N_COL, LANES), f32)
    snd = jnp.zeros((2 * N_ROW, LANES), f32)
    for r in range(N_ROW):
        sel = to_col[r * N_COL : (r + 1) * N_COL] > 0.5
        value = split(jnp.where(sel, local[r : r + 1, :], 0))
        put = exact(sub == jnp.where(slot1[r : r + 1, :] < CAP_COL, slot1[r : r + 1, :], -1))
        req = req + lax.dot_general(exact(value), put, NT, preferred_element_type=f32)
        value = split(jnp.where((row_label == r) & mine[r : r + 1, :], pos1[r : r + 1, :], 0))
        put = exact(sub == jnp.where(slot2[r : r + 1, :] < CAP_ROW, slot2[r : r + 1, :], -1))
        snd = snd + lax.dot_general(exact(value), put, NT, preferred_element_type=f32)
    req = (req[0:N_COL] * 256.0 + req[N_COL : 2 * N_COL]).astype(i32)
    req_ref[...] = jnp.where(iota((N_COL, LANES), 1) == LANES - 1, over, req)
    snd_ref[...] = (snd[0:N_ROW] * 256.0 + snd[N_ROW : 2 * N_ROW]).astype(i32)


def make_index(gathered, slip, ctl=()):
    square = jax.ShapeDtypeStruct((N_ROW, LANES), i32)
    return call(
        index_kernel,
        (gathered, *ctl),
        [VMEM] + [SMEM] * len(ctl),
        (jax.ShapeDtypeStruct((N_COL, LANES), i32), square, jax.ShapeDtypeStruct((1, LANES), i32)),
        (VMEM, VMEM, VMEM),
        "index",
        ((slip, 0, CLU_DEV),),
    )


def gather_kernel(idx_ref, slip_ref, out_ref):
    def one_col(c, _):
        for k in range(CAP_COL):
            out_ref[c * CAP_COL + k] = slip_ref[idx_ref[c, k]]
        return 0

    lax.fori_loop(0, N_COL, one_col, 0)


def gather_rows(idx, slip):
    return call(
        gather_kernel,
        (idx, slip),
        [SMEM, VMEM],
        (jax.ShapeDtypeStruct((N_COL * CAP_COL, 2, B), f32),),
        (VMEM,),
        "gather",
    )[0]


def forward_kernel(idx_ref, got_ref, out_ref):
    def one_row(r, _):
        for k in range(CAP_ROW):
            out_ref[r * CAP_ROW + k] = got_ref[idx_ref[r, k]]
        return 0

    lax.fori_loop(0, N_ROW, one_row, 0)


def forward_rows(idx, got):
    return call(
        forward_kernel,
        (idx, got),
        [SMEM, VMEM],
        (jax.ShapeDtypeStruct((N_ROW * CAP_ROW, 2, B), f32),),
        (VMEM,),
        "forward",
        span=SPAN,
    )[0]


CHUNK = 64


def add_near(acc_ref, near_ref, at, x, row):
    x0, x1 = x[0:1, :], x[1:2, :]
    here = iota((CHUNK, LANES), 1) == row
    for s in range(0, 2 * B, CHUNK):
        rows = pl.ds(s, CHUNK)
        prod = near_ref[at, rows, 0:B] * x0 + near_ref[at, rows, B : 2 * B] * x1
        total = jnp.sum(prod[:, 0:LANES] + prod[:, LANES:B], axis=1, keepdims=True)
        old = acc_ref[rows, :]
        acc_ref[rows, :] = jnp.where(here, old + total, old)


def add_far(out_ref, left_ref, right_ref, at, x, row):
    x = x.astype(bf16).astype(f32)
    right = right_ref[at].astype(f32)
    prod = right[:, 0:B] * x[0:1, :] + right[:, B : 2 * B] * x[1:2, :]
    coef = jnp.sum(prod[:, 0:LANES] + prod[:, LANES:B], axis=1, keepdims=True)
    coef = coef.astype(bf16).astype(f32)
    far = jnp.sum(left_ref[at].astype(f32) * coef, axis=0, keepdims=True)
    rows = pl.ds(row, 1)
    out_ref[rows, :] = out_ref[rows, :] + far


def blocks_kernel(
    pos_hbm, asked_hbm, near_row_hbm, far_row_hbm, a_hbm, b_hbm, s_hbm, fault_ref, x_ref, left_ref,
    right_ref, near_ref,
    out_ref, param_ref, rounds_out, to_do_out,
    acc_ref, pos_ref, asked_ref, near_row_ref, far_row_ref, a_ref, b_ref, s_ref,
    rounds_ref, small_sems, out_sems,
):
    small = [
        pltpu.make_async_copy(one, to, small_sems.at[k])
        for k, (one, to) in enumerate(
            [
                (pos_hbm, pos_ref),
                (far_row_hbm, far_row_ref),
                (near_row_hbm, near_row_ref),
                (asked_hbm, asked_ref),
                (a_hbm, a_ref),
                (b_hbm, b_ref),
                (s_hbm, s_ref),
            ]
        )
    ]
    for copy in small:
        copy.start()
    out_ref[...] = jnp.zeros_like(out_ref)
    acc_ref[...] = jnp.zeros_like(acc_ref)
    for copy in small:
        copy.wait()
    over = asked_ref[0, LANES - 1]
    for c in range(1, N_COL):
        over = jnp.maximum(over, asked_ref[c, LANES - 1])
    rounds_ref[0] = jnp.where(over == 0, 0, jnp.where(over == 1, HALVES, ROUNDS))
    told = [
        pltpu.make_async_copy(rounds_ref, to, out_sems.at[k])
        for k, to in enumerate((rounds_out, to_do_out))
    ]
    for copy in told:
        copy.start()
    fault = fault_ref[...]
    found = [jnp.zeros(fault.shape, f32) for _ in range(3)]
    for f in range(FAULTS):
        here = fault == f
        found = [jnp.where(here, one[f], old) for one, old in zip((a_ref, b_ref, s_ref), found)]
    for k in range(3):
        param_ref[k] = found[k]

    def some_far(p, _):
        for t in range(FP):
            n = p * FP + t
            add_far(out_ref, left_ref, right_ref, n, x_ref[pos_ref[0, NEAR + n]], far_row_ref[0, n])
        return 0

    lax.fori_loop(0, N_ROW, some_far, 0)
    def two_near(q, _):
        for t in range(2):
            n = 2 * q + t
            add_near(acc_ref, near_ref, n, x_ref[pos_ref[0, n]], near_row_ref[0, n])
        return 0

    lax.fori_loop(0, NEAR // 2, two_near, 0)
    out_ref[...] = out_ref[...] + acc_ref[...].T
    for copy in told:
        copy.wait()


def block_sums(pos, asked, near_index, far_index, params, fault, x, left, right, near):
    one = jax.ShapeDtypeStruct((1,), i32)
    small = (pos, asked, near_index, far_index, *params)
    return pl.pallas_call(
        blocks_kernel,
        out_shape=(
            jax.ShapeDtypeStruct((RC_DEV, 2 * B), f32),
            jax.ShapeDtypeStruct((3,) + fault.shape, f32),
            one,
            one,
        ),
        in_specs=[ANY] * len(small) + [VMEM, VMEM, VMEM, VMEM, VMEM],
        out_specs=(VMEM, VMEM, ANY, ANY),
        scratch_shapes=[
            pltpu.VMEM((2 * B, LANES), f32),
            *(pltpu.SMEM(x.shape, x.dtype) for x in small),
            pltpu.SMEM((1,), i32),
            pltpu.SemaphoreType.DMA((len(small),)),
            pltpu.SemaphoreType.DMA((2,)),
        ],
        compiler_params=pltpu.CompilerParams(vmem_limit_bytes=28 * 1024 * 1024),
        name="blocks",
    )(*small, fault, x, left, right, near)


def pick_kernel(to_do_ref, rounds_ref, pos_ref, x_ref, out_ref):
    def one(n, _):
        taken = active_in(n, (to_do_ref[0] - 1, rounds_ref[0]))
        x = x_ref[pos_ref[0, n]]
        out_ref[n] = jnp.where(taken, x, jnp.zeros_like(x))
        return 0

    lax.fori_loop(0, LANES, one, 0)


def pick_rows(to_do, rounds, pos, x):
    return call(
        pick_kernel,
        (to_do, rounds, pos, x),
        [SMEM, SMEM, SMEM, VMEM],
        (jax.ShapeDtypeStruct((LANES, 2, B), f32),),
        (VMEM,),
        "pick",
    )[0]


def round_kernel(
    pos_ref, near_row_ref, far_row_ref, x_ref, near_ref, left_ref, right_ref, out_ref, acc_ref
):
    p = pl.program_id(0)

    @pl.when(p == 0)
    def _():
        out_ref[...] = jnp.zeros_like(out_ref)
        acc_ref[...] = jnp.zeros_like(acc_ref)

    for t in range(NP):
        n = p * NP + t
        add_near(acc_ref, near_ref, t, x_ref[pos_ref[0, n]], near_row_ref[0, n])
    for t in range(FP):
        n = p * FP + t
        add_far(out_ref, left_ref, right_ref, t, x_ref[pos_ref[0, NEAR + n]], far_row_ref[0, n])

    @pl.when(p == N_ROW - 1)
    def _():
        out_ref[...] = out_ref[...] + acc_ref[...].T


def round_sums(pos, near_index, far_index, x, near, left, right):
    return pl.pallas_call(
        round_kernel,
        grid=(N_ROW,),
        out_shape=jax.ShapeDtypeStruct((RC_DEV, 2 * B), f32),
        in_specs=[SMEM, SMEM, SMEM, pl.BlockSpec(x.shape, lambda p: (0, 0, 0))]
        + [
            pl.BlockSpec((one.shape[0] // N_ROW,) + one.shape[1:], lambda p: (p, 0, 0))
            for one in (near, left, right)
        ],
        out_specs=pl.BlockSpec((RC_DEV, 2 * B), lambda p: (0, 0)),
        scratch_shapes=[pltpu.VMEM((2 * B, LANES), f32)],
        compiler_params=pltpu.CompilerParams(vmem_limit_bytes=10 * 1024 * 1024),
        name="round",
    )(pos, near_index, far_index, x, in_hbm(near), in_hbm(left), in_hbm(right))


def final_kernel(param_ref, parts_ref, stress_ref, state_ref, out_stress, out_rate, out_state):
    total = parts_ref[0]
    for c in range(1, N_COL):
        total = total + parts_ref[c]
    groups = RC_DEV // N_COL
    for h in range(2):
        every = pl.ds(h, groups, stride=2)
        state = state_ref[every, :]
        a, b, sigma = (param_ref[k, every, :] for k in range(3))
        square = jnp.ones_like(state)
        for k in range(2):
            old = jnp.concatenate(
                [
                    stress_ref[k : k + 1, g * B + h * LANES : g * B + (h + 1) * LANES]
                    for g in range(groups)
                ],
                axis=0,
            )
            new = old + STEP_SIZE * total[:, k * B + h * LANES : k * B + (h + 1) * LANES]
            for g in range(groups):
                out_stress[k : k + 1, g * B + h * LANES : g * B + (h + 1) * LANES] = new[g : g + 1, :]
            square = square + new * new
        z = jnp.sqrt(square) / (a * sigma)
        u = state / a
        rate = jnp.exp(z - u) - jnp.exp(-z - u)
        out_rate[every, :] = rate
        out_state[every, :] = state + STEP_SIZE * b * (jnp.exp(-state / b) - rate)


def finish(params, parts, stress, state):
    rows = stress.shape[1] // LANES
    new_stress, new_rate, new_state = call(
        final_kernel,
        (params, parts.reshape(N_COL, RC_DEV // N_COL, 2 * B), stress, state.reshape(rows, LANES)),
        [VMEM] * 4,
        (
            jax.ShapeDtypeStruct(stress.shape, f32),
            jax.ShapeDtypeStruct((rows, LANES), f32),
            jax.ShapeDtypeStruct((rows, LANES), f32),
        ),
        (VMEM,) * 3,
        "finish",
    )
    return (new_stress, new_rate.reshape(-1), new_state.reshape(-1))


def body(
    slip_rate,
    source_cluster,
    near_kernel,
    near_pattern,
    far_left,
    far_right,
    far_pattern,
    stress,
    state,
    fault_of_row,
    direct_effect,
    evolution_effect,
    normal_stress,
):
    near, left, right = near_kernel[0, 0], far_left[0, 0], far_right[0, 0]
    near_index, far_index = near_pattern[0, 0], far_pattern[0, 0]
    slip = jnp.transpose(slip_rate.reshape(2, CLU_DEV, B), (1, 0, 2))
    gathered = lax.all_to_all(
        make_payload(source_cluster, near_index, far_index), "row", 0, 0, tiled=True
    )

    def fetch(*ctl):
        req, snd, pos, slip_held = make_index(gathered, slip, ctl)
        asked = lax.all_to_all(req, "col", 0, 0, tiled=True)
        got = lax.all_to_all(gather_rows(asked, slip_held), "col", 0, 0, tiled=True)
        return lax.all_to_all(forward_rows(snd, got), "row", 0, 0, tiled=True), pos, asked

    x, pos, asked = fetch()
    faults = (direct_effect, evolution_effect, normal_stress)
    fault = fault_of_row.reshape(-1, LANES)
    fast, params, rounds, to_do = block_sums(
        pos, asked, near_index, far_index, faults, fault, x, left, right, near
    )

    def one_round(carry):
        to_do, total = carry
        now = to_do.reshape(1)
        x, pos, _ = fetch(now, rounds)
        rows = pick_rows(now, rounds, pos, x)
        n = jnp.arange(LANES, dtype=i32)[None, :]
        part = round_sums(n, near_index, far_index, rows, near, left, right)
        return to_do - 1, jnp.where(to_do == rounds[0], 0.0, total) + part

    _, summed = lax.while_loop(lambda carry: carry[0] > 0, one_round, (to_do.reshape(()), fast))
    parts = lax.all_to_all(summed, "col", 0, 0, tiled=True)
    return finish(params, parts, stress, state)


def solution(mesh):
    return jax.shard_map(
        body,
        mesh=mesh,
        in_specs=(
            P(None, ("row", "col")),
            P(("row", "col")),
            P("row", "col", None, None, None),
            P("row", "col", None, None),
            P("row", "col", None, None, None),
            P("row", "col", None, None, None),
            P("row", "col", None, None),
            P(None, ("row", "col")),
            P(("row", "col")),
            P(("row", "col")),
            P(),
            P(),
            P(),
        ),
        out_specs=(P(None, ("row", "col")), P(("row", "col")), P(("row", "col"))),
        check_vma=False,
    )
```

```python
import functools

import functools

import jax
import jax.numpy as jnp
from jax import lax
from jax.experimental import pallas as pl
from jax.experimental.pallas import tpu as pltpu
from jax.sharding import PartitionSpec as P

B = 256
R = 32
CLU_DEV = 512
RC_DEV = 128
NP = 2
FP = 12
N_ROW = 8
N_COL = 16
NEAR = N_ROW * NP
FAR = N_ROW * FP
BLOCKS = NEAR + FAR
LANES = 128
CAP_COL = 24
CAP_ROW = 32
HALVES = 2
SPAN = 15 * 10**9
ROUNDS = 56
PIECE_ROWS = 8
FAULTS = 40
STEP_SIZE = 0.25

VMEM = pl.BlockSpec(memory_space=pltpu.VMEM)
SMEM = pl.BlockSpec(memory_space=pltpu.SMEM)
HBM = pl.BlockSpec(memory_space=pltpu.HBM)
ANY = pl.BlockSpec(memory_space=pl.ANY)
f32 = jnp.float32
bf16 = jnp.bfloat16
i32 = jnp.int32
NT = (((1,), (1,)), ((), ()))
SMALL = pltpu.CompilerParams(vmem_limit_bytes=6 * 1024 * 1024)


def in_hbm(x):
    return pltpu.with_memory_space_constraint(x, pltpu.HBM)


def call(kernel, ins, specs, outs, out_specs, name, staged=(), span=0):
    count, given, made = len(staged), len(ins), len(outs)

    def run(*refs):
        held = refs[given + count + made : given + 2 * count + made]
        copies = [
            pltpu.make_async_copy(one.at[pl.ds(first, size)], to, done)
            for one, to, done, (_, first, size) in zip(
                refs[given : given + count], held, refs[given + 2 * count + made :], staged
            )
        ]
        for copy in copies:
            copy.start()
        kernel(*refs[:given], *refs[given + count : given + count + made])
        for copy in copies:
            copy.wait()

    return pl.pallas_call(
        run,
        out_shape=tuple(outs)
        + tuple(pltpu.VMEM((size,) + one.shape[1:], one.dtype) for one, _, size in staged),
        in_specs=list(specs) + [HBM] * count,
        out_specs=tuple(out_specs) + (VMEM,) * count,
        scratch_shapes=[pltpu.SemaphoreType.DMA] * count,
        compiler_params=SMALL,
        cost_estimate=pl.CostEstimate(flops=span, transcendentals=0, bytes_accessed=0) if span else None,
        name=name,
    )(*ins, *(in_hbm(one) for one, _, _ in staged))


def iota(shape, dim):
    return lax.broadcasted_iota(i32, shape, dim)


def exact(x):
    return x.astype(f32).astype(bf16)


def split(x):
    return jnp.concatenate([x >> 8, x & 255], axis=0)


def piece_of(n):
    return jnp.where(n < NEAR, n >> 1, ((n - NEAR) * 43) >> 9)


def active_in(n, ctl=None):
    if ctl is None:
        return n < BLOCKS
    rnd, rounds = ctl
    piece = piece_of(n)
    within = jnp.where(n < NEAR, n & 1, NP + (n - NEAR) - FP * piece)
    of = (rnd * 37) >> 8
    pair = (piece == of) & ((within >> 1) == rnd - 7 * of)
    return (n < BLOCKS) & (((rounds == HALVES) & ((piece >> 2) == rnd)) | ((rounds != HALVES) & pair))


def payload_kernel(table_ref, near_ref, far_ref, out_ref):
    out_ref[...] = jnp.zeros_like(out_ref)
    for r in range(N_ROW):
        out_ref[r, 0:4, :] = table_ref[...]
        out_ref[r, 4:5, 0:NEAR] = near_ref[1:2, :]
        out_ref[r, 5:6, 0:FAR] = far_ref[1:2, :]
        out_ref[r, 6:7, :] = jnp.full((1, LANES), r, i32)


def make_payload(source_cluster, near_index, far_index):
    return call(
        payload_kernel,
        [in_hbm(one) for one in (source_cluster.reshape(4, LANES), near_index, far_index)],
        [VMEM, VMEM, VMEM],
        (jax.ShapeDtypeStruct((N_ROW, PIECE_ROWS, LANES), i32),),
        (VMEM,),
        "payload",
    )[0]


def index_kernel(g_ref, *refs):
    req_ref, snd_ref, pos_ref = refs[-3:]
    ctl = (refs[0][0] - 1, refs[1][0]) if len(refs) > 3 else None
    rho = g_ref[0, 6:7, :]
    tables = jnp.concatenate([g_ref[:, q, :] for q in range(4)], axis=1)
    n = iota((N_ROW, LANES), 1)
    m = jnp.where(n < NEAR, g_ref[:, 4, :], pltpu.roll(g_ref[:, 5, :], NEAR, 1))
    active = active_in(n, ctl)
    tab = exact(split(tables))
    piece_mask = (iota((N_ROW, LANES), 0) == piece_of(n)).astype(f32)
    place = iota((CLU_DEV, LANES), 0)
    rows = []
    for r in range(N_ROW):
        onehot = exact(place == m[r : r + 1, :])
        found = jnp.dot(tab, onehot, preferred_element_type=f32)
        value = found[0:N_ROW] * 256.0 + found[N_ROW : 2 * N_ROW]
        rows.append(jnp.sum(value * piece_mask, axis=0, keepdims=True))
    gid = jnp.concatenate(rows, axis=0).astype(i32)
    owner = jnp.where(active, gid >> 9, -1)
    owner_row = owner >> 4
    local = gid & (CLU_DEV - 1)
    every = iota((LANES, LANES), 0)
    counts = jnp.zeros((LANES, LANES), f32)
    for r in range(N_ROW):
        counts = counts + (every == owner[r : r + 1, :]).astype(f32)
    early = (piece_of(iota((1, LANES), 1)) < N_ROW // 2).astype(f32)
    col_label = iota((N_COL, LANES), 0) + rho * N_COL
    row_label = iota((N_ROW, LANES), 0)
    to_col = jnp.concatenate([(col_label == owner[r : r + 1, :]).astype(f32) for r in range(N_ROW)], axis=0)
    to_row = jnp.concatenate([(row_label == owner_row[r : r + 1, :]).astype(f32) for r in range(N_ROW)], axis=0)
    sub, lane = iota((LANES, LANES), 0), iota((LANES, LANES), 1)
    scan = jnp.concatenate([exact(sub < lane), jnp.ones((LANES, LANES), bf16)], axis=1)
    ahead = jnp.dot(to_col.astype(bf16), scan, preferred_element_type=f32)
    earlier = exact(((sub & (N_COL - 1)) == (lane & (N_COL - 1))) & (sub > lane))
    offset = jnp.dot(earlier, ahead[:, LANES:].astype(bf16), preferred_element_type=f32)
    first = to_col * (ahead[:, :LANES] + offset)
    second = to_row * jnp.dot(to_row.astype(bf16), scan[:, :LANES], preferred_element_type=f32)
    slot1 = jnp.concatenate(
        [jnp.sum(first[r * N_COL : (r + 1) * N_COL], axis=0, keepdims=True) for r in range(N_ROW)], axis=0
    ).astype(i32)
    slot2 = jnp.concatenate(
        [jnp.sum(second[r * N_ROW : (r + 1) * N_ROW], axis=0, keepdims=True) for r in range(N_ROW)], axis=0
    ).astype(i32)
    fits = [
        (jnp.max(jnp.sum(counts * part, axis=1, keepdims=True)) <= CAP_COL)
        & (jnp.max(jnp.sum(to_row * part, axis=1, keepdims=True)) <= CAP_ROW)
        for part in (jnp.ones((1, LANES), f32), early, 1.0 - early)
    ]
    over = jnp.where(fits[0], 0, jnp.where(fits[1] & fits[2], 1, 2))
    pos = jnp.clip(owner_row * CAP_ROW + slot2, 0, N_ROW * CAP_ROW - 1)
    pos_ref[...] = jnp.sum(jnp.where(row_label == rho, pos, 0).astype(f32), axis=0, keepdims=True).astype(i32)
    mine = owner_row == rho
    pos1 = jnp.clip((owner & (N_COL - 1)) * CAP_COL + slot1, 0, N_COL * CAP_COL - 1)
    req = jnp.zeros((2 * N_COL, LANES), f32)
    snd = jnp.zeros((2 * N_ROW, LANES), f32)
    for r in range(N_ROW):
        sel = to_col[r * N_COL : (r + 1) * N_COL] > 0.5
        value = split(jnp.where(sel, local[r : r + 1, :], 0))
        put = exact(sub == jnp.where(slot1[r : r + 1, :] < CAP_COL, slot1[r : r + 1, :], -1))
        req = req + lax.dot_general(exact(value), put, NT, preferred_element_type=f32)
        value = split(jnp.where((row_label == r) & mine[r : r + 1, :], pos1[r : r + 1, :], 0))
        put = exact(sub == jnp.where(slot2[r : r + 1, :] < CAP_ROW, slot2[r : r + 1, :], -1))
        snd = snd + lax.dot_general(exact(value), put, NT, preferred_element_type=f32)
    req = (req[0:N_COL] * 256.0 + req[N_COL : 2 * N_COL]).astype(i32)
    req_ref[...] = jnp.where(iota((N_COL, LANES), 1) == LANES - 1, over, req)
    snd_ref[...] = (snd[0:N_ROW] * 256.0 + snd[N_ROW : 2 * N_ROW]).astype(i32)


def make_index(gathered, ctl=()):
    square = jax.ShapeDtypeStruct((N_ROW, LANES), i32)
    return call(
        index_kernel,
        (gathered, *ctl),
        [VMEM] + [SMEM] * len(ctl),
        (jax.ShapeDtypeStruct((N_COL, LANES), i32), square, jax.ShapeDtypeStruct((1, LANES), i32)),
        (VMEM, VMEM, VMEM),
        "index",
        span=SPAN,
    )


def gather_kernel(idx_ref, slip_ref, out_ref):
    def one_col(c, _):
        for k in range(CAP_COL):
            out_ref[c * CAP_COL + k] = slip_ref[idx_ref[c, k]]
        return 0

    lax.fori_loop(0, N_COL, one_col, 0)


def gather_rows(idx, slip):
    return call(
        gather_kernel,
        (idx, slip),
        [SMEM, VMEM],
        (jax.ShapeDtypeStruct((N_COL * CAP_COL, 2, B), f32),),
        (VMEM,),
        "gather",
    )[0]


def forward_kernel(idx_ref, got_ref, out_ref):
    def one_row(r, _):
        for k in range(CAP_ROW):
            out_ref[r * CAP_ROW + k] = got_ref[idx_ref[r, k]]
        return 0

    lax.fori_loop(0, N_ROW, one_row, 0)


def forward_rows(idx, got):
    return call(
        forward_kernel,
        (idx, got),
        [SMEM, VMEM],
        (jax.ShapeDtypeStruct((N_ROW * CAP_ROW, 2, B), f32),),
        (VMEM,),
        "forward",
    )[0]


CHUNK = 128


def near_sum(near_ref, at, rows, x):
    prod = near_ref[at, rows, 0:B] * x[0:1, :] + near_ref[at, rows, B : 2 * B] * x[1:2, :]
    return jnp.sum(prod[:, 0:LANES] + prod[:, LANES:B], axis=1, keepdims=True)


def add_near(acc_ref, near_ref, at, x, row):
    here = iota((CHUNK, LANES), 1) == row
    for s in range(0, 2 * B, CHUNK):
        rows = pl.ds(s, CHUNK)
        old = acc_ref[rows, :]
        acc_ref[rows, :] = jnp.where(here, old + near_sum(near_ref, at, rows, x), old)


def add_far(out_ref, left_ref, right_ref, at, x, row):
    x = x.astype(bf16).astype(f32)
    right = right_ref[at].astype(f32)
    prod = right[:, 0:B] * x[0:1, :] + right[:, B : 2 * B] * x[1:2, :]
    coef = jnp.sum(prod[:, 0:LANES] + prod[:, LANES:B], axis=1, keepdims=True)
    coef = coef.astype(bf16).astype(f32)
    far = jnp.sum(left_ref[at].astype(f32) * coef, axis=0, keepdims=True)
    rows = pl.ds(row, 1)
    out_ref[rows, :] = out_ref[rows, :] + far


def blocks_kernel(
    pos_hbm, asked_hbm, near_row_hbm, far_row_hbm, a_hbm, b_hbm, s_hbm, fault_ref, x_ref, left_ref,
    right_ref, near_ref,
    out_ref, param_ref, rounds_out, to_do_out,
    acc_ref, pos_ref, asked_ref, near_row_ref, far_row_ref, a_ref, b_ref, s_ref,
    rounds_ref, small_sems, out_sems,
):
    small = [
        pltpu.make_async_copy(one, to, small_sems.at[k])
        for k, (one, to) in enumerate(
            [
                (pos_hbm, pos_ref),
                (far_row_hbm, far_row_ref),
                (near_row_hbm, near_row_ref),
                (asked_hbm, asked_ref),
                (a_hbm, a_ref),
                (b_hbm, b_ref),
                (s_hbm, s_ref),
            ]
        )
    ]
    for copy in small:
        copy.start()
    out_ref[...] = jnp.zeros_like(out_ref)
    for copy in small:
        copy.wait()
    over = asked_ref[0, LANES - 1]
    for c in range(1, N_COL):
        over = jnp.maximum(over, asked_ref[c, LANES - 1])
    rounds_ref[0] = jnp.where(over == 0, 0, jnp.where(over == 1, HALVES, ROUNDS))
    told = [
        pltpu.make_async_copy(rounds_ref, to, out_sems.at[k])
        for k, to in enumerate((rounds_out, to_do_out))
    ]
    for copy in told:
        copy.start()
    fault = fault_ref[...]
    found = [jnp.zeros(fault.shape, f32) for _ in range(3)]
    for f in range(FAULTS):
        here = fault == f
        found = [jnp.where(here, one[f], old) for one, old in zip((a_ref, b_ref, s_ref), found)]
    for k in range(3):
        param_ref[k] = found[k]

    def some_far(p, _):
        for t in range(FP):
            n = p * FP + t
            add_far(out_ref, left_ref, right_ref, n, x_ref[pos_ref[0, NEAR + n]], far_row_ref[0, n])
        return 0

    lax.fori_loop(0, N_ROW, some_far, 0)
    xs = [x_ref[pos_ref[0, n]] for n in range(NEAR)]
    lane = iota((CHUNK, LANES), 1)

    def some_rows(q, _):
        rows = pl.ds(pl.multiple_of(q * CHUNK, CHUNK), CHUNK)
        acc = jnp.zeros((CHUNK, LANES), f32)
        for n in range(NEAR):
            acc = jnp.where(lane == near_row_ref[0, n], acc + near_sum(near_ref, n, rows, xs[n]), acc)
        acc_ref[rows, :] = acc
        return 0

    lax.fori_loop(0, 2 * B // CHUNK, some_rows, 0)
    out_ref[...] = out_ref[...] + acc_ref[...].T
    for copy in told:
        copy.wait()


def block_sums(pos, asked, near_index, far_index, params, fault, x, left, right, near):
    one = jax.ShapeDtypeStruct((1,), i32)
    small = (pos, asked, near_index, far_index, *params)
    return pl.pallas_call(
        blocks_kernel,
        out_shape=(
            jax.ShapeDtypeStruct((RC_DEV, 2 * B), f32),
            jax.ShapeDtypeStruct((3,) + fault.shape, f32),
            one,
            one,
        ),
        in_specs=[ANY] * len(small) + [VMEM, VMEM, VMEM, VMEM, VMEM],
        out_specs=(VMEM, VMEM, ANY, ANY),
        scratch_shapes=[
            pltpu.VMEM((2 * B, LANES), f32),
            *(pltpu.SMEM(x.shape, x.dtype) for x in small),
            pltpu.SMEM((1,), i32),
            pltpu.SemaphoreType.DMA((len(small),)),
            pltpu.SemaphoreType.DMA((2,)),
        ],
        compiler_params=pltpu.CompilerParams(vmem_limit_bytes=28 * 1024 * 1024),
        name="blocks",
    )(*small, fault, x, left, right, near)


def pick_kernel(to_do_ref, rounds_ref, pos_ref, x_ref, out_ref):
    def one(n, _):
        taken = active_in(n, (to_do_ref[0] - 1, rounds_ref[0]))
        x = x_ref[pos_ref[0, n]]
        out_ref[n] = jnp.where(taken, x, jnp.zeros_like(x))
        return 0

    lax.fori_loop(0, LANES, one, 0)


def pick_rows(to_do, rounds, pos, x):
    return call(
        pick_kernel,
        (to_do, rounds, pos, x),
        [SMEM, SMEM, SMEM, VMEM],
        (jax.ShapeDtypeStruct((LANES, 2, B), f32),),
        (VMEM,),
        "pick",
    )[0]


def round_kernel(
    pos_ref, near_row_ref, far_row_ref, x_ref, near_ref, left_ref, right_ref, out_ref, acc_ref
):
    p = pl.program_id(0)

    @pl.when(p == 0)
    def _():
        out_ref[...] = jnp.zeros_like(out_ref)
        acc_ref[...] = jnp.zeros_like(acc_ref)

    for t in range(NP):
        n = p * NP + t
        add_near(acc_ref, near_ref, t, x_ref[pos_ref[0, n]], near_row_ref[0, n])
    for t in range(FP):
        n = p * FP + t
        add_far(out_ref, left_ref, right_ref, t, x_ref[pos_ref[0, NEAR + n]], far_row_ref[0, n])

    @pl.when(p == N_ROW - 1)
    def _():
        out_ref[...] = out_ref[...] + acc_ref[...].T


def round_sums(pos, near_index, far_index, x, near, left, right):
    return pl.pallas_call(
        round_kernel,
        grid=(N_ROW,),
        out_shape=jax.ShapeDtypeStruct((RC_DEV, 2 * B), f32),
        in_specs=[SMEM, SMEM, SMEM, pl.BlockSpec(x.shape, lambda p: (0, 0, 0))]
        + [
            pl.BlockSpec((one.shape[0] // N_ROW,) + one.shape[1:], lambda p: (p, 0, 0))
            for one in (near, left, right)
        ],
        out_specs=pl.BlockSpec((RC_DEV, 2 * B), lambda p: (0, 0)),
        scratch_shapes=[pltpu.VMEM((2 * B, LANES), f32)],
        compiler_params=pltpu.CompilerParams(vmem_limit_bytes=10 * 1024 * 1024),
        name="round",
    )(pos, near_index, far_index, x, in_hbm(near), in_hbm(left), in_hbm(right))


def final_kernel(param_ref, parts_ref, stress_ref, state_ref, out_stress, out_rate, out_state):
    total = parts_ref[0]
    for c in range(1, N_COL):
        total = total + parts_ref[c]
    groups = RC_DEV // N_COL
    for h in range(2):
        every = pl.ds(h, groups, stride=2)
        state = state_ref[every, :]
        a, b, sigma = (param_ref[k, every, :] for k in range(3))
        square = jnp.ones_like(state)
        for k in range(2):
            old = jnp.concatenate(
                [
                    stress_ref[k : k + 1, g * B + h * LANES : g * B + (h + 1) * LANES]
                    for g in range(groups)
                ],
                axis=0,
            )
            new = old + STEP_SIZE * total[:, k * B + h * LANES : k * B + (h + 1) * LANES]
            for g in range(groups):
                out_stress[k : k + 1, g * B + h * LANES : g * B + (h + 1) * LANES] = new[g : g + 1, :]
            square = square + new * new
        z = jnp.sqrt(square) / (a * sigma)
        u = state / a
        rate = jnp.exp(z - u) - jnp.exp(-z - u)
        out_rate[every, :] = rate
        out_state[every, :] = state + STEP_SIZE * b * (jnp.exp(-state / b) - rate)


def finish(params, parts, stress, state):
    rows = stress.shape[1] // LANES
    new_stress, new_rate, new_state = call(
        final_kernel,
        (params, parts.reshape(N_COL, RC_DEV // N_COL, 2 * B), stress, state.reshape(rows, LANES)),
        [VMEM] * 4,
        (
            jax.ShapeDtypeStruct(stress.shape, f32),
            jax.ShapeDtypeStruct((rows, LANES), f32),
            jax.ShapeDtypeStruct((rows, LANES), f32),
        ),
        (VMEM,) * 3,
        "finish",
    )
    return (new_stress, new_rate.reshape(-1), new_state.reshape(-1))


def body(
    slip_rate,
    source_cluster,
    near_kernel,
    near_pattern,
    far_left,
    far_right,
    far_pattern,
    stress,
    state,
    fault_of_row,
    direct_effect,
    evolution_effect,
    normal_stress,
):
    near, left, right = near_kernel[0, 0], far_left[0, 0], far_right[0, 0]
    near_index, far_index = near_pattern[0, 0], far_pattern[0, 0]
    slip = jnp.transpose(slip_rate.reshape(2, CLU_DEV, B), (1, 0, 2))
    gathered = lax.all_to_all(
        make_payload(source_cluster, near_index, far_index), "row", 0, 0, tiled=True
    )

    def fetch(*ctl):
        req, snd, pos = make_index(gathered, ctl)
        asked = lax.all_to_all(req, "col", 0, 0, tiled=True)
        got = lax.all_to_all(gather_rows(asked, slip), "col", 0, 0, tiled=True)
        return lax.all_to_all(forward_rows(snd, got), "row", 0, 0, tiled=True), pos, asked

    x, pos, asked = fetch()
    faults = (direct_effect, evolution_effect, normal_stress)
    fault = fault_of_row.reshape(-1, LANES)
    fast, params, rounds, to_do = block_sums(
        pos, asked, near_index, far_index, faults, fault, x, left, right, near
    )

    def one_round(carry):
        to_do, total = carry
        now = to_do.reshape(1)
        x, pos, _ = fetch(now, rounds)
        rows = pick_rows(now, rounds, pos, x)
        n = jnp.arange(LANES, dtype=i32)[None, :]
        part = round_sums(n, near_index, far_index, rows, near, left, right)
        return to_do - 1, jnp.where(to_do == rounds[0], 0.0, total) + part

    _, summed = lax.while_loop(lambda carry: carry[0] > 0, one_round, (to_do.reshape(()), fast))
    parts = lax.all_to_all(summed, "col", 0, 0, tiled=True)
    return finish(params, parts, stress, state)


def solution(mesh):
    return jax.shard_map(
        body,
        mesh=mesh,
        in_specs=(
            P(None, ("row", "col")),
            P(("row", "col")),
            P("row", "col", None, None, None),
            P("row", "col", None, None),
            P("row", "col", None, None, None),
            P("row", "col", None, None, None),
            P("row", "col", None, None),
            P(None, ("row", "col")),
            P(("row", "col")),
            P(("row", "col")),
            P(),
            P(),
            P(),
        ),
        out_specs=(P(None, ("row", "col")), P(("row", "col")), P(("row", "col"))),
        check_vma=False,
    )
```

```python
import functools

import functools

import jax
import jax.numpy as jnp
from jax import lax
from jax.experimental import pallas as pl
from jax.experimental.pallas import tpu as pltpu
from jax.sharding import PartitionSpec as P

B = 256
R = 32
CLU_DEV = 512
RC_DEV = 128
NP = 2
FP = 12
N_ROW = 8
N_COL = 16
NEAR = N_ROW * NP
FAR = N_ROW * FP
BLOCKS = NEAR + FAR
LANES = 128
CAP_COL = 24
CAP_ROW = 32
HALVES = 2
SPAN = 15 * 10**9
ROUNDS = 56
PIECE_ROWS = 8
FAULTS = 40
STEP_SIZE = 0.25

VMEM = pl.BlockSpec(memory_space=pltpu.VMEM)
SMEM = pl.BlockSpec(memory_space=pltpu.SMEM)
HBM = pl.BlockSpec(memory_space=pltpu.HBM)
ANY = pl.BlockSpec(memory_space=pl.ANY)
f32 = jnp.float32
bf16 = jnp.bfloat16
i32 = jnp.int32
NT = (((1,), (1,)), ((), ()))
SMALL = pltpu.CompilerParams(vmem_limit_bytes=6 * 1024 * 1024)


def in_hbm(x):
    return pltpu.with_memory_space_constraint(x, pltpu.HBM)


def call(kernel, ins, specs, outs, out_specs, name):
    return pl.pallas_call(
        kernel,
        out_shape=tuple(outs),
        in_specs=list(specs),
        out_specs=tuple(out_specs),
        compiler_params=SMALL,
        name=name,
    )(*ins)


def iota(shape, dim):
    return lax.broadcasted_iota(i32, shape, dim)


def exact(x):
    return x.astype(f32).astype(bf16)


def split(x):
    return jnp.concatenate([x >> 8, x & 255], axis=0)


def piece_of(n):
    return jnp.where(n < NEAR, n >> 1, ((n - NEAR) * 43) >> 9)


def active_in(n, ctl=None):
    if ctl is None:
        return n < BLOCKS
    rnd, rounds = ctl
    piece = piece_of(n)
    within = jnp.where(n < NEAR, n & 1, NP + (n - NEAR) - FP * piece)
    of = (rnd * 37) >> 8
    pair = (piece == of) & ((within >> 1) == rnd - 7 * of)
    return (n < BLOCKS) & (((rounds == HALVES) & ((piece >> 2) == rnd)) | ((rounds != HALVES) & pair))


def payload_kernel(table_ref, near_ref, far_ref, out_ref):
    out_ref[...] = jnp.zeros_like(out_ref)
    for r in range(N_ROW):
        out_ref[r, 0:4, :] = table_ref[...]
        out_ref[r, 4:5, 0:NEAR] = near_ref[1:2, :]
        out_ref[r, 5:6, 0:FAR] = far_ref[1:2, :]
        out_ref[r, 6:7, :] = jnp.full((1, LANES), r, i32)


def make_payload(source_cluster, near_index, far_index):
    return call(
        payload_kernel,
        [in_hbm(one) for one in (source_cluster.reshape(4, LANES), near_index, far_index)],
        [VMEM, VMEM, VMEM],
        (jax.ShapeDtypeStruct((N_ROW, PIECE_ROWS, LANES), i32),),
        (VMEM,),
        "payload",
    )[0]


def index_kernel(g_ref, *refs):
    near_hbm, far_hbm = refs[0:2]
    req_ref, snd_out, pos_out, near_out, far_out, snd_ref, pos_ref, sems = refs[-8:]
    ctl = (refs[2][0] - 1, refs[3][0]) if len(refs) > 10 else None
    clusters = [
        pltpu.make_async_copy(near_hbm, near_out, sems.at[0]),
        pltpu.make_async_copy(far_hbm, far_out, sems.at[1]),
    ]
    lists = [
        pltpu.make_async_copy(pos_ref, pos_out, sems.at[2]),
        pltpu.make_async_copy(snd_ref, snd_out, sems.at[3]),
    ]
    for copy in clusters:
        copy.start()
    rho = g_ref[0, 6:7, :]
    tables = jnp.concatenate([g_ref[:, q, :] for q in range(4)], axis=1)
    n = iota((N_ROW, LANES), 1)
    m = jnp.where(n < NEAR, g_ref[:, 4, :], pltpu.roll(g_ref[:, 5, :], NEAR, 1))
    active = active_in(n, ctl)
    tab = exact(split(tables))
    piece_mask = (iota((N_ROW, LANES), 0) == piece_of(n)).astype(f32)
    place = iota((CLU_DEV, LANES), 0)
    rows = []
    for r in range(N_ROW):
        onehot = exact(place == m[r : r + 1, :])
        found = jnp.dot(tab, onehot, preferred_element_type=f32)
        value = found[0:N_ROW] * 256.0 + found[N_ROW : 2 * N_ROW]
        rows.append(jnp.sum(value * piece_mask, axis=0, keepdims=True))
    gid = jnp.concatenate(rows, axis=0).astype(i32)
    owner = jnp.where(active, gid >> 9, -1)
    owner_row = owner >> 4
    local = gid & (CLU_DEV - 1)
    every = iota((LANES, LANES), 0)
    counts = jnp.zeros((LANES, LANES), f32)
    for r in range(N_ROW):
        counts = counts + (every == owner[r : r + 1, :]).astype(f32)
    early = (piece_of(iota((1, LANES), 1)) < N_ROW // 2).astype(f32)
    col_label = iota((N_COL, LANES), 0) + rho * N_COL
    row_label = iota((N_ROW, LANES), 0)
    to_col = jnp.concatenate([(col_label == owner[r : r + 1, :]).astype(f32) for r in range(N_ROW)], axis=0)
    to_row = jnp.concatenate([(row_label == owner_row[r : r + 1, :]).astype(f32) for r in range(N_ROW)], axis=0)
    sub, lane = iota((LANES, LANES), 0), iota((LANES, LANES), 1)
    scan = jnp.concatenate([exact(sub < lane), jnp.ones((LANES, LANES), bf16)], axis=1)
    ahead = jnp.dot(to_col.astype(bf16), scan, preferred_element_type=f32)
    earlier = exact(((sub & (N_COL - 1)) == (lane & (N_COL - 1))) & (sub > lane))
    offset = jnp.dot(earlier, ahead[:, LANES:].astype(bf16), preferred_element_type=f32)
    first = to_col * (ahead[:, :LANES] + offset)
    second = to_row * jnp.dot(to_row.astype(bf16), scan[:, :LANES], preferred_element_type=f32)
    slot1 = jnp.concatenate(
        [jnp.sum(first[r * N_COL : (r + 1) * N_COL], axis=0, keepdims=True) for r in range(N_ROW)], axis=0
    ).astype(i32)
    slot2 = jnp.concatenate(
        [jnp.sum(second[r * N_ROW : (r + 1) * N_ROW], axis=0, keepdims=True) for r in range(N_ROW)], axis=0
    ).astype(i32)
    fits = [
        (jnp.max(jnp.sum(counts * part, axis=1, keepdims=True)) <= CAP_COL)
        & (jnp.max(jnp.sum(to_row * part, axis=1, keepdims=True)) <= CAP_ROW)
        for part in (jnp.ones((1, LANES), f32), early, 1.0 - early)
    ]
    over = jnp.where(fits[0], 0, jnp.where(fits[1] & fits[2], 1, 2))
    pos = jnp.clip(owner_row * CAP_ROW + slot2, 0, N_ROW * CAP_ROW - 1)
    pos_ref[...] = jnp.sum(jnp.where(row_label == rho, pos, 0).astype(f32), axis=0, keepdims=True).astype(i32)
    lists[0].start()
    mine = owner_row == rho
    pos1 = jnp.clip((owner & (N_COL - 1)) * CAP_COL + slot1, 0, N_COL * CAP_COL - 1)
    snd = jnp.zeros((2 * N_ROW, LANES), f32)
    for r in range(N_ROW):
        value = split(jnp.where((row_label == r) & mine[r : r + 1, :], pos1[r : r + 1, :], 0))
        put = exact(sub == jnp.where(slot2[r : r + 1, :] < CAP_ROW, slot2[r : r + 1, :], -1))
        snd = snd + lax.dot_general(exact(value), put, NT, preferred_element_type=f32)
    snd_ref[...] = (snd[0:N_ROW] * 256.0 + snd[N_ROW : 2 * N_ROW]).astype(i32)
    lists[1].start()
    req = jnp.zeros((2 * N_COL, LANES), f32)
    for r in range(N_ROW):
        sel = to_col[r * N_COL : (r + 1) * N_COL] > 0.5
        value = split(jnp.where(sel, local[r : r + 1, :], 0))
        put = exact(sub == jnp.where(slot1[r : r + 1, :] < CAP_COL, slot1[r : r + 1, :], -1))
        req = req + lax.dot_general(exact(value), put, NT, preferred_element_type=f32)
    req = (req[0:N_COL] * 256.0 + req[N_COL : 2 * N_COL]).astype(i32)
    req_ref[...] = jnp.where(iota((N_COL, LANES), 1) == LANES - 1, over, req)
    for copy in clusters + lists:
        copy.wait()


def make_index(gathered, near_index, far_index, ctl=()):
    scalars = ((N_ROW, LANES), (1, LANES), near_index.shape, far_index.shape)
    return pl.pallas_call(
        index_kernel,
        out_shape=(jax.ShapeDtypeStruct((N_COL, LANES), i32), *(pltpu.SMEM(one, i32) for one in scalars)),
        in_specs=[VMEM, HBM, HBM] + [SMEM] * len(ctl),
        out_specs=(VMEM, SMEM, SMEM, SMEM, SMEM),
        scratch_shapes=[
            pltpu.VMEM((N_ROW, LANES), i32),
            pltpu.VMEM((1, LANES), i32),
            pltpu.SemaphoreType.DMA((4,)),
        ],
        compiler_params=SMALL,
        cost_estimate=pl.CostEstimate(flops=SPAN, transcendentals=0, bytes_accessed=0),
        name="index",
    )(gathered, in_hbm(near_index), in_hbm(far_index), *ctl)


def gather_kernel(idx_ref, slip_ref, out_ref):
    def one_col(c, _):
        for k in range(CAP_COL):
            out_ref[c * CAP_COL + k] = slip_ref[idx_ref[c, k]]
        return 0

    lax.fori_loop(0, N_COL, one_col, 0)


def gather_rows(idx, slip):
    return call(
        gather_kernel,
        (idx, slip),
        [SMEM, VMEM],
        (jax.ShapeDtypeStruct((N_COL * CAP_COL, 2, B), f32),),
        (VMEM,),
        "gather",
    )[0]


def forward_kernel(idx_ref, got_ref, out_ref):
    def one_row(r, _):
        for k in range(CAP_ROW):
            out_ref[r * CAP_ROW + k] = got_ref[idx_ref[r, k]]
        return 0

    lax.fori_loop(0, N_ROW, one_row, 0)


def forward_rows(idx, got):
    return call(
        forward_kernel,
        (idx, got),
        [SMEM, VMEM],
        (jax.ShapeDtypeStruct((N_ROW * CAP_ROW, 2, B), f32),),
        (VMEM,),
        "forward",
    )[0]


CHUNK = 128


def near_sum(near_ref, at, rows, x):
    prod = near_ref[at, rows, 0:B] * x[0:1, :] + near_ref[at, rows, B : 2 * B] * x[1:2, :]
    return jnp.sum(prod[:, 0:LANES] + prod[:, LANES:B], axis=1, keepdims=True)


def add_near(acc_ref, near_ref, at, x, row):
    here = iota((CHUNK, LANES), 1) == row
    for s in range(0, 2 * B, CHUNK):
        rows = pl.ds(s, CHUNK)
        old = acc_ref[rows, :]
        acc_ref[rows, :] = jnp.where(here, old + near_sum(near_ref, at, rows, x), old)


def add_far(out_ref, left_ref, right_ref, at, x, row):
    x = x.astype(bf16).astype(f32)
    right = right_ref[at].astype(f32)
    prod = right[:, 0:B] * x[0:1, :] + right[:, B : 2 * B] * x[1:2, :]
    coef = jnp.sum(prod[:, 0:LANES] + prod[:, LANES:B], axis=1, keepdims=True)
    coef = coef.astype(bf16).astype(f32)
    far = jnp.sum(left_ref[at].astype(f32) * coef, axis=0, keepdims=True)
    rows = pl.ds(row, 1)
    out_ref[rows, :] = out_ref[rows, :] + far


def blocks_kernel(
    pos_ref, near_row_ref, far_row_ref, asked_hbm, a_hbm, b_hbm, s_hbm, fault_ref, x_ref, left_ref,
    right_ref, near_ref,
    out_ref, param_ref, rounds_out, to_do_out,
    acc_ref, asked_ref, a_ref, b_ref, s_ref, rounds_ref, small_sems, out_sems,
):
    small = [
        pltpu.make_async_copy(one, to, small_sems.at[k])
        for k, (one, to) in enumerate(
            [(asked_hbm, asked_ref), (a_hbm, a_ref), (b_hbm, b_ref), (s_hbm, s_ref)]
        )
    ]
    for copy in small:
        copy.start()
    out_ref[...] = jnp.zeros_like(out_ref)

    def some_far(p, _):
        for t in range(FP):
            n = p * FP + t
            add_far(out_ref, left_ref, right_ref, n, x_ref[pos_ref[0, NEAR + n]], far_row_ref[0, n])
        return 0

    lax.fori_loop(0, N_ROW, some_far, 0)
    for copy in small:
        copy.wait()
    over = asked_ref[0, LANES - 1]
    for c in range(1, N_COL):
        over = jnp.maximum(over, asked_ref[c, LANES - 1])
    rounds_ref[0] = jnp.where(over == 0, 0, jnp.where(over == 1, HALVES, ROUNDS))
    told = [
        pltpu.make_async_copy(rounds_ref, to, out_sems.at[k])
        for k, to in enumerate((rounds_out, to_do_out))
    ]
    for copy in told:
        copy.start()
    fault = fault_ref[...]
    found = [jnp.zeros(fault.shape, f32) for _ in range(3)]
    for f in range(FAULTS):
        here = fault == f
        found = [jnp.where(here, one[f], old) for one, old in zip((a_ref, b_ref, s_ref), found)]
    for k in range(3):
        param_ref[k] = found[k]

    xs = [x_ref[pos_ref[0, n]] for n in range(NEAR)]
    lane = iota((CHUNK, LANES), 1)

    def some_rows(q, _):
        rows = pl.ds(pl.multiple_of(q * CHUNK, CHUNK), CHUNK)
        acc = jnp.zeros((CHUNK, LANES), f32)
        for n in range(NEAR):
            acc = jnp.where(lane == near_row_ref[0, n], acc + near_sum(near_ref, n, rows, xs[n]), acc)
        acc_ref[rows, :] = acc
        return 0

    lax.fori_loop(0, 2 * B // CHUNK, some_rows, 0)
    out_ref[...] = out_ref[...] + acc_ref[...].T
    for copy in told:
        copy.wait()


def block_sums(lists, asked, params, fault, x, left, right, near):
    one = jax.ShapeDtypeStruct((1,), i32)
    small = (asked, *params)
    return pl.pallas_call(
        blocks_kernel,
        out_shape=(
            jax.ShapeDtypeStruct((RC_DEV, 2 * B), f32),
            jax.ShapeDtypeStruct((3,) + fault.shape, f32),
            one,
            one,
        ),
        in_specs=[SMEM] * 3 + [ANY] * len(small) + [VMEM] * 5,
        out_specs=(VMEM, VMEM, ANY, ANY),
        scratch_shapes=[
            pltpu.VMEM((2 * B, LANES), f32),
            *(pltpu.SMEM(x.shape, x.dtype) for x in small),
            pltpu.SMEM((1,), i32),
            pltpu.SemaphoreType.DMA((len(small),)),
            pltpu.SemaphoreType.DMA((2,)),
        ],
        compiler_params=pltpu.CompilerParams(vmem_limit_bytes=28 * 1024 * 1024),
        name="blocks",
    )(*lists, *small, fault, x, left, right, near)


def pick_kernel(to_do_ref, rounds_ref, pos_ref, x_ref, out_ref):
    def one(n, _):
        taken = active_in(n, (to_do_ref[0] - 1, rounds_ref[0]))
        x = x_ref[pos_ref[0, n]]
        out_ref[n] = jnp.where(taken, x, jnp.zeros_like(x))
        return 0

    lax.fori_loop(0, LANES, one, 0)


def pick_rows(to_do, rounds, pos, x):
    return call(
        pick_kernel,
        (to_do, rounds, pos, x),
        [SMEM, SMEM, SMEM, VMEM],
        (jax.ShapeDtypeStruct((LANES, 2, B), f32),),
        (VMEM,),
        "pick",
    )[0]


def round_kernel(
    pos_ref, near_row_ref, far_row_ref, x_ref, near_ref, left_ref, right_ref, out_ref, acc_ref
):
    p = pl.program_id(0)

    @pl.when(p == 0)
    def _():
        out_ref[...] = jnp.zeros_like(out_ref)
        acc_ref[...] = jnp.zeros_like(acc_ref)

    for t in range(NP):
        n = p * NP + t
        add_near(acc_ref, near_ref, t, x_ref[pos_ref[0, n]], near_row_ref[0, n])
    for t in range(FP):
        n = p * FP + t
        add_far(out_ref, left_ref, right_ref, t, x_ref[pos_ref[0, NEAR + n]], far_row_ref[0, n])

    @pl.when(p == N_ROW - 1)
    def _():
        out_ref[...] = out_ref[...] + acc_ref[...].T


def round_sums(pos, near_index, far_index, x, near, left, right):
    return pl.pallas_call(
        round_kernel,
        grid=(N_ROW,),
        out_shape=jax.ShapeDtypeStruct((RC_DEV, 2 * B), f32),
        in_specs=[SMEM, SMEM, SMEM, pl.BlockSpec(x.shape, lambda p: (0, 0, 0))]
        + [
            pl.BlockSpec((one.shape[0] // N_ROW,) + one.shape[1:], lambda p: (p, 0, 0))
            for one in (near, left, right)
        ],
        out_specs=pl.BlockSpec((RC_DEV, 2 * B), lambda p: (0, 0)),
        scratch_shapes=[pltpu.VMEM((2 * B, LANES), f32)],
        compiler_params=pltpu.CompilerParams(vmem_limit_bytes=10 * 1024 * 1024),
        name="round",
    )(pos, near_index, far_index, x, in_hbm(near), in_hbm(left), in_hbm(right))


def final_kernel(param_ref, parts_ref, stress_ref, state_ref, out_stress, out_rate, out_state):
    total = parts_ref[0]
    for c in range(1, N_COL):
        total = total + parts_ref[c]
    groups = RC_DEV // N_COL
    for h in range(2):
        every = pl.ds(h, groups, stride=2)
        state = state_ref[every, :]
        a, b, sigma = (param_ref[k, every, :] for k in range(3))
        square = jnp.ones_like(state)
        for k in range(2):
            old = jnp.concatenate(
                [
                    stress_ref[k : k + 1, g * B + h * LANES : g * B + (h + 1) * LANES]
                    for g in range(groups)
                ],
                axis=0,
            )
            new = old + STEP_SIZE * total[:, k * B + h * LANES : k * B + (h + 1) * LANES]
            for g in range(groups):
                out_stress[k : k + 1, g * B + h * LANES : g * B + (h + 1) * LANES] = new[g : g + 1, :]
            square = square + new * new
        z = jnp.sqrt(square) / (a * sigma)
        u = state / a
        rate = jnp.exp(z - u) - jnp.exp(-z - u)
        out_rate[every, :] = rate
        out_state[every, :] = state + STEP_SIZE * b * (jnp.exp(-state / b) - rate)


def finish(params, parts, stress, state):
    rows = stress.shape[1] // LANES
    new_stress, new_rate, new_state = call(
        final_kernel,
        (params, parts.reshape(N_COL, RC_DEV // N_COL, 2 * B), stress, state.reshape(rows, LANES)),
        [VMEM] * 4,
        (
            jax.ShapeDtypeStruct(stress.shape, f32),
            jax.ShapeDtypeStruct((rows, LANES), f32),
            jax.ShapeDtypeStruct((rows, LANES), f32),
        ),
        (VMEM,) * 3,
        "finish",
    )
    return (new_stress, new_rate.reshape(-1), new_state.reshape(-1))


def body(
    slip_rate,
    source_cluster,
    near_kernel,
    near_pattern,
    far_left,
    far_right,
    far_pattern,
    stress,
    state,
    fault_of_row,
    direct_effect,
    evolution_effect,
    normal_stress,
):
    near, left, right = near_kernel[0, 0], far_left[0, 0], far_right[0, 0]
    near_index, far_index = near_pattern[0, 0], far_pattern[0, 0]
    slip = jnp.transpose(slip_rate.reshape(2, CLU_DEV, B), (1, 0, 2))
    gathered = lax.all_to_all(
        make_payload(source_cluster, near_index, far_index), "row", 0, 0, tiled=True
    )

    def fetch(*ctl):
        req, snd, *lists = make_index(gathered, near_index, far_index, ctl)
        asked = lax.all_to_all(req, "col", 0, 0, tiled=True)
        got = lax.all_to_all(gather_rows(asked, slip), "col", 0, 0, tiled=True)
        return lax.all_to_all(forward_rows(snd, got), "row", 0, 0, tiled=True), lists, asked

    x, lists, asked = fetch()
    faults = (direct_effect, evolution_effect, normal_stress)
    fault = fault_of_row.reshape(-1, LANES)
    fast, params, rounds, to_do = block_sums(lists, asked, faults, fault, x, left, right, near)

    def one_round(carry):
        to_do, total = carry
        now = to_do.reshape(1)
        x, lists, _ = fetch(now, rounds)
        rows = pick_rows(now, rounds, lists[0], x)
        n = jnp.arange(LANES, dtype=i32)[None, :]
        part = round_sums(n, near_index, far_index, rows, near, left, right)
        return to_do - 1, jnp.where(to_do == rounds[0], 0.0, total) + part

    _, summed = lax.while_loop(lambda carry: carry[0] > 0, one_round, (to_do.reshape(()), fast))
    parts = lax.all_to_all(summed, "col", 0, 0, tiled=True)
    return finish(params, parts, stress, state)


def solution(mesh):
    return jax.shard_map(
        body,
        mesh=mesh,
        in_specs=(
            P(None, ("row", "col")),
            P(("row", "col")),
            P("row", "col", None, None, None),
            P("row", "col", None, None),
            P("row", "col", None, None, None),
            P("row", "col", None, None, None),
            P("row", "col", None, None),
            P(None, ("row", "col")),
            P(("row", "col")),
            P(("row", "col")),
            P(),
            P(),
            P(),
        ),
        out_specs=(P(None, ("row", "col")), P(("row", "col")), P(("row", "col"))),
        check_vma=False,
    )
```

```python
import functools

import functools

import jax
import jax.numpy as jnp
from jax import lax
from jax.experimental import pallas as pl
from jax.experimental.pallas import tpu as pltpu
from jax.sharding import PartitionSpec as P

B = 256
R = 32
CLU_DEV = 512
RC_DEV = 128
NP = 2
FP = 12
N_ROW = 8
N_COL = 16
NEAR = N_ROW * NP
FAR = N_ROW * FP
BLOCKS = NEAR + FAR
LANES = 128
CAP_COL = 24
CAP_ROW = 32
HALVES = 2
SPAN = 15 * 10**9
ROUNDS = 56
PIECE_ROWS = 8
FAULTS = 40
STEP_SIZE = 0.25

VMEM = pl.BlockSpec(memory_space=pltpu.VMEM)
SMEM = pl.BlockSpec(memory_space=pltpu.SMEM)
HBM = pl.BlockSpec(memory_space=pltpu.HBM)
ANY = pl.BlockSpec(memory_space=pl.ANY)
f32 = jnp.float32
bf16 = jnp.bfloat16
i32 = jnp.int32
NT = (((1,), (1,)), ((), ()))
SMALL = pltpu.CompilerParams(vmem_limit_bytes=6 * 1024 * 1024)


def in_hbm(x):
    return pltpu.with_memory_space_constraint(x, pltpu.HBM)


def call(kernel, ins, specs, outs, out_specs, name):
    return pl.pallas_call(
        kernel,
        out_shape=tuple(outs),
        in_specs=list(specs),
        out_specs=tuple(out_specs),
        compiler_params=SMALL,
        name=name,
    )(*ins)


def iota(shape, dim):
    return lax.broadcasted_iota(i32, shape, dim)


def exact(x):
    return x.astype(f32).astype(bf16)


def split(x):
    return jnp.concatenate([x >> 8, x & 255], axis=0)


def piece_of(n):
    return jnp.where(n < NEAR, n >> 1, ((n - NEAR) * 43) >> 9)


def active_in(n, ctl=None):
    if ctl is None:
        return n < BLOCKS
    rnd, rounds = ctl
    piece = piece_of(n)
    within = jnp.where(n < NEAR, n & 1, NP + (n - NEAR) - FP * piece)
    of = (rnd * 37) >> 8
    pair = (piece == of) & ((within >> 1) == rnd - 7 * of)
    return (n < BLOCKS) & (((rounds == HALVES) & ((piece >> 2) == rnd)) | ((rounds != HALVES) & pair))


def payload_kernel(table_ref, near_ref, far_ref, out_ref):
    out_ref[...] = jnp.zeros_like(out_ref)
    for r in range(N_ROW):
        out_ref[r, 0:4, :] = table_ref[...]
        out_ref[r, 4:5, 0:NEAR] = near_ref[1:2, :]
        out_ref[r, 5:6, 0:FAR] = far_ref[1:2, :]
        out_ref[r, 6:7, :] = jnp.full((1, LANES), r, i32)


def make_payload(source_cluster, near_index, far_index):
    return call(
        payload_kernel,
        [in_hbm(one) for one in (source_cluster.reshape(4, LANES), near_index, far_index)],
        [VMEM, VMEM, VMEM],
        (jax.ShapeDtypeStruct((N_ROW, PIECE_ROWS, LANES), i32),),
        (VMEM,),
        "payload",
    )[0]


def index_kernel(g_ref, *refs):
    req_ref, snd_ref, pos_ref = refs[-3:]
    ctl = (refs[0][0] - 1, refs[1][0]) if len(refs) > 3 else None
    rho = g_ref[0, 6:7, :]
    tables = jnp.concatenate([g_ref[:, q, :] for q in range(4)], axis=1)
    n = iota((N_ROW, LANES), 1)
    m = jnp.where(n < NEAR, g_ref[:, 4, :], pltpu.roll(g_ref[:, 5, :], NEAR, 1))
    active = active_in(n, ctl)
    tab = exact(split(tables))
    piece_mask = (iota((N_ROW, LANES), 0) == piece_of(n)).astype(f32)
    place = iota((CLU_DEV, LANES), 0)
    rows = []
    for r in range(N_ROW):
        onehot = exact(place == m[r : r + 1, :])
        found = jnp.dot(tab, onehot, preferred_element_type=f32)
        value = found[0:N_ROW] * 256.0 + found[N_ROW : 2 * N_ROW]
        rows.append(jnp.sum(value * piece_mask, axis=0, keepdims=True))
    gid = jnp.concatenate(rows, axis=0).astype(i32)
    owner = jnp.where(active, gid >> 9, -1)
    owner_row = owner >> 4
    local = gid & (CLU_DEV - 1)
    every = iota((LANES, LANES), 0)
    counts = jnp.zeros((LANES, LANES), f32)
    for r in range(N_ROW):
        counts = counts + (every == owner[r : r + 1, :]).astype(f32)
    early = (piece_of(iota((1, LANES), 1)) < N_ROW // 2).astype(f32)
    col_label = iota((N_COL, LANES), 0) + rho * N_COL
    row_label = iota((N_ROW, LANES), 0)
    to_col = jnp.concatenate([(col_label == owner[r : r + 1, :]).astype(f32) for r in range(N_ROW)], axis=0)
    to_row = jnp.concatenate([(row_label == owner_row[r : r + 1, :]).astype(f32) for r in range(N_ROW)], axis=0)
    sub, lane = iota((LANES, LANES), 0), iota((LANES, LANES), 1)
    scan = jnp.concatenate([exact(sub < lane), jnp.ones((LANES, LANES), bf16)], axis=1)
    ahead = jnp.dot(to_col.astype(bf16), scan, preferred_element_type=f32)
    earlier = exact(((sub & (N_COL - 1)) == (lane & (N_COL - 1))) & (sub > lane))
    offset = jnp.dot(earlier, ahead[:, LANES:].astype(bf16), preferred_element_type=f32)
    first = to_col * (ahead[:, :LANES] + offset)
    second = to_row * jnp.dot(to_row.astype(bf16), scan[:, :LANES], preferred_element_type=f32)
    slot1 = jnp.concatenate(
        [jnp.sum(first[r * N_COL : (r + 1) * N_COL], axis=0, keepdims=True) for r in range(N_ROW)], axis=0
    ).astype(i32)
    slot2 = jnp.concatenate(
        [jnp.sum(second[r * N_ROW : (r + 1) * N_ROW], axis=0, keepdims=True) for r in range(N_ROW)], axis=0
    ).astype(i32)
    fits = [
        (jnp.max(jnp.sum(counts * part, axis=1, keepdims=True)) <= CAP_COL)
        & (jnp.max(jnp.sum(to_row * part, axis=1, keepdims=True)) <= CAP_ROW)
        for part in (jnp.ones((1, LANES), f32), early, 1.0 - early)
    ]
    over = jnp.where(fits[0], 0, jnp.where(fits[1] & fits[2], 1, 2))
    pos = jnp.clip(owner_row * CAP_ROW + slot2, 0, N_ROW * CAP_ROW - 1)
    pos_ref[...] = jnp.sum(jnp.where(row_label == rho, pos, 0).astype(f32), axis=0, keepdims=True).astype(i32)
    mine = owner_row == rho
    pos1 = jnp.clip((owner & (N_COL - 1)) * CAP_COL + slot1, 0, N_COL * CAP_COL - 1)
    snd = jnp.zeros((2 * N_ROW, LANES), f32)
    for r in range(N_ROW):
        value = split(jnp.where((row_label == r) & mine[r : r + 1, :], pos1[r : r + 1, :], 0))
        put = exact(sub == jnp.where(slot2[r : r + 1, :] < CAP_ROW, slot2[r : r + 1, :], -1))
        snd = snd + lax.dot_general(exact(value), put, NT, preferred_element_type=f32)
    snd_ref[...] = (snd[0:N_ROW] * 256.0 + snd[N_ROW : 2 * N_ROW]).astype(i32)
    req = jnp.zeros((2 * N_COL, LANES), f32)
    for r in range(N_ROW):
        sel = to_col[r * N_COL : (r + 1) * N_COL] > 0.5
        value = split(jnp.where(sel, local[r : r + 1, :], 0))
        put = exact(sub == jnp.where(slot1[r : r + 1, :] < CAP_COL, slot1[r : r + 1, :], -1))
        req = req + lax.dot_general(exact(value), put, NT, preferred_element_type=f32)
    req = (req[0:N_COL] * 256.0 + req[N_COL : 2 * N_COL]).astype(i32)
    req_ref[...] = jnp.where(iota((N_COL, LANES), 1) == LANES - 1, over, req)


def make_index(gathered, ctl=()):
    return pl.pallas_call(
        index_kernel,
        out_shape=(
            jax.ShapeDtypeStruct((N_COL, LANES), i32),
            jax.ShapeDtypeStruct((N_ROW, LANES), i32),
            jax.ShapeDtypeStruct((1, LANES), i32),
        ),
        in_specs=[VMEM] + [SMEM] * len(ctl),
        out_specs=(VMEM, VMEM, VMEM),
        compiler_params=SMALL,
        cost_estimate=pl.CostEstimate(flops=SPAN, transcendentals=0, bytes_accessed=0),
        name="index",
    )(gathered, *ctl)


def gather_kernel(idx_ref, slip_ref, *refs):
    lists, out_ref, held, sems = refs[:4], refs[4], refs[5:9], refs[9]
    copies = [pltpu.make_async_copy(one, to, sems.at[k]) for k, (one, to) in enumerate(zip(lists, held))]
    for copy in copies:
        copy.start()

    def one_col(c, _):
        for k in range(CAP_COL):
            out_ref[c * CAP_COL + k] = slip_ref[idx_ref[c, k]]
        return 0

    lax.fori_loop(0, N_COL, one_col, 0)
    for copy in copies:
        copy.wait()


def gather_rows(idx, slip, lists):
    return pl.pallas_call(
        gather_kernel,
        out_shape=(
            jax.ShapeDtypeStruct((N_COL * CAP_COL, 2, B), f32),
            *(pltpu.SMEM(one.shape, i32) for one in lists),
        ),
        in_specs=[SMEM, VMEM] + [ANY] * len(lists),
        out_specs=(VMEM,) + (SMEM,) * len(lists),
        scratch_shapes=[pltpu.SemaphoreType.DMA((len(lists),))],
        compiler_params=SMALL,
        name="gather",
    )(idx, slip, *lists)


def forward_kernel(idx_ref, got_ref, out_ref):
    def one_row(r, _):
        for k in range(CAP_ROW):
            out_ref[r * CAP_ROW + k] = got_ref[idx_ref[r, k]]
        return 0

    lax.fori_loop(0, N_ROW, one_row, 0)


def forward_rows(idx, got):
    return call(
        forward_kernel,
        (idx, got),
        [SMEM, VMEM],
        (jax.ShapeDtypeStruct((N_ROW * CAP_ROW, 2, B), f32),),
        (VMEM,),
        "forward",
    )[0]


CHUNK = 128


def near_sum(near_ref, at, rows, x):
    prod = near_ref[at, rows, 0:B] * x[0:1, :] + near_ref[at, rows, B : 2 * B] * x[1:2, :]
    return jnp.sum(prod[:, 0:LANES] + prod[:, LANES:B], axis=1, keepdims=True)


def add_near(acc_ref, near_ref, at, x, row):
    here = iota((CHUNK, LANES), 1) == row
    for s in range(0, 2 * B, CHUNK):
        rows = pl.ds(s, CHUNK)
        old = acc_ref[rows, :]
        acc_ref[rows, :] = jnp.where(here, old + near_sum(near_ref, at, rows, x), old)


def add_far(out_ref, left_ref, right_ref, at, x, row):
    x = x.astype(bf16).astype(f32)
    right = right_ref[at].astype(f32)
    prod = right[:, 0:B] * x[0:1, :] + right[:, B : 2 * B] * x[1:2, :]
    coef = jnp.sum(prod[:, 0:LANES] + prod[:, LANES:B], axis=1, keepdims=True)
    coef = coef.astype(bf16).astype(f32)
    far = jnp.sum(left_ref[at].astype(f32) * coef, axis=0, keepdims=True)
    rows = pl.ds(row, 1)
    out_ref[rows, :] = out_ref[rows, :] + far


def blocks_kernel(
    pos_ref, near_row_ref, far_row_ref, asked_hbm, a_hbm, b_hbm, s_hbm, fault_ref, x_ref, left_ref,
    right_ref, near_ref,
    out_ref, param_ref, rounds_out, to_do_out,
    acc_ref, asked_ref, a_ref, b_ref, s_ref, rounds_ref, small_sems, out_sems,
):
    small = [
        pltpu.make_async_copy(one, to, small_sems.at[k])
        for k, (one, to) in enumerate(
            [(asked_hbm, asked_ref), (a_hbm, a_ref), (b_hbm, b_ref), (s_hbm, s_ref)]
        )
    ]
    for copy in small:
        copy.start()
    out_ref[...] = jnp.zeros_like(out_ref)

    def some_far(p, _):
        for t in range(FP):
            n = p * FP + t
            add_far(out_ref, left_ref, right_ref, n, x_ref[pos_ref[0, NEAR + n]], far_row_ref[0, n])
        return 0

    lax.fori_loop(0, N_ROW, some_far, 0)
    for copy in small:
        copy.wait()
    over = asked_ref[0, LANES - 1]
    for c in range(1, N_COL):
        over = jnp.maximum(over, asked_ref[c, LANES - 1])
    rounds_ref[0] = jnp.where(over == 0, 0, jnp.where(over == 1, HALVES, ROUNDS))
    told = [
        pltpu.make_async_copy(rounds_ref, to, out_sems.at[k])
        for k, to in enumerate((rounds_out, to_do_out))
    ]
    for copy in told:
        copy.start()
    fault = fault_ref[...]
    found = [jnp.zeros(fault.shape, f32) for _ in range(3)]
    for f in range(FAULTS):
        here = fault == f
        found = [jnp.where(here, one[f], old) for one, old in zip((a_ref, b_ref, s_ref), found)]
    for k in range(3):
        param_ref[k] = found[k]

    xs = [x_ref[pos_ref[0, n]] for n in range(NEAR)]
    lane = iota((CHUNK, LANES), 1)

    def some_rows(q, _):
        rows = pl.ds(pl.multiple_of(q * CHUNK, CHUNK), CHUNK)
        acc = jnp.zeros((CHUNK, LANES), f32)
        for n in range(NEAR):
            acc = jnp.where(lane == near_row_ref[0, n], acc + near_sum(near_ref, n, rows, xs[n]), acc)
        acc_ref[rows, :] = acc
        return 0

    lax.fori_loop(0, 2 * B // CHUNK, some_rows, 0)
    out_ref[...] = out_ref[...] + acc_ref[...].T
    for copy in told:
        copy.wait()


def block_sums(lists, asked, params, fault, x, left, right, near):
    one = jax.ShapeDtypeStruct((1,), i32)
    small = (asked, *params)
    return pl.pallas_call(
        blocks_kernel,
        out_shape=(
            jax.ShapeDtypeStruct((RC_DEV, 2 * B), f32),
            jax.ShapeDtypeStruct((3,) + fault.shape, f32),
            one,
            one,
        ),
        in_specs=[SMEM] * 3 + [ANY] * len(small) + [VMEM] * 5,
        out_specs=(VMEM, VMEM, ANY, ANY),
        scratch_shapes=[
            pltpu.VMEM((2 * B, LANES), f32),
            *(pltpu.SMEM(x.shape, x.dtype) for x in small),
            pltpu.SMEM((1,), i32),
            pltpu.SemaphoreType.DMA((len(small),)),
            pltpu.SemaphoreType.DMA((2,)),
        ],
        compiler_params=pltpu.CompilerParams(vmem_limit_bytes=28 * 1024 * 1024),
        name="blocks",
    )(*lists, *small, fault, x, left, right, near)


def pick_kernel(to_do_ref, rounds_ref, pos_ref, x_ref, out_ref):
    def one(n, _):
        taken = active_in(n, (to_do_ref[0] - 1, rounds_ref[0]))
        x = x_ref[pos_ref[0, n]]
        out_ref[n] = jnp.where(taken, x, jnp.zeros_like(x))
        return 0

    lax.fori_loop(0, LANES, one, 0)


def pick_rows(to_do, rounds, pos, x):
    return call(
        pick_kernel,
        (to_do, rounds, pos, x),
        [SMEM, SMEM, SMEM, VMEM],
        (jax.ShapeDtypeStruct((LANES, 2, B), f32),),
        (VMEM,),
        "pick",
    )[0]


def round_kernel(
    pos_ref, near_row_ref, far_row_ref, x_ref, near_ref, left_ref, right_ref, out_ref, acc_ref
):
    p = pl.program_id(0)

    @pl.when(p == 0)
    def _():
        out_ref[...] = jnp.zeros_like(out_ref)
        acc_ref[...] = jnp.zeros_like(acc_ref)

    for t in range(NP):
        n = p * NP + t
        add_near(acc_ref, near_ref, t, x_ref[pos_ref[0, n]], near_row_ref[0, n])
    for t in range(FP):
        n = p * FP + t
        add_far(out_ref, left_ref, right_ref, t, x_ref[pos_ref[0, NEAR + n]], far_row_ref[0, n])

    @pl.when(p == N_ROW - 1)
    def _():
        out_ref[...] = out_ref[...] + acc_ref[...].T


def round_sums(pos, near_index, far_index, x, near, left, right):
    return pl.pallas_call(
        round_kernel,
        grid=(N_ROW,),
        out_shape=jax.ShapeDtypeStruct((RC_DEV, 2 * B), f32),
        in_specs=[SMEM, SMEM, SMEM, pl.BlockSpec(x.shape, lambda p: (0, 0, 0))]
        + [
            pl.BlockSpec((one.shape[0] // N_ROW,) + one.shape[1:], lambda p: (p, 0, 0))
            for one in (near, left, right)
        ],
        out_specs=pl.BlockSpec((RC_DEV, 2 * B), lambda p: (0, 0)),
        scratch_shapes=[pltpu.VMEM((2 * B, LANES), f32)],
        compiler_params=pltpu.CompilerParams(vmem_limit_bytes=10 * 1024 * 1024),
        name="round",
    )(pos, near_index, far_index, x, in_hbm(near), in_hbm(left), in_hbm(right))


def final_kernel(param_ref, parts_ref, stress_ref, state_ref, out_stress, out_rate, out_state):
    total = parts_ref[0]
    for c in range(1, N_COL):
        total = total + parts_ref[c]
    groups = RC_DEV // N_COL
    for h in range(2):
        every = pl.ds(h, groups, stride=2)
        state = state_ref[every, :]
        a, b, sigma = (param_ref[k, every, :] for k in range(3))
        square = jnp.ones_like(state)
        for k in range(2):
            old = jnp.concatenate(
                [
                    stress_ref[k : k + 1, g * B + h * LANES : g * B + (h + 1) * LANES]
                    for g in range(groups)
                ],
                axis=0,
            )
            new = old + STEP_SIZE * total[:, k * B + h * LANES : k * B + (h + 1) * LANES]
            for g in range(groups):
                out_stress[k : k + 1, g * B + h * LANES : g * B + (h + 1) * LANES] = new[g : g + 1, :]
            square = square + new * new
        z = jnp.sqrt(square) / (a * sigma)
        u = state / a
        rate = jnp.exp(z - u) - jnp.exp(-z - u)
        out_rate[every, :] = rate
        out_state[every, :] = state + STEP_SIZE * b * (jnp.exp(-state / b) - rate)


def finish(params, parts, stress, state):
    rows = stress.shape[1] // LANES
    new_stress, new_rate, new_state = call(
        final_kernel,
        (params, parts.reshape(N_COL, RC_DEV // N_COL, 2 * B), stress, state.reshape(rows, LANES)),
        [VMEM] * 4,
        (
            jax.ShapeDtypeStruct(stress.shape, f32),
            jax.ShapeDtypeStruct((rows, LANES), f32),
            jax.ShapeDtypeStruct((rows, LANES), f32),
        ),
        (VMEM,) * 3,
        "finish",
    )
    return (new_stress, new_rate.reshape(-1), new_state.reshape(-1))


def body(
    slip_rate,
    source_cluster,
    near_kernel,
    near_pattern,
    far_left,
    far_right,
    far_pattern,
    stress,
    state,
    fault_of_row,
    direct_effect,
    evolution_effect,
    normal_stress,
):
    near, left, right = near_kernel[0, 0], far_left[0, 0], far_right[0, 0]
    near_index, far_index = near_pattern[0, 0], far_pattern[0, 0]
    slip = jnp.transpose(slip_rate.reshape(2, CLU_DEV, B), (1, 0, 2))
    gathered = lax.all_to_all(
        make_payload(source_cluster, near_index, far_index), "row", 0, 0, tiled=True
    )

    def fetch(*ctl):
        req, snd, pos = make_index(gathered, ctl)
        asked = lax.all_to_all(req, "col", 0, 0, tiled=True)
        reply, snd, *lists = gather_rows(asked, slip, (snd, pos, near_index, far_index))
        got = lax.all_to_all(reply, "col", 0, 0, tiled=True)
        return lax.all_to_all(forward_rows(snd, got), "row", 0, 0, tiled=True), lists, asked

    x, lists, asked = fetch()
    faults = (direct_effect, evolution_effect, normal_stress)
    fault = fault_of_row.reshape(-1, LANES)
    fast, params, rounds, to_do = block_sums(lists, asked, faults, fault, x, left, right, near)

    def one_round(carry):
        to_do, total = carry
        now = to_do.reshape(1)
        x, lists, _ = fetch(now, rounds)
        rows = pick_rows(now, rounds, lists[0], x)
        n = jnp.arange(LANES, dtype=i32)[None, :]
        part = round_sums(n, near_index, far_index, rows, near, left, right)
        return to_do - 1, jnp.where(to_do == rounds[0], 0.0, total) + part

    _, summed = lax.while_loop(lambda carry: carry[0] > 0, one_round, (to_do.reshape(()), fast))
    parts = lax.all_to_all(summed, "col", 0, 0, tiled=True)
    return finish(params, parts, stress, state)


def solution(mesh):
    return jax.shard_map(
        body,
        mesh=mesh,
        in_specs=(
            P(None, ("row", "col")),
            P(("row", "col")),
            P("row", "col", None, None, None),
            P("row", "col", None, None),
            P("row", "col", None, None, None),
            P("row", "col", None, None, None),
            P("row", "col", None, None),
            P(None, ("row", "col")),
            P(("row", "col")),
            P(("row", "col")),
            P(),
            P(),
            P(),
        ),
        out_specs=(P(None, ("row", "col")), P(("row", "col")), P(("row", "col"))),
        check_vma=False,
    )
```

```python
import functools

import functools

import jax
import jax.numpy as jnp
from jax import lax
from jax.experimental import pallas as pl
from jax.experimental.pallas import tpu as pltpu
from jax.sharding import PartitionSpec as P

B = 256
R = 32
CLU_DEV = 512
RC_DEV = 128
NP = 2
FP = 12
N_ROW = 8
N_COL = 16
NEAR = N_ROW * NP
FAR = N_ROW * FP
BLOCKS = NEAR + FAR
LANES = 128
CAP_COL = 24
CAP_ROW = 32
HALVES = 2
SPAN = 15 * 10**9
ROUNDS = 56
PIECE_ROWS = 8
FAULTS = 40
STEP_SIZE = 0.25

VMEM = pl.BlockSpec(memory_space=pltpu.VMEM)
SMEM = pl.BlockSpec(memory_space=pltpu.SMEM)
HBM = pl.BlockSpec(memory_space=pltpu.HBM)
ANY = pl.BlockSpec(memory_space=pl.ANY)
f32 = jnp.float32
bf16 = jnp.bfloat16
i32 = jnp.int32
NT = (((1,), (1,)), ((), ()))
SMALL = pltpu.CompilerParams(vmem_limit_bytes=6 * 1024 * 1024)


def in_hbm(x):
    return pltpu.with_memory_space_constraint(x, pltpu.HBM)


def call(kernel, ins, specs, outs, out_specs, name):
    return pl.pallas_call(
        kernel,
        out_shape=tuple(outs),
        in_specs=list(specs),
        out_specs=tuple(out_specs),
        compiler_params=SMALL,
        name=name,
    )(*ins)


def iota(shape, dim):
    return lax.broadcasted_iota(i32, shape, dim)


def exact(x):
    return x.astype(f32).astype(bf16)


def split(x):
    return jnp.concatenate([x >> 8, x & 255], axis=0)


def piece_of(n):
    return jnp.where(n < NEAR, n >> 1, ((n - NEAR) * 43) >> 9)


def active_in(n, ctl=None):
    if ctl is None:
        return n < BLOCKS
    rnd, rounds = ctl
    piece = piece_of(n)
    within = jnp.where(n < NEAR, n & 1, NP + (n - NEAR) - FP * piece)
    of = (rnd * 37) >> 8
    pair = (piece == of) & ((within >> 1) == rnd - 7 * of)
    return (n < BLOCKS) & (((rounds == HALVES) & ((piece >> 2) == rnd)) | ((rounds != HALVES) & pair))


def payload_kernel(table_ref, near_ref, far_ref, out_ref):
    out_ref[...] = jnp.zeros_like(out_ref)
    for r in range(N_ROW):
        out_ref[r, 0:4, :] = table_ref[...]
        out_ref[r, 4:5, 0:NEAR] = near_ref[1:2, :]
        out_ref[r, 5:6, 0:FAR] = far_ref[1:2, :]
        out_ref[r, 6:7, :] = jnp.full((1, LANES), r, i32)


def make_payload(source_cluster, near_index, far_index):
    return call(
        payload_kernel,
        [in_hbm(one) for one in (source_cluster.reshape(4, LANES), near_index, far_index)],
        [VMEM, VMEM, VMEM],
        (jax.ShapeDtypeStruct((N_ROW, PIECE_ROWS, LANES), i32),),
        (VMEM,),
        "payload",
    )[0]


def index_kernel(g_ref, *refs):
    req_ref, snd_ref, pos_ref = refs[-3:]
    ctl = (refs[0][0] - 1, refs[1][0]) if len(refs) > 3 else None
    rho = g_ref[0, 6:7, :]
    tables = jnp.concatenate([g_ref[:, q, :] for q in range(4)], axis=1)
    n = iota((N_ROW, LANES), 1)
    m = jnp.where(n < NEAR, g_ref[:, 4, :], pltpu.roll(g_ref[:, 5, :], NEAR, 1))
    active = active_in(n, ctl)
    tab = exact(split(tables))
    piece_mask = (iota((N_ROW, LANES), 0) == piece_of(n)).astype(f32)
    place = iota((CLU_DEV, LANES), 0)
    rows = []
    for r in range(N_ROW):
        onehot = exact(place == m[r : r + 1, :])
        found = jnp.dot(tab, onehot, preferred_element_type=f32)
        value = found[0:N_ROW] * 256.0 + found[N_ROW : 2 * N_ROW]
        rows.append(jnp.sum(value * piece_mask, axis=0, keepdims=True))
    gid = jnp.concatenate(rows, axis=0).astype(i32)
    owner = jnp.where(active, gid >> 9, -1)
    owner_row = owner >> 4
    local = gid & (CLU_DEV - 1)
    every = iota((LANES, LANES), 0)
    counts = jnp.zeros((LANES, LANES), f32)
    for r in range(N_ROW):
        counts = counts + (every == owner[r : r + 1, :]).astype(f32)
    early = (piece_of(iota((1, LANES), 1)) < N_ROW // 2).astype(f32)
    col_label = iota((N_COL, LANES), 0) + rho * N_COL
    row_label = iota((N_ROW, LANES), 0)
    to_col = jnp.concatenate([(col_label == owner[r : r + 1, :]).astype(f32) for r in range(N_ROW)], axis=0)
    to_row = jnp.concatenate([(row_label == owner_row[r : r + 1, :]).astype(f32) for r in range(N_ROW)], axis=0)
    sub, lane = iota((LANES, LANES), 0), iota((LANES, LANES), 1)
    scan = jnp.concatenate([exact(sub < lane), jnp.ones((LANES, LANES), bf16)], axis=1)
    ahead = jnp.dot(to_col.astype(bf16), scan, preferred_element_type=f32)
    earlier = exact(((sub & (N_COL - 1)) == (lane & (N_COL - 1))) & (sub > lane))
    offset = jnp.dot(earlier, ahead[:, LANES:].astype(bf16), preferred_element_type=f32)
    first = to_col * (ahead[:, :LANES] + offset)
    second = to_row * jnp.dot(to_row.astype(bf16), scan[:, :LANES], preferred_element_type=f32)
    slot1 = jnp.concatenate(
        [jnp.sum(first[r * N_COL : (r + 1) * N_COL], axis=0, keepdims=True) for r in range(N_ROW)], axis=0
    ).astype(i32)
    slot2 = jnp.concatenate(
        [jnp.sum(second[r * N_ROW : (r + 1) * N_ROW], axis=0, keepdims=True) for r in range(N_ROW)], axis=0
    ).astype(i32)
    fits = [
        (jnp.max(jnp.sum(counts * part, axis=1, keepdims=True)) <= CAP_COL)
        & (jnp.max(jnp.sum(to_row * part, axis=1, keepdims=True)) <= CAP_ROW)
        for part in (jnp.ones((1, LANES), f32), early, 1.0 - early)
    ]
    over = jnp.where(fits[0], 0, jnp.where(fits[1] & fits[2], 1, 2))
    pos = jnp.clip(owner_row * CAP_ROW + slot2, 0, N_ROW * CAP_ROW - 1)
    pos_ref[...] = jnp.sum(jnp.where(row_label == rho, pos, 0).astype(f32), axis=0, keepdims=True).astype(i32)
    mine = owner_row == rho
    pos1 = jnp.clip((owner & (N_COL - 1)) * CAP_COL + slot1, 0, N_COL * CAP_COL - 1)
    place = iota((CAP_ROW, LANES), 0)
    snd = jnp.zeros((2 * N_ROW, CAP_ROW), f32)
    req = jnp.zeros((2 * N_COL, CAP_ROW), f32)
    for r in range(N_ROW):
        value = split(jnp.where((row_label == r) & mine[r : r + 1, :], pos1[r : r + 1, :], 0))
        put = exact(place == slot2[r : r + 1, :])
        snd = snd + lax.dot_general(exact(value), put, NT, preferred_element_type=f32)
        sel = to_col[r * N_COL : (r + 1) * N_COL] > 0.5
        value = split(jnp.where(sel, local[r : r + 1, :], 0))
        put = exact(place == jnp.where(slot1[r : r + 1, :] < CAP_COL, slot1[r : r + 1, :], -1))
        req = req + lax.dot_general(exact(value), put, NT, preferred_element_type=f32)
    snd_ref[...] = jnp.zeros_like(snd_ref)
    snd_ref[:, 0:CAP_ROW] = (snd[0:N_ROW] * 256.0 + snd[N_ROW : 2 * N_ROW]).astype(i32)
    req_ref[...] = jnp.full(req_ref.shape, over, i32)
    req_ref[:, 0:CAP_ROW] = (req[0:N_COL] * 256.0 + req[N_COL : 2 * N_COL]).astype(i32)


def make_index(gathered, ctl=()):
    return pl.pallas_call(
        index_kernel,
        out_shape=(
            jax.ShapeDtypeStruct((N_COL, LANES), i32),
            jax.ShapeDtypeStruct((N_ROW, LANES), i32),
            jax.ShapeDtypeStruct((1, LANES), i32),
        ),
        in_specs=[VMEM] + [SMEM] * len(ctl),
        out_specs=(VMEM, VMEM, VMEM),
        compiler_params=SMALL,
        cost_estimate=pl.CostEstimate(flops=SPAN, transcendentals=0, bytes_accessed=0),
        name="index",
    )(gathered, *ctl)


def gather_kernel(idx_hbm, slip_ref, *refs):
    lists, out_ref, held, idx_ref, sems = refs[:4], refs[4], refs[5:9], refs[9], refs[10]
    pairs = [(idx_hbm, idx_ref), *zip(lists, held)]
    copies = [pltpu.make_async_copy(one, to, sems.at[k]) for k, (one, to) in enumerate(pairs)]
    for copy in copies:
        copy.start()
    copies[0].wait()

    def one_col(c, _):
        for k in range(CAP_COL):
            out_ref[c * CAP_COL + k] = slip_ref[idx_ref[c, k]]
        return 0

    lax.fori_loop(0, N_COL, one_col, 0)
    for copy in copies[1:]:
        copy.wait()


def gather_rows(idx, slip, lists):
    return pl.pallas_call(
        gather_kernel,
        out_shape=(
            jax.ShapeDtypeStruct((N_COL * CAP_COL, 2, B), f32),
            *(pltpu.SMEM(one.shape, i32) for one in lists),
        ),
        in_specs=[ANY, VMEM] + [ANY] * len(lists),
        out_specs=(VMEM,) + (SMEM,) * len(lists),
        scratch_shapes=[pltpu.SMEM(idx.shape, i32), pltpu.SemaphoreType.DMA((1 + len(lists),))],
        compiler_params=SMALL,
        name="gather",
    )(idx, slip, *lists)


def forward_kernel(idx_ref, got_ref, out_ref):
    def one_row(r, _):
        for k in range(CAP_ROW):
            out_ref[r * CAP_ROW + k] = got_ref[idx_ref[r, k]]
        return 0

    lax.fori_loop(0, N_ROW, one_row, 0)


def forward_rows(idx, got):
    return call(
        forward_kernel,
        (idx, got),
        [SMEM, VMEM],
        (jax.ShapeDtypeStruct((N_ROW * CAP_ROW, 2, B), f32),),
        (VMEM,),
        "forward",
    )[0]


CHUNK = 128


def near_sum(near_ref, at, rows, x):
    prod = near_ref[at, rows, 0:B] * x[0:1, :] + near_ref[at, rows, B : 2 * B] * x[1:2, :]
    return jnp.sum(prod[:, 0:LANES] + prod[:, LANES:B], axis=1, keepdims=True)


def add_near(acc_ref, near_ref, at, x, row):
    here = iota((CHUNK, LANES), 1) == row
    for s in range(0, 2 * B, CHUNK):
        rows = pl.ds(s, CHUNK)
        old = acc_ref[rows, :]
        acc_ref[rows, :] = jnp.where(here, old + near_sum(near_ref, at, rows, x), old)


def add_far(out_ref, left_ref, right_ref, at, x, row):
    x = x.astype(bf16).astype(f32)
    right = right_ref[at].astype(f32)
    prod = right[:, 0:B] * x[0:1, :] + right[:, B : 2 * B] * x[1:2, :]
    coef = jnp.sum(prod[:, 0:LANES] + prod[:, LANES:B], axis=1, keepdims=True)
    coef = coef.astype(bf16).astype(f32)
    far = jnp.sum(left_ref[at].astype(f32) * coef, axis=0, keepdims=True)
    rows = pl.ds(row, 1)
    out_ref[rows, :] = out_ref[rows, :] + far


def blocks_kernel(
    pos_ref, near_row_ref, far_row_ref, asked_hbm, a_hbm, b_hbm, s_hbm, fault_ref, x_ref, left_ref,
    right_ref, near_ref,
    out_ref, param_ref, rounds_out, to_do_out,
    acc_ref, asked_ref, a_ref, b_ref, s_ref, rounds_ref, small_sems, out_sems,
):
    small = [
        pltpu.make_async_copy(one, to, small_sems.at[k])
        for k, (one, to) in enumerate(
            [(asked_hbm, asked_ref), (a_hbm, a_ref), (b_hbm, b_ref), (s_hbm, s_ref)]
        )
    ]
    for copy in small:
        copy.start()
    out_ref[...] = jnp.zeros_like(out_ref)

    def some_far(p, _):
        for t in range(FP):
            n = p * FP + t
            add_far(out_ref, left_ref, right_ref, n, x_ref[pos_ref[0, NEAR + n]], far_row_ref[0, n])
        return 0

    lax.fori_loop(0, N_ROW, some_far, 0, unroll=4)
    for copy in small:
        copy.wait()
    over = asked_ref[0, LANES - 1]
    for c in range(1, N_COL):
        over = jnp.maximum(over, asked_ref[c, LANES - 1])
    rounds_ref[0] = jnp.where(over == 0, 0, jnp.where(over == 1, HALVES, ROUNDS))
    told = [
        pltpu.make_async_copy(rounds_ref, to, out_sems.at[k])
        for k, to in enumerate((rounds_out, to_do_out))
    ]
    for copy in told:
        copy.start()
    fault = fault_ref[...]
    found = [jnp.zeros(fault.shape, f32) for _ in range(3)]
    for f in range(FAULTS):
        here = fault == f
        found = [jnp.where(here, one[f], old) for one, old in zip((a_ref, b_ref, s_ref), found)]
    for k in range(3):
        param_ref[k] = found[k]

    xs = [x_ref[pos_ref[0, n]] for n in range(NEAR)]
    lane = iota((CHUNK, LANES), 1)

    def some_rows(q, _):
        rows = pl.ds(pl.multiple_of(q * CHUNK, CHUNK), CHUNK)
        acc = jnp.zeros((CHUNK, LANES), f32)
        for n in range(NEAR):
            acc = jnp.where(lane == near_row_ref[0, n], acc + near_sum(near_ref, n, rows, xs[n]), acc)
        acc_ref[rows, :] = acc
        return 0

    lax.fori_loop(0, 2 * B // CHUNK, some_rows, 0, unroll=2)
    out_ref[...] = out_ref[...] + acc_ref[...].T
    for copy in told:
        copy.wait()


def block_sums(lists, asked, params, fault, x, left, right, near):
    one = jax.ShapeDtypeStruct((1,), i32)
    small = (asked, *params)
    return pl.pallas_call(
        blocks_kernel,
        out_shape=(
            jax.ShapeDtypeStruct((RC_DEV, 2 * B), f32),
            jax.ShapeDtypeStruct((3,) + fault.shape, f32),
            one,
            one,
        ),
        in_specs=[SMEM] * 3 + [ANY] * len(small) + [VMEM] * 5,
        out_specs=(VMEM, VMEM, ANY, ANY),
        scratch_shapes=[
            pltpu.VMEM((2 * B, LANES), f32),
            *(pltpu.SMEM(x.shape, x.dtype) for x in small),
            pltpu.SMEM((1,), i32),
            pltpu.SemaphoreType.DMA((len(small),)),
            pltpu.SemaphoreType.DMA((2,)),
        ],
        compiler_params=pltpu.CompilerParams(vmem_limit_bytes=28 * 1024 * 1024),
        name="blocks",
    )(*lists, *small, fault, x, left, right, near)


def pick_kernel(to_do_ref, rounds_ref, pos_ref, x_ref, out_ref):
    def one(n, _):
        taken = active_in(n, (to_do_ref[0] - 1, rounds_ref[0]))
        x = x_ref[pos_ref[0, n]]
        out_ref[n] = jnp.where(taken, x, jnp.zeros_like(x))
        return 0

    lax.fori_loop(0, LANES, one, 0)


def pick_rows(to_do, rounds, pos, x):
    return call(
        pick_kernel,
        (to_do, rounds, pos, x),
        [SMEM, SMEM, SMEM, VMEM],
        (jax.ShapeDtypeStruct((LANES, 2, B), f32),),
        (VMEM,),
        "pick",
    )[0]


def round_kernel(
    pos_ref, near_row_ref, far_row_ref, x_ref, near_ref, left_ref, right_ref, out_ref, acc_ref
):
    p = pl.program_id(0)

    @pl.when(p == 0)
    def _():
        out_ref[...] = jnp.zeros_like(out_ref)
        acc_ref[...] = jnp.zeros_like(acc_ref)

    for t in range(NP):
        n = p * NP + t
        add_near(acc_ref, near_ref, t, x_ref[pos_ref[0, n]], near_row_ref[0, n])
    for t in range(FP):
        n = p * FP + t
        add_far(out_ref, left_ref, right_ref, t, x_ref[pos_ref[0, NEAR + n]], far_row_ref[0, n])

    @pl.when(p == N_ROW - 1)
    def _():
        out_ref[...] = out_ref[...] + acc_ref[...].T


def round_sums(pos, near_index, far_index, x, near, left, right):
    return pl.pallas_call(
        round_kernel,
        grid=(N_ROW,),
        out_shape=jax.ShapeDtypeStruct((RC_DEV, 2 * B), f32),
        in_specs=[SMEM, SMEM, SMEM, pl.BlockSpec(x.shape, lambda p: (0, 0, 0))]
        + [
            pl.BlockSpec((one.shape[0] // N_ROW,) + one.shape[1:], lambda p: (p, 0, 0))
            for one in (near, left, right)
        ],
        out_specs=pl.BlockSpec((RC_DEV, 2 * B), lambda p: (0, 0)),
        scratch_shapes=[pltpu.VMEM((2 * B, LANES), f32)],
        compiler_params=pltpu.CompilerParams(vmem_limit_bytes=10 * 1024 * 1024),
        name="round",
    )(pos, near_index, far_index, x, in_hbm(near), in_hbm(left), in_hbm(right))


def final_kernel(param_ref, parts_ref, stress_ref, state_ref, out_stress, out_rate, out_state):
    total = parts_ref[0]
    for c in range(1, N_COL):
        total = total + parts_ref[c]
    groups = RC_DEV // N_COL
    for h in range(2):
        every = pl.ds(h, groups, stride=2)
        state = state_ref[every, :]
        a, b, sigma = (param_ref[k, every, :] for k in range(3))
        square = jnp.ones_like(state)
        for k in range(2):
            old = jnp.concatenate(
                [
                    stress_ref[k : k + 1, g * B + h * LANES : g * B + (h + 1) * LANES]
                    for g in range(groups)
                ],
                axis=0,
            )
            new = old + STEP_SIZE * total[:, k * B + h * LANES : k * B + (h + 1) * LANES]
            for g in range(groups):
                out_stress[k : k + 1, g * B + h * LANES : g * B + (h + 1) * LANES] = new[g : g + 1, :]
            square = square + new * new
        z = jnp.sqrt(square) / (a * sigma)
        u = state / a
        rate = jnp.exp(z - u) - jnp.exp(-z - u)
        out_rate[every, :] = rate
        out_state[every, :] = state + STEP_SIZE * b * (jnp.exp(-state / b) - rate)


def finish(params, parts, stress, state):
    rows = stress.shape[1] // LANES
    new_stress, new_rate, new_state = call(
        final_kernel,
        (params, parts.reshape(N_COL, RC_DEV // N_COL, 2 * B), stress, state.reshape(rows, LANES)),
        [VMEM] * 4,
        (
            jax.ShapeDtypeStruct(stress.shape, f32),
            jax.ShapeDtypeStruct((rows, LANES), f32),
            jax.ShapeDtypeStruct((rows, LANES), f32),
        ),
        (VMEM,) * 3,
        "finish",
    )
    return (new_stress, new_rate.reshape(-1), new_state.reshape(-1))


def body(
    slip_rate,
    source_cluster,
    near_kernel,
    near_pattern,
    far_left,
    far_right,
    far_pattern,
    stress,
    state,
    fault_of_row,
    direct_effect,
    evolution_effect,
    normal_stress,
):
    near, left, right = near_kernel[0, 0], far_left[0, 0], far_right[0, 0]
    near_index, far_index = near_pattern[0, 0], far_pattern[0, 0]
    slip = jnp.transpose(slip_rate.reshape(2, CLU_DEV, B), (1, 0, 2))
    gathered = lax.all_to_all(
        make_payload(source_cluster, near_index, far_index), "row", 0, 0, tiled=True
    )

    def fetch(*ctl):
        req, snd, pos = make_index(gathered, ctl)
        asked = lax.all_to_all(req, "col", 0, 0, tiled=True)
        reply, snd, *lists = gather_rows(asked, slip, (snd, pos, near_index, far_index))
        got = lax.all_to_all(reply, "col", 0, 0, tiled=True)
        return lax.all_to_all(forward_rows(snd, got), "row", 0, 0, tiled=True), lists, asked

    x, lists, asked = fetch()
    faults = (direct_effect, evolution_effect, normal_stress)
    fault = fault_of_row.reshape(-1, LANES)
    fast, params, rounds, to_do = block_sums(lists, asked, faults, fault, x, left, right, near)

    def one_round(carry):
        to_do, total = carry
        now = to_do.reshape(1)
        x, lists, _ = fetch(now, rounds)
        rows = pick_rows(now, rounds, lists[0], x)
        n = jnp.arange(LANES, dtype=i32)[None, :]
        part = round_sums(n, near_index, far_index, rows, near, left, right)
        return to_do - 1, jnp.where(to_do == rounds[0], 0.0, total) + part

    _, summed = lax.while_loop(lambda carry: carry[0] > 0, one_round, (to_do.reshape(()), fast))
    parts = lax.all_to_all(summed, "col", 0, 0, tiled=True)
    return finish(params, parts, stress, state)


def solution(mesh):
    return jax.shard_map(
        body,
        mesh=mesh,
        in_specs=(
            P(None, ("row", "col")),
            P(("row", "col")),
            P("row", "col", None, None, None),
            P("row", "col", None, None),
            P("row", "col", None, None, None),
            P("row", "col", None, None, None),
            P("row", "col", None, None),
            P(None, ("row", "col")),
            P(("row", "col")),
            P(("row", "col")),
            P(),
            P(),
            P(),
        ),
        out_specs=(P(None, ("row", "col")), P(("row", "col")), P(("row", "col"))),
        check_vma=False,
    )
```

```python
import functools

import functools

import jax
import jax.numpy as jnp
from jax import lax
from jax.experimental import pallas as pl
from jax.experimental.pallas import tpu as pltpu
from jax.sharding import PartitionSpec as P

B = 256
R = 32
CLU_DEV = 512
RC_DEV = 128
NP = 2
FP = 12
N_ROW = 8
N_COL = 16
NEAR = N_ROW * NP
FAR = N_ROW * FP
BLOCKS = NEAR + FAR
LANES = 128
CAP_COL = 24
CAP_ROW = 32
HALVES = 2
SPAN = 15 * 10**9
ROUNDS = 56
PIECE_ROWS = 8
FAULTS = 40
STEP_SIZE = 0.25

VMEM = pl.BlockSpec(memory_space=pltpu.VMEM)
SMEM = pl.BlockSpec(memory_space=pltpu.SMEM)
HBM = pl.BlockSpec(memory_space=pltpu.HBM)
ANY = pl.BlockSpec(memory_space=pl.ANY)
f32 = jnp.float32
bf16 = jnp.bfloat16
i32 = jnp.int32
NT = (((1,), (1,)), ((), ()))
SMALL = pltpu.CompilerParams(vmem_limit_bytes=6 * 1024 * 1024)


def in_hbm(x):
    return pltpu.with_memory_space_constraint(x, pltpu.HBM)


def call(kernel, ins, specs, outs, out_specs, name):
    return pl.pallas_call(
        kernel,
        out_shape=tuple(outs),
        in_specs=list(specs),
        out_specs=tuple(out_specs),
        compiler_params=SMALL,
        name=name,
    )(*ins)


def iota(shape, dim):
    return lax.broadcasted_iota(i32, shape, dim)


def exact(x):
    return x.astype(f32).astype(bf16)


def split(x):
    return jnp.concatenate([x >> 8, x & 255], axis=0)


def piece_of(n):
    return jnp.where(n < NEAR, n >> 1, ((n - NEAR) * 43) >> 9)


def active_in(n, ctl=None):
    if ctl is None:
        return n < BLOCKS
    rnd, rounds = ctl
    piece = piece_of(n)
    within = jnp.where(n < NEAR, n & 1, NP + (n - NEAR) - FP * piece)
    of = (rnd * 37) >> 8
    pair = (piece == of) & ((within >> 1) == rnd - 7 * of)
    return (n < BLOCKS) & (((rounds == HALVES) & ((piece >> 2) == rnd)) | ((rounds != HALVES) & pair))


def payload_kernel(table_ref, near_ref, far_ref, out_ref):
    out_ref[...] = jnp.zeros_like(out_ref)
    for r in range(N_ROW):
        out_ref[r, 0:4, :] = table_ref[...]
        out_ref[r, 4:5, 0:NEAR] = near_ref[1:2, :]
        out_ref[r, 5:6, 0:FAR] = far_ref[1:2, :]
        out_ref[r, 6:7, :] = jnp.full((1, LANES), r, i32)


def make_payload(source_cluster, near_index, far_index):
    return call(
        payload_kernel,
        [in_hbm(one) for one in (source_cluster.reshape(4, LANES), near_index, far_index)],
        [VMEM, VMEM, VMEM],
        (jax.ShapeDtypeStruct((N_ROW, PIECE_ROWS, LANES), i32),),
        (VMEM,),
        "payload",
    )[0]


def index_kernel(g_ref, *refs):
    req_ref, snd_ref, pos_ref = refs[-3:]
    ctl = (refs[0][0] - 1, refs[1][0]) if len(refs) > 3 else None
    rho = g_ref[0, 6:7, :]
    tables = jnp.concatenate([g_ref[:, q, :] for q in range(4)], axis=1)
    n = iota((N_ROW, LANES), 1)
    m = jnp.where(n < NEAR, g_ref[:, 4, :], pltpu.roll(g_ref[:, 5, :], NEAR, 1))
    active = active_in(n, ctl)
    tab = exact(split(tables))
    piece_mask = (iota((N_ROW, LANES), 0) == piece_of(n)).astype(f32)
    place = iota((CLU_DEV, LANES), 0)
    rows = []
    for r in range(N_ROW):
        onehot = exact(place == m[r : r + 1, :])
        found = jnp.dot(tab, onehot, preferred_element_type=f32)
        value = found[0:N_ROW] * 256.0 + found[N_ROW : 2 * N_ROW]
        rows.append(jnp.sum(value * piece_mask, axis=0, keepdims=True))
    gid = jnp.concatenate(rows, axis=0).astype(i32)
    owner = jnp.where(active, gid >> 9, -1)
    owner_row = owner >> 4
    local = gid & (CLU_DEV - 1)
    every = iota((LANES, LANES), 0)
    counts = jnp.zeros((LANES, LANES), f32)
    for r in range(N_ROW):
        counts = counts + (every == owner[r : r + 1, :]).astype(f32)
    early = (piece_of(iota((1, LANES), 1)) < N_ROW // 2).astype(f32)
    col_label = iota((N_COL, LANES), 0) + rho * N_COL
    row_label = iota((N_ROW, LANES), 0)
    to_col = jnp.concatenate([(col_label == owner[r : r + 1, :]).astype(f32) for r in range(N_ROW)], axis=0)
    to_row = jnp.concatenate([(row_label == owner_row[r : r + 1, :]).astype(f32) for r in range(N_ROW)], axis=0)
    sub, lane = iota((LANES, LANES), 0), iota((LANES, LANES), 1)
    scan = jnp.concatenate([exact(sub < lane), jnp.ones((LANES, LANES), bf16)], axis=1)
    ahead = jnp.dot(to_col.astype(bf16), scan, preferred_element_type=f32)
    earlier = exact(((sub & (N_COL - 1)) == (lane & (N_COL - 1))) & (sub > lane))
    offset = jnp.dot(earlier, ahead[:, LANES:].astype(bf16), preferred_element_type=f32)
    first = to_col * (ahead[:, :LANES] + offset)
    second = to_row * jnp.dot(to_row.astype(bf16), scan[:, :LANES], preferred_element_type=f32)
    slot1 = jnp.concatenate(
        [jnp.sum(first[r * N_COL : (r + 1) * N_COL], axis=0, keepdims=True) for r in range(N_ROW)], axis=0
    ).astype(i32)
    slot2 = jnp.concatenate(
        [jnp.sum(second[r * N_ROW : (r + 1) * N_ROW], axis=0, keepdims=True) for r in range(N_ROW)], axis=0
    ).astype(i32)
    fits = [
        (jnp.max(jnp.sum(counts * part, axis=1, keepdims=True)) <= CAP_COL)
        & (jnp.max(jnp.sum(to_row * part, axis=1, keepdims=True)) <= CAP_ROW)
        for part in (jnp.ones((1, LANES), f32), early, 1.0 - early)
    ]
    over = jnp.where(fits[0], 0, jnp.where(fits[1] & fits[2], 1, 2))
    pos = jnp.clip(owner_row * CAP_ROW + slot2, 0, N_ROW * CAP_ROW - 1)
    pos_ref[...] = jnp.sum(jnp.where(row_label == rho, pos, 0).astype(f32), axis=0, keepdims=True).astype(i32)
    mine = owner_row == rho
    pos1 = jnp.clip((owner & (N_COL - 1)) * CAP_COL + slot1, 0, N_COL * CAP_COL - 1)
    place = iota((CAP_ROW, LANES), 0)
    snd = jnp.zeros((2 * N_ROW, CAP_ROW), f32)
    req = jnp.zeros((2 * N_COL, CAP_ROW), f32)
    for r in range(N_ROW):
        value = split(jnp.where((row_label == r) & mine[r : r + 1, :], pos1[r : r + 1, :], 0))
        put = exact(place == slot2[r : r + 1, :])
        snd = snd + lax.dot_general(exact(value), put, NT, preferred_element_type=f32)
        sel = to_col[r * N_COL : (r + 1) * N_COL] > 0.5
        value = split(jnp.where(sel, local[r : r + 1, :], 0))
        put = exact(place == jnp.where(slot1[r : r + 1, :] < CAP_COL, slot1[r : r + 1, :], -1))
        req = req + lax.dot_general(exact(value), put, NT, preferred_element_type=f32)
    snd_ref[...] = jnp.zeros_like(snd_ref)
    snd_ref[:, 0:CAP_ROW] = (snd[0:N_ROW] * 256.0 + snd[N_ROW : 2 * N_ROW]).astype(i32)
    req_ref[...] = jnp.full(req_ref.shape, over, i32)
    req_ref[:, 0:CAP_ROW] = (req[0:N_COL] * 256.0 + req[N_COL : 2 * N_COL]).astype(i32)


def make_index(gathered, ctl=()):
    return pl.pallas_call(
        index_kernel,
        out_shape=(
            jax.ShapeDtypeStruct((N_COL, LANES), i32),
            jax.ShapeDtypeStruct((N_ROW, LANES), i32),
            jax.ShapeDtypeStruct((1, LANES), i32),
        ),
        in_specs=[VMEM] + [SMEM] * len(ctl),
        out_specs=(VMEM, VMEM, VMEM),
        compiler_params=SMALL,
        cost_estimate=pl.CostEstimate(flops=SPAN, transcendentals=0, bytes_accessed=0),
        name="index",
    )(gathered, *ctl)


def gather_kernel(idx_hbm, slip_ref, *refs):
    lists, out_ref, held, idx_ref, sems = refs[:4], refs[4], refs[5:9], refs[9], refs[10]
    pairs = [(idx_hbm, idx_ref), *zip(lists, held)]
    copies = [pltpu.make_async_copy(one, to, sems.at[k]) for k, (one, to) in enumerate(pairs)]
    for copy in copies:
        copy.start()
    copies[0].wait()

    def one_col(c, _):
        for k in range(CAP_COL):
            out_ref[c * CAP_COL + k] = slip_ref[idx_ref[c, k]]
        return 0

    lax.fori_loop(0, N_COL, one_col, 0)
    for copy in copies[1:]:
        copy.wait()


def gather_rows(idx, slip, lists):
    return pl.pallas_call(
        gather_kernel,
        out_shape=(
            jax.ShapeDtypeStruct((N_COL * CAP_COL, 2, B), f32),
            *(pltpu.SMEM(one.shape, i32) for one in lists),
        ),
        in_specs=[ANY, VMEM] + [ANY] * len(lists),
        out_specs=(VMEM,) + (SMEM,) * len(lists),
        scratch_shapes=[pltpu.SMEM(idx.shape, i32), pltpu.SemaphoreType.DMA((1 + len(lists),))],
        compiler_params=SMALL,
        name="gather",
    )(idx, slip, *lists)


def forward_kernel(idx_ref, got_ref, out_ref):
    def one_row(r, _):
        for k in range(CAP_ROW):
            out_ref[r * CAP_ROW + k] = got_ref[idx_ref[r, k]]
        return 0

    lax.fori_loop(0, N_ROW, one_row, 0)


def forward_rows(idx, got):
    return call(
        forward_kernel,
        (idx, got),
        [SMEM, VMEM],
        (jax.ShapeDtypeStruct((N_ROW * CAP_ROW, 2, B), f32),),
        (VMEM,),
        "forward",
    )[0]


CHUNK = 128


def near_sum(near_ref, at, rows, x):
    prod = near_ref[at, rows, 0:B] * x[0:1, :] + near_ref[at, rows, B : 2 * B] * x[1:2, :]
    return jnp.sum(prod[:, 0:LANES] + prod[:, LANES:B], axis=1, keepdims=True)


def add_near(acc_ref, near_ref, at, x, row):
    here = iota((CHUNK, LANES), 1) == row
    for s in range(0, 2 * B, CHUNK):
        rows = pl.ds(s, CHUNK)
        old = acc_ref[rows, :]
        acc_ref[rows, :] = jnp.where(here, old + near_sum(near_ref, at, rows, x), old)


def add_far(out_ref, left_ref, right_ref, at, x, row):
    x = x.astype(bf16).astype(f32)
    right = right_ref[at].astype(f32)
    prod = right[:, 0:B] * x[0:1, :] + right[:, B : 2 * B] * x[1:2, :]
    coef = jnp.sum(prod[:, 0:LANES] + prod[:, LANES:B], axis=1, keepdims=True)
    coef = coef.astype(bf16).astype(f32)
    far = jnp.sum(left_ref[at].astype(f32) * coef, axis=0, keepdims=True)
    rows = pl.ds(row, 1)
    out_ref[rows, :] = out_ref[rows, :] + far


def blocks_kernel(
    pos_ref, near_row_ref, far_row_ref, asked_hbm, a_hbm, b_hbm, s_hbm, fault_ref, x_ref, left_ref,
    right_ref, near_ref,
    out_ref, param_ref, rounds_out, to_do_out,
    acc_ref, asked_ref, a_ref, b_ref, s_ref, rounds_ref, small_sems, out_sems,
):
    small = [
        pltpu.make_async_copy(one, to, small_sems.at[k])
        for k, (one, to) in enumerate(
            [(asked_hbm, asked_ref), (a_hbm, a_ref), (b_hbm, b_ref), (s_hbm, s_ref)]
        )
    ]
    for copy in small:
        copy.start()
    xs = [x_ref[pos_ref[0, n]] for n in range(NEAR)]
    lane = iota((CHUNK, LANES), 1)

    def some_rows(q, _):
        rows = pl.ds(pl.multiple_of(q * CHUNK, CHUNK), CHUNK)
        acc = jnp.zeros((CHUNK, LANES), f32)
        for n in range(NEAR):
            acc = jnp.where(lane == near_row_ref[0, n], acc + near_sum(near_ref, n, rows, xs[n]), acc)
        acc_ref[rows, :] = acc
        return 0

    lax.fori_loop(0, 2 * B // CHUNK, some_rows, 0, unroll=2)
    out_ref[...] = acc_ref[...].T
    for copy in small:
        copy.wait()
    over = asked_ref[0, LANES - 1]
    for c in range(1, N_COL):
        over = jnp.maximum(over, asked_ref[c, LANES - 1])
    rounds_ref[0] = jnp.where(over == 0, 0, jnp.where(over == 1, HALVES, ROUNDS))
    told = [
        pltpu.make_async_copy(rounds_ref, to, out_sems.at[k])
        for k, to in enumerate((rounds_out, to_do_out))
    ]
    for copy in told:
        copy.start()
    fault = fault_ref[...]
    found = [jnp.zeros(fault.shape, f32) for _ in range(3)]
    for f in range(FAULTS):
        here = fault == f
        found = [jnp.where(here, one[f], old) for one, old in zip((a_ref, b_ref, s_ref), found)]
    for k in range(3):
        param_ref[k] = found[k]

    def some_far(p, _):
        for t in range(FP):
            n = p * FP + t
            add_far(out_ref, left_ref, right_ref, n, x_ref[pos_ref[0, NEAR + n]], far_row_ref[0, n])
        return 0

    lax.fori_loop(0, N_ROW, some_far, 0, unroll=4)
    for copy in told:
        copy.wait()


def block_sums(lists, asked, params, fault, x, left, right, near):
    one = jax.ShapeDtypeStruct((1,), i32)
    small = (asked, *params)
    return pl.pallas_call(
        blocks_kernel,
        out_shape=(
            jax.ShapeDtypeStruct((RC_DEV, 2 * B), f32),
            jax.ShapeDtypeStruct((3,) + fault.shape, f32),
            one,
            one,
        ),
        in_specs=[SMEM] * 3 + [ANY] * len(small) + [VMEM] * 5,
        out_specs=(VMEM, VMEM, ANY, ANY),
        scratch_shapes=[
            pltpu.VMEM((2 * B, LANES), f32),
            *(pltpu.SMEM(x.shape, x.dtype) for x in small),
            pltpu.SMEM((1,), i32),
            pltpu.SemaphoreType.DMA((len(small),)),
            pltpu.SemaphoreType.DMA((2,)),
        ],
        compiler_params=pltpu.CompilerParams(vmem_limit_bytes=28 * 1024 * 1024),
        name="blocks",
    )(*lists, *small, fault, x, left, right, near)


def pick_kernel(to_do_ref, rounds_ref, pos_ref, x_ref, out_ref):
    def one(n, _):
        taken = active_in(n, (to_do_ref[0] - 1, rounds_ref[0]))
        x = x_ref[pos_ref[0, n]]
        out_ref[n] = jnp.where(taken, x, jnp.zeros_like(x))
        return 0

    lax.fori_loop(0, LANES, one, 0)


def pick_rows(to_do, rounds, pos, x):
    return call(
        pick_kernel,
        (to_do, rounds, pos, x),
        [SMEM, SMEM, SMEM, VMEM],
        (jax.ShapeDtypeStruct((LANES, 2, B), f32),),
        (VMEM,),
        "pick",
    )[0]


def round_kernel(
    pos_ref, near_row_ref, far_row_ref, x_ref, near_ref, left_ref, right_ref, out_ref, acc_ref
):
    p = pl.program_id(0)

    @pl.when(p == 0)
    def _():
        out_ref[...] = jnp.zeros_like(out_ref)
        acc_ref[...] = jnp.zeros_like(acc_ref)

    for t in range(NP):
        n = p * NP + t
        add_near(acc_ref, near_ref, t, x_ref[pos_ref[0, n]], near_row_ref[0, n])
    for t in range(FP):
        n = p * FP + t
        add_far(out_ref, left_ref, right_ref, t, x_ref[pos_ref[0, NEAR + n]], far_row_ref[0, n])

    @pl.when(p == N_ROW - 1)
    def _():
        out_ref[...] = out_ref[...] + acc_ref[...].T


def round_sums(pos, near_index, far_index, x, near, left, right):
    return pl.pallas_call(
        round_kernel,
        grid=(N_ROW,),
        out_shape=jax.ShapeDtypeStruct((RC_DEV, 2 * B), f32),
        in_specs=[SMEM, SMEM, SMEM, pl.BlockSpec(x.shape, lambda p: (0, 0, 0))]
        + [
            pl.BlockSpec((one.shape[0] // N_ROW,) + one.shape[1:], lambda p: (p, 0, 0))
            for one in (near, left, right)
        ],
        out_specs=pl.BlockSpec((RC_DEV, 2 * B), lambda p: (0, 0)),
        scratch_shapes=[pltpu.VMEM((2 * B, LANES), f32)],
        compiler_params=pltpu.CompilerParams(vmem_limit_bytes=10 * 1024 * 1024),
        name="round",
    )(pos, near_index, far_index, x, in_hbm(near), in_hbm(left), in_hbm(right))


def final_kernel(param_ref, parts_ref, stress_ref, state_ref, out_stress, out_rate, out_state):
    total = parts_ref[0]
    for c in range(1, N_COL):
        total = total + parts_ref[c]
    groups = RC_DEV // N_COL
    for h in range(2):
        every = pl.ds(h, groups, stride=2)
        state = state_ref[every, :]
        a, b, sigma = (param_ref[k, every, :] for k in range(3))
        square = jnp.ones_like(state)
        for k in range(2):
            old = jnp.concatenate(
                [
                    stress_ref[k : k + 1, g * B + h * LANES : g * B + (h + 1) * LANES]
                    for g in range(groups)
                ],
                axis=0,
            )
            new = old + STEP_SIZE * total[:, k * B + h * LANES : k * B + (h + 1) * LANES]
            for g in range(groups):
                out_stress[k : k + 1, g * B + h * LANES : g * B + (h + 1) * LANES] = new[g : g + 1, :]
            square = square + new * new
        z = jnp.sqrt(square) / (a * sigma)
        u = state / a
        rate = jnp.exp(z - u) - jnp.exp(-z - u)
        out_rate[every, :] = rate
        out_state[every, :] = state + STEP_SIZE * b * (jnp.exp(-state / b) - rate)


def finish(params, parts, stress, state):
    rows = stress.shape[1] // LANES
    new_stress, new_rate, new_state = call(
        final_kernel,
        (params, parts.reshape(N_COL, RC_DEV // N_COL, 2 * B), stress, state.reshape(rows, LANES)),
        [VMEM] * 4,
        (
            jax.ShapeDtypeStruct(stress.shape, f32),
            jax.ShapeDtypeStruct((rows, LANES), f32),
            jax.ShapeDtypeStruct((rows, LANES), f32),
        ),
        (VMEM,) * 3,
        "finish",
    )
    return (new_stress, new_rate.reshape(-1), new_state.reshape(-1))


def body(
    slip_rate,
    source_cluster,
    near_kernel,
    near_pattern,
    far_left,
    far_right,
    far_pattern,
    stress,
    state,
    fault_of_row,
    direct_effect,
    evolution_effect,
    normal_stress,
):
    near, left, right = near_kernel[0, 0], far_left[0, 0], far_right[0, 0]
    near_index, far_index = near_pattern[0, 0], far_pattern[0, 0]
    slip = jnp.transpose(slip_rate.reshape(2, CLU_DEV, B), (1, 0, 2))
    gathered = lax.all_to_all(
        make_payload(source_cluster, near_index, far_index), "row", 0, 0, tiled=True
    )

    def fetch(*ctl):
        req, snd, pos = make_index(gathered, ctl)
        asked = lax.all_to_all(req, "col", 0, 0, tiled=True)
        reply, snd, *lists = gather_rows(asked, slip, (snd, pos, near_index, far_index))
        got = lax.all_to_all(reply, "col", 0, 0, tiled=True)
        return lax.all_to_all(forward_rows(snd, got), "row", 0, 0, tiled=True), lists, asked

    x, lists, asked = fetch()
    faults = (direct_effect, evolution_effect, normal_stress)
    fault = fault_of_row.reshape(-1, LANES)
    fast, params, rounds, to_do = block_sums(lists, asked, faults, fault, x, left, right, near)

    def one_round(carry):
        to_do, total = carry
        now = to_do.reshape(1)
        x, lists, _ = fetch(now, rounds)
        rows = pick_rows(now, rounds, lists[0], x)
        n = jnp.arange(LANES, dtype=i32)[None, :]
        part = round_sums(n, near_index, far_index, rows, near, left, right)
        return to_do - 1, jnp.where(to_do == rounds[0], 0.0, total) + part

    _, summed = lax.while_loop(lambda carry: carry[0] > 0, one_round, (to_do.reshape(()), fast))
    parts = lax.all_to_all(summed, "col", 0, 0, tiled=True)
    return finish(params, parts, stress, state)


def solution(mesh):
    return jax.shard_map(
        body,
        mesh=mesh,
        in_specs=(
            P(None, ("row", "col")),
            P(("row", "col")),
            P("row", "col", None, None, None),
            P("row", "col", None, None),
            P("row", "col", None, None, None),
            P("row", "col", None, None, None),
            P("row", "col", None, None),
            P(None, ("row", "col")),
            P(("row", "col")),
            P(("row", "col")),
            P(),
            P(),
            P(),
        ),
        out_specs=(P(None, ("row", "col")), P(("row", "col")), P(("row", "col"))),
        check_vma=False,
    )
```

```python
import functools

import functools

import jax
import jax.numpy as jnp
from jax import lax
from jax.experimental import pallas as pl
from jax.experimental.pallas import tpu as pltpu
from jax.sharding import PartitionSpec as P

B = 256
R = 32
CLU_DEV = 512
RC_DEV = 128
NP = 2
FP = 12
N_ROW = 8
N_COL = 16
NEAR = N_ROW * NP
FAR = N_ROW * FP
BLOCKS = NEAR + FAR
LANES = 128
CAP_COL = 24
CAP_ROW = 32
HALVES = 2
SPAN = 15 * 10**9
ROUNDS = 56
PIECE_ROWS = 8
FAULTS = 40
STEP_SIZE = 0.25

VMEM = pl.BlockSpec(memory_space=pltpu.VMEM)
SMEM = pl.BlockSpec(memory_space=pltpu.SMEM)
HBM = pl.BlockSpec(memory_space=pltpu.HBM)
ANY = pl.BlockSpec(memory_space=pl.ANY)
f32 = jnp.float32
bf16 = jnp.bfloat16
i32 = jnp.int32
NT = (((1,), (1,)), ((), ()))
SMALL = pltpu.CompilerParams(vmem_limit_bytes=6 * 1024 * 1024)


def in_hbm(x):
    return pltpu.with_memory_space_constraint(x, pltpu.HBM)


def call(kernel, ins, specs, outs, out_specs, name):
    return pl.pallas_call(
        kernel,
        out_shape=tuple(outs),
        in_specs=list(specs),
        out_specs=tuple(out_specs),
        compiler_params=SMALL,
        name=name,
    )(*ins)


def iota(shape, dim):
    return lax.broadcasted_iota(i32, shape, dim)


def exact(x):
    return x.astype(f32).astype(bf16)


def split(x):
    return jnp.concatenate([x >> 8, x & 255], axis=0)


def piece_of(n):
    return jnp.where(n < NEAR, n >> 1, ((n - NEAR) * 43) >> 9)


def active_in(n, ctl=None):
    if ctl is None:
        return n < BLOCKS
    rnd, rounds = ctl
    piece = piece_of(n)
    within = jnp.where(n < NEAR, n & 1, NP + (n - NEAR) - FP * piece)
    of = (rnd * 37) >> 8
    pair = (piece == of) & ((within >> 1) == rnd - 7 * of)
    return (n < BLOCKS) & (((rounds == HALVES) & ((piece >> 2) == rnd)) | ((rounds != HALVES) & pair))


def payload_kernel(table_ref, near_ref, far_ref, out_ref):
    out_ref[...] = jnp.zeros_like(out_ref)
    for r in range(N_ROW):
        out_ref[r, 0:4, :] = table_ref[...]
        out_ref[r, 4:5, 0:NEAR] = near_ref[1:2, :]
        out_ref[r, 5:6, 0:FAR] = far_ref[1:2, :]
        out_ref[r, 6:7, :] = jnp.full((1, LANES), r, i32)


def make_payload(source_cluster, near_index, far_index):
    return call(
        payload_kernel,
        [in_hbm(one) for one in (source_cluster.reshape(4, LANES), near_index, far_index)],
        [VMEM, VMEM, VMEM],
        (jax.ShapeDtypeStruct((N_ROW, PIECE_ROWS, LANES), i32),),
        (VMEM,),
        "payload",
    )[0]


def index_kernel(g_ref, *refs):
    req_ref, snd_ref, pos_ref = refs[-3:]
    ctl = (refs[0][0] - 1, refs[1][0]) if len(refs) > 3 else None
    rho = g_ref[0, 6:7, :]
    tables = jnp.concatenate([g_ref[:, q, :] for q in range(4)], axis=1)
    n = iota((N_ROW, LANES), 1)
    m = jnp.where(n < NEAR, g_ref[:, 4, :], pltpu.roll(g_ref[:, 5, :], NEAR, 1))
    active = active_in(n, ctl)
    tab = exact(split(tables))
    piece_mask = (iota((N_ROW, LANES), 0) == piece_of(n)).astype(f32)
    place = iota((CLU_DEV, LANES), 0)
    rows = []
    for r in range(N_ROW):
        onehot = exact(place == m[r : r + 1, :])
        found = jnp.dot(tab, onehot, preferred_element_type=f32)
        value = found[0:N_ROW] * 256.0 + found[N_ROW : 2 * N_ROW]
        rows.append(jnp.sum(value * piece_mask, axis=0, keepdims=True))
    gid = jnp.concatenate(rows, axis=0).astype(i32)
    owner = jnp.where(active, gid >> 9, -1)
    owner_row = owner >> 4
    local = gid & (CLU_DEV - 1)
    every = iota((LANES, LANES), 0)
    counts = jnp.zeros((LANES, LANES), f32)
    for r in range(N_ROW):
        counts = counts + (every == owner[r : r + 1, :]).astype(f32)
    early = (piece_of(iota((1, LANES), 1)) < N_ROW // 2).astype(f32)
    col_label = iota((N_COL, LANES), 0) + rho * N_COL
    row_label = iota((N_ROW, LANES), 0)
    to_col = jnp.concatenate([(col_label == owner[r : r + 1, :]).astype(f32) for r in range(N_ROW)], axis=0)
    to_row = jnp.concatenate([(row_label == owner_row[r : r + 1, :]).astype(f32) for r in range(N_ROW)], axis=0)
    sub, lane = iota((LANES, LANES), 0), iota((LANES, LANES), 1)
    scan = jnp.concatenate([exact(sub < lane), jnp.ones((LANES, LANES), bf16)], axis=1)
    ahead = jnp.dot(to_col.astype(bf16), scan, preferred_element_type=f32)
    earlier = exact(((sub & (N_COL - 1)) == (lane & (N_COL - 1))) & (sub > lane))
    offset = jnp.dot(earlier, ahead[:, LANES:].astype(bf16), preferred_element_type=f32)
    first = to_col * (ahead[:, :LANES] + offset)
    second = to_row * jnp.dot(to_row.astype(bf16), scan[:, :LANES], preferred_element_type=f32)
    slot1 = jnp.concatenate(
        [jnp.sum(first[r * N_COL : (r + 1) * N_COL], axis=0, keepdims=True) for r in range(N_ROW)], axis=0
    ).astype(i32)
    slot2 = jnp.concatenate(
        [jnp.sum(second[r * N_ROW : (r + 1) * N_ROW], axis=0, keepdims=True) for r in range(N_ROW)], axis=0
    ).astype(i32)
    fits = [
        (jnp.max(jnp.sum(counts * part, axis=1, keepdims=True)) <= CAP_COL)
        & (jnp.max(jnp.sum(to_row * part, axis=1, keepdims=True)) <= CAP_ROW)
        for part in (jnp.ones((1, LANES), f32), early, 1.0 - early)
    ]
    over = jnp.where(fits[0], 0, jnp.where(fits[1] & fits[2], 1, 2))
    pos = jnp.clip(owner_row * CAP_ROW + slot2, 0, N_ROW * CAP_ROW - 1)
    pos_ref[...] = jnp.sum(jnp.where(row_label == rho, pos, 0).astype(f32), axis=0, keepdims=True).astype(i32)
    mine = owner_row == rho
    pos1 = jnp.clip((owner & (N_COL - 1)) * CAP_COL + slot1, 0, N_COL * CAP_COL - 1)
    place = iota((CAP_ROW, LANES), 0)
    snd = jnp.zeros((2 * N_ROW, CAP_ROW), f32)
    req = jnp.zeros((2 * N_COL, CAP_ROW), f32)
    for r in range(N_ROW):
        value = split(jnp.where((row_label == r) & mine[r : r + 1, :], pos1[r : r + 1, :], 0))
        put = exact(place == slot2[r : r + 1, :])
        snd = snd + lax.dot_general(exact(value), put, NT, preferred_element_type=f32)
        sel = to_col[r * N_COL : (r + 1) * N_COL] > 0.5
        value = split(jnp.where(sel, local[r : r + 1, :], 0))
        put = exact(place == jnp.where(slot1[r : r + 1, :] < CAP_COL, slot1[r : r + 1, :], -1))
        req = req + lax.dot_general(exact(value), put, NT, preferred_element_type=f32)
    snd_ref[...] = jnp.zeros_like(snd_ref)
    snd_ref[:, 0:CAP_ROW] = (snd[0:N_ROW] * 256.0 + snd[N_ROW : 2 * N_ROW]).astype(i32)
    req_ref[...] = jnp.full(req_ref.shape, over, i32)
    req_ref[:, 0:CAP_ROW] = (req[0:N_COL] * 256.0 + req[N_COL : 2 * N_COL]).astype(i32)


def make_index(gathered, ctl=()):
    return pl.pallas_call(
        index_kernel,
        out_shape=(
            jax.ShapeDtypeStruct((N_COL, LANES), i32),
            jax.ShapeDtypeStruct((N_ROW, LANES), i32),
            jax.ShapeDtypeStruct((1, LANES), i32),
        ),
        in_specs=[VMEM] + [SMEM] * len(ctl),
        out_specs=(VMEM, VMEM, VMEM),
        compiler_params=SMALL,
        cost_estimate=pl.CostEstimate(flops=SPAN, transcendentals=0, bytes_accessed=0),
        name="index",
    )(gathered, *ctl)


def gather_kernel(idx_hbm, slip_ref, *refs):
    lists, out_ref, held, idx_ref, sems = refs[:4], refs[4], refs[5:9], refs[9], refs[10]
    pairs = [(idx_hbm, idx_ref), *zip(lists, held)]
    copies = [pltpu.make_async_copy(one, to, sems.at[k]) for k, (one, to) in enumerate(pairs)]
    for copy in copies:
        copy.start()
    copies[0].wait()

    def one_col(c, _):
        for k in range(CAP_COL):
            out_ref[c * CAP_COL + k] = slip_ref[idx_ref[c, k]]
        return 0

    lax.fori_loop(0, N_COL, one_col, 0)
    for copy in copies[1:]:
        copy.wait()


def gather_rows(idx, slip, lists):
    return pl.pallas_call(
        gather_kernel,
        out_shape=(
            jax.ShapeDtypeStruct((N_COL * CAP_COL, 2, B), f32),
            *(pltpu.SMEM(one.shape, i32) for one in lists),
        ),
        in_specs=[ANY, VMEM] + [ANY] * len(lists),
        out_specs=(VMEM,) + (SMEM,) * len(lists),
        scratch_shapes=[pltpu.SMEM(idx.shape, i32), pltpu.SemaphoreType.DMA((1 + len(lists),))],
        compiler_params=SMALL,
        name="gather",
    )(idx, slip, *lists)


def forward_kernel(idx_ref, got_ref, out_ref):
    def one_row(r, _):
        for k in range(CAP_ROW):
            out_ref[r * CAP_ROW + k] = got_ref[idx_ref[r, k]]
        return 0

    lax.fori_loop(0, N_ROW, one_row, 0)


def forward_rows(idx, got):
    return call(
        forward_kernel,
        (idx, got),
        [SMEM, VMEM],
        (jax.ShapeDtypeStruct((N_ROW * CAP_ROW, 2, B), f32),),
        (VMEM,),
        "forward",
    )[0]


CHUNK = 128


def near_sum(near_ref, at, rows, x):
    prod = near_ref[at, rows, 0:B] * x[0:1, :] + near_ref[at, rows, B : 2 * B] * x[1:2, :]
    return jnp.sum(prod[:, 0:LANES] + prod[:, LANES:B], axis=1, keepdims=True)


def add_near(acc_ref, near_ref, at, x, row):
    here = iota((CHUNK, LANES), 1) == row
    for s in range(0, 2 * B, CHUNK):
        rows = pl.ds(s, CHUNK)
        old = acc_ref[rows, :]
        acc_ref[rows, :] = jnp.where(here, old + near_sum(near_ref, at, rows, x), old)


def add_far(out_ref, left_ref, right_ref, at, x, row):
    x = x.astype(bf16).astype(f32)
    right = right_ref[at].astype(f32)
    prod = right[:, 0:B] * x[0:1, :] + right[:, B : 2 * B] * x[1:2, :]
    coef = jnp.sum(prod[:, 0:LANES] + prod[:, LANES:B], axis=1, keepdims=True)
    coef = coef.astype(bf16).astype(f32)
    far = jnp.sum(left_ref[at].astype(f32) * coef, axis=0, keepdims=True)
    rows = pl.ds(row, 1)
    out_ref[rows, :] = out_ref[rows, :] + far


def blocks_kernel(
    pos_ref, near_row_ref, far_row_ref, asked_hbm, a_hbm, b_hbm, s_hbm, fault_ref, x_ref, left_ref,
    right_ref, near_ref,
    out_ref, param_ref, rounds_out, to_do_out,
    acc_ref, asked_ref, a_ref, b_ref, s_ref, rounds_ref, small_sems, out_sems,
):
    small = [
        pltpu.make_async_copy(one, to, small_sems.at[k])
        for k, (one, to) in enumerate(
            [(asked_hbm, asked_ref), (a_hbm, a_ref), (b_hbm, b_ref), (s_hbm, s_ref)]
        )
    ]
    for copy in small:
        copy.start()
    xs = [x_ref[pos_ref[0, n]] for n in range(NEAR)]
    lane = iota((CHUNK, LANES), 1)

    def some_rows(q, _):
        rows = pl.ds(pl.multiple_of(q * CHUNK, CHUNK), CHUNK)
        acc = jnp.zeros((CHUNK, LANES), f32)
        for n in range(NEAR):
            acc = jnp.where(lane == near_row_ref[0, n], acc + near_sum(near_ref, n, rows, xs[n]), acc)
        acc_ref[rows, :] = acc
        return 0

    lax.fori_loop(0, 2 * B // CHUNK, some_rows, 0, unroll=4)
    out_ref[...] = acc_ref[...].T
    for copy in small:
        copy.wait()
    over = asked_ref[0, LANES - 1]
    for c in range(1, N_COL):
        over = jnp.maximum(over, asked_ref[c, LANES - 1])
    rounds_ref[0] = jnp.where(over == 0, 0, jnp.where(over == 1, HALVES, ROUNDS))
    told = [
        pltpu.make_async_copy(rounds_ref, to, out_sems.at[k])
        for k, to in enumerate((rounds_out, to_do_out))
    ]
    for copy in told:
        copy.start()
    fault = fault_ref[...]
    found = [jnp.zeros(fault.shape, f32) for _ in range(3)]
    for f in range(FAULTS):
        here = fault == f
        found = [jnp.where(here, one[f], old) for one, old in zip((a_ref, b_ref, s_ref), found)]
    for k in range(3):
        param_ref[k] = found[k]

    def some_far(p, _):
        for t in range(FP):
            n = p * FP + t
            add_far(out_ref, left_ref, right_ref, n, x_ref[pos_ref[0, NEAR + n]], far_row_ref[0, n])
        return 0

    lax.fori_loop(0, N_ROW, some_far, 0, unroll=8)
    for copy in told:
        copy.wait()


def block_sums(lists, asked, params, fault, x, left, right, near):
    one = jax.ShapeDtypeStruct((1,), i32)
    small = (asked, *params)
    return pl.pallas_call(
        blocks_kernel,
        out_shape=(
            jax.ShapeDtypeStruct((RC_DEV, 2 * B), f32),
            jax.ShapeDtypeStruct((3,) + fault.shape, f32),
            one,
            one,
        ),
        in_specs=[SMEM] * 3 + [ANY] * len(small) + [VMEM] * 5,
        out_specs=(VMEM, VMEM, ANY, ANY),
        scratch_shapes=[
            pltpu.VMEM((2 * B, LANES), f32),
            *(pltpu.SMEM(x.shape, x.dtype) for x in small),
            pltpu.SMEM((1,), i32),
            pltpu.SemaphoreType.DMA((len(small),)),
            pltpu.SemaphoreType.DMA((2,)),
        ],
        compiler_params=pltpu.CompilerParams(vmem_limit_bytes=28 * 1024 * 1024),
        name="blocks",
    )(*lists, *small, fault, x, left, right, near)


def pick_kernel(to_do_ref, rounds_ref, pos_ref, x_ref, out_ref):
    def one(n, _):
        taken = active_in(n, (to_do_ref[0] - 1, rounds_ref[0]))
        x = x_ref[pos_ref[0, n]]
        out_ref[n] = jnp.where(taken, x, jnp.zeros_like(x))
        return 0

    lax.fori_loop(0, LANES, one, 0)


def pick_rows(to_do, rounds, pos, x):
    return call(
        pick_kernel,
        (to_do, rounds, pos, x),
        [SMEM, SMEM, SMEM, VMEM],
        (jax.ShapeDtypeStruct((LANES, 2, B), f32),),
        (VMEM,),
        "pick",
    )[0]


def round_kernel(
    pos_ref, near_row_ref, far_row_ref, x_ref, near_ref, left_ref, right_ref, out_ref, acc_ref
):
    p = pl.program_id(0)

    @pl.when(p == 0)
    def _():
        out_ref[...] = jnp.zeros_like(out_ref)
        acc_ref[...] = jnp.zeros_like(acc_ref)

    for t in range(NP):
        n = p * NP + t
        add_near(acc_ref, near_ref, t, x_ref[pos_ref[0, n]], near_row_ref[0, n])
    for t in range(FP):
        n = p * FP + t
        add_far(out_ref, left_ref, right_ref, t, x_ref[pos_ref[0, NEAR + n]], far_row_ref[0, n])

    @pl.when(p == N_ROW - 1)
    def _():
        out_ref[...] = out_ref[...] + acc_ref[...].T


def round_sums(pos, near_index, far_index, x, near, left, right):
    return pl.pallas_call(
        round_kernel,
        grid=(N_ROW,),
        out_shape=jax.ShapeDtypeStruct((RC_DEV, 2 * B), f32),
        in_specs=[SMEM, SMEM, SMEM, pl.BlockSpec(x.shape, lambda p: (0, 0, 0))]
        + [
            pl.BlockSpec((one.shape[0] // N_ROW,) + one.shape[1:], lambda p: (p, 0, 0))
            for one in (near, left, right)
        ],
        out_specs=pl.BlockSpec((RC_DEV, 2 * B), lambda p: (0, 0)),
        scratch_shapes=[pltpu.VMEM((2 * B, LANES), f32)],
        compiler_params=pltpu.CompilerParams(vmem_limit_bytes=10 * 1024 * 1024),
        name="round",
    )(pos, near_index, far_index, x, in_hbm(near), in_hbm(left), in_hbm(right))


def final_kernel(param_ref, parts_ref, stress_ref, state_ref, out_stress, out_rate, out_state):
    total = parts_ref[0]
    for c in range(1, N_COL):
        total = total + parts_ref[c]
    groups = RC_DEV // N_COL
    for h in range(2):
        every = pl.ds(h, groups, stride=2)
        state = state_ref[every, :]
        a, b, sigma = (param_ref[k, every, :] for k in range(3))
        square = jnp.ones_like(state)
        for k in range(2):
            old = jnp.concatenate(
                [
                    stress_ref[k : k + 1, g * B + h * LANES : g * B + (h + 1) * LANES]
                    for g in range(groups)
                ],
                axis=0,
            )
            new = old + STEP_SIZE * total[:, k * B + h * LANES : k * B + (h + 1) * LANES]
            for g in range(groups):
                out_stress[k : k + 1, g * B + h * LANES : g * B + (h + 1) * LANES] = new[g : g + 1, :]
            square = square + new * new
        z = jnp.sqrt(square) / (a * sigma)
        u = state / a
        rate = jnp.exp(z - u) - jnp.exp(-z - u)
        out_rate[every, :] = rate
        out_state[every, :] = state + STEP_SIZE * b * (jnp.exp(-state / b) - rate)


def finish(params, parts, stress, state):
    rows = stress.shape[1] // LANES
    new_stress, new_rate, new_state = call(
        final_kernel,
        (params, parts.reshape(N_COL, RC_DEV // N_COL, 2 * B), stress, state.reshape(rows, LANES)),
        [VMEM] * 4,
        (
            jax.ShapeDtypeStruct(stress.shape, f32),
            jax.ShapeDtypeStruct((rows, LANES), f32),
            jax.ShapeDtypeStruct((rows, LANES), f32),
        ),
        (VMEM,) * 3,
        "finish",
    )
    return (new_stress, new_rate.reshape(-1), new_state.reshape(-1))


def body(
    slip_rate,
    source_cluster,
    near_kernel,
    near_pattern,
    far_left,
    far_right,
    far_pattern,
    stress,
    state,
    fault_of_row,
    direct_effect,
    evolution_effect,
    normal_stress,
):
    near, left, right = near_kernel[0, 0], far_left[0, 0], far_right[0, 0]
    near_index, far_index = near_pattern[0, 0], far_pattern[0, 0]
    slip = jnp.transpose(slip_rate.reshape(2, CLU_DEV, B), (1, 0, 2))
    gathered = lax.all_to_all(
        make_payload(source_cluster, near_index, far_index), "row", 0, 0, tiled=True
    )

    def fetch(*ctl):
        req, snd, pos = make_index(gathered, ctl)
        asked = lax.all_to_all(req, "col", 0, 0, tiled=True)
        reply, snd, *lists = gather_rows(asked, slip, (snd, pos, near_index, far_index))
        got = lax.all_to_all(reply, "col", 0, 0, tiled=True)
        return lax.all_to_all(forward_rows(snd, got), "row", 0, 0, tiled=True), lists, asked

    x, lists, asked = fetch()
    faults = (direct_effect, evolution_effect, normal_stress)
    fault = fault_of_row.reshape(-1, LANES)
    fast, params, rounds, to_do = block_sums(lists, asked, faults, fault, x, left, right, near)

    def one_round(carry):
        to_do, total = carry
        now = to_do.reshape(1)
        x, lists, _ = fetch(now, rounds)
        rows = pick_rows(now, rounds, lists[0], x)
        n = jnp.arange(LANES, dtype=i32)[None, :]
        part = round_sums(n, near_index, far_index, rows, near, left, right)
        return to_do - 1, jnp.where(to_do == rounds[0], 0.0, total) + part

    _, summed = lax.while_loop(lambda carry: carry[0] > 0, one_round, (to_do.reshape(()), fast))
    parts = lax.all_to_all(summed, "col", 0, 0, tiled=True)
    return finish(params, parts, stress, state)


def solution(mesh):
    return jax.shard_map(
        body,
        mesh=mesh,
        in_specs=(
            P(None, ("row", "col")),
            P(("row", "col")),
            P("row", "col", None, None, None),
            P("row", "col", None, None),
            P("row", "col", None, None, None),
            P("row", "col", None, None, None),
            P("row", "col", None, None),
            P(None, ("row", "col")),
            P(("row", "col")),
            P(("row", "col")),
            P(),
            P(),
            P(),
        ),
        out_specs=(P(None, ("row", "col")), P(("row", "col")), P(("row", "col"))),
        check_vma=False,
    )
```
